512 devices in a mesh: gx: 16 (over z), gy: 32 (over x, y, core).
Axes of the slice: x: 4, y: 4, z: 16, core: 2. Of those that a mesh axis runs over, the one named last changes fastest.
Arguments:
- samples: bfloat16 [524288, 32], P(('gx', 'gy')), may hold values from -6 to 6
- site_order: int32 [524288], P(('gx', 'gy')), may hold values from 0 to 1023, as said below
- leaf_basis: bfloat16 [64, 128, 64, 32], P('gx', 'gy'), may hold values from -0.75 to 0.75
- near_blocks: bfloat16 [64, 128, 9, 64, 64], P('gx', 'gy'), may hold values from -0.25 to 0.25
- transfer: bfloat16 [2, 4, 32, 32], replicated, may hold values from -0.75 to 0.75
- coupling: bfloat16 [3, 40, 32, 32], replicated, may hold values from -0.21875 to 0.21875
Outputs:
- covariance_product: bfloat16 [524288, 32], P(('gx', 'gy'))
The draws below stay inside these ranges and needn't reach their ends.
Inputs may be any that keep to these rules, and one draw needn't show every extreme that they name: `site_order`: each device's block of 1024 consecutive entries, devices ordered by gx then gy, is a permutation of 0 to 1023.
All inputs are finite; a program needn't handle non-finite values.
Results may differ from the reference program's by a relative error of at most 0.0065.
Values may be sent and summed in bfloat16 or wider, within the bound.
No kernel may reach another device: no remote copies, remote signals or barrier semaphores. Data moves between devices by JAX's collectives and lax.ppermute only.
A program may use at most 64 MiB of HBM per device.

```python
import jax
import jax.numpy as jnp

SITES_LEAF = 64
BASIS_RANK = 32
VECTORS = 32
LEVELS = 3
BOXES_X = 4
BOXES_Y = 4
SITES_DEV = 1024
GRID_X = 64
GRID_Y = 128
SITES = 524288
N_GX = 16
N_GY = 32


def draw_site_order(key, part):
    key = jax.random.fold_in(key, 11)
    key_list = jax.random.split(key, N_GX * N_GY)

    def one_block(subkey):
        return jax.random.permutation(subkey, SITES_DEV)
    orders = jax.vmap(one_block)(key_list)
    return orders.reshape(-1).astype(jnp.int32)


def shard_levels(stream_key, dims, pieces, least, largest):
    gain = 1.0
    for dim, shards_of in pieces:
        steps = jax.random.uniform(jax.random.fold_in(jax.random.fold_in(stream_key, 6), dim), (shards_of,), jnp.float32, least / len(pieces), largest / len(pieces))
        gain = gain * jnp.repeat(jnp.exp(steps), dims[dim] // shards_of).reshape((-1,) + (1,) * (len(dims) - 1 - dim))
    return gain


def gaussian(rng, dims, deviation, limit, shards=(), kind=jnp.bfloat16):
    result = jax.random.normal(rng, dims, jnp.float32) * deviation
    if len(shards) > 0:
        result = shard_levels(rng, dims, shards, -0.22, 0.18) * result
    return jnp.clip(result, min=-limit, max=limit).astype(kind)


def setup_inputs(seed: int = 0) -> dict:
    splits = jax.random.split(jax.random.key(seed), 7)
    return {
        "samples": gaussian(splits[0], (SITES, VECTORS), 1.0, 6.0, ((0, 512),)),
        "site_order": draw_site_order(jax.random.fold_in(splits[6], 71), 0),
        "leaf_basis": gaussian(splits[2], (GRID_X, GRID_Y, SITES_LEAF, BASIS_RANK), SITES_LEAF ** -0.5, 0.75, ((0, 16), (1, 32))),
        "near_blocks": gaussian(splits[3], (GRID_X, GRID_Y, 9, SITES_LEAF, SITES_LEAF), (9 * SITES_LEAF) ** -0.5, 0.25, ((0, 16), (1, 32))),
        "transfer": gaussian(splits[4], (LEVELS - 1, 4, BASIS_RANK, BASIS_RANK), (2 * BASIS_RANK) ** -0.5, 0.75),
        "coupling": gaussian(splits[5], (LEVELS, 40, BASIS_RANK, BASIS_RANK), (27 * BASIS_RANK) ** -0.5, 0.21875),
    }


OFFSETS = [(shift_row, shift_column) for shift_row in range(-3, 4) for shift_column in range(-3, 4) if max(abs(shift_row), abs(shift_column)) >= 2]


def allowed(parity, offset):
    parent_step = jnp.floor_divide(parity + offset, 2)
    return (parent_step >= -1) & (parent_step <= 1)


def lift_level(expansions, matrices):
    row_count, column_count = expansions.shape[0], expansions.shape[1]
    grouped = expansions.reshape(row_count // 2, 2, column_count // 2, 2, expansions.shape[2], expansions.shape[3])
    blocks = matrices.reshape(2, 2, matrices.shape[1], matrices.shape[2])
    return jnp.einsum('xiyjkv,ijkm->xymv', grouped.astype(jnp.float32), blocks.astype(jnp.float32))


def lower_level(downward, matrices):
    row_count, column_count = downward.shape[0], downward.shape[1]
    blocks = matrices.reshape(2, 2, matrices.shape[1], matrices.shape[2])
    spread = jnp.einsum('ijkm,xymv->xiyjkv', blocks.astype(jnp.float32), downward.astype(jnp.float32))
    return spread.reshape(2 * row_count, 2 * column_count, downward.shape[2], downward.shape[3])


def far_sum(expansions, matrices):
    row_count, column_count = expansions.shape[0], expansions.shape[1]
    padded = jnp.pad(expansions.astype(jnp.float32), ((3, 3), (3, 3), (0, 0), (0, 0)))
    row_parity = jnp.arange(row_count, dtype=jnp.int32) % 2
    column_parity = jnp.arange(column_count, dtype=jnp.int32) % 2
    total = jnp.zeros(expansions.shape, jnp.float32)
    for position, (shift_row, shift_column) in enumerate(OFFSETS):
        window = padded[3 + shift_row:3 + shift_row + row_count, 3 + shift_column:3 + shift_column + column_count]
        inside = allowed(row_parity, shift_row)[:, None] & allowed(column_parity, shift_column)[None, :]
        term = jnp.einsum('ij,abjv->abiv', matrices[position].astype(jnp.float32), window)
        total = total + jnp.where(inside[:, :, None, None], term, jnp.zeros_like(term))
    return total


def place_rows(rows_in, indices):
    return jnp.zeros_like(rows_in).at[indices].set(rows_in)


def reference(samples, site_order, leaf_basis, near_blocks, transfer, coupling):
    devices_all = N_GX * N_GY
    box_order = site_order.reshape(devices_all, SITES_DEV)
    ordered = jnp.take_along_axis(samples.reshape(devices_all, SITES_DEV, VECTORS), box_order[:, :, None], axis=1)
    leaf_values = ordered.reshape(N_GX, N_GY, BOXES_X, BOXES_Y, SITES_LEAF, VECTORS).transpose(0, 2, 1, 3, 4, 5).reshape(GRID_X, GRID_Y, SITES_LEAF, VECTORS)
    padded_values = jnp.pad(leaf_values.astype(jnp.float32), ((1, 1), (1, 1), (0, 0), (0, 0)))
    near_field = jnp.zeros((GRID_X, GRID_Y, SITES_LEAF, VECTORS), jnp.float32)
    for position in range(9):
        shift_row = position // 3 - 1
        shift_column = position % 3 - 1
        window = padded_values[1 + shift_row:1 + shift_row + GRID_X, 1 + shift_column:1 + shift_column + GRID_Y]
        near_field = near_field + jnp.einsum('abpq,abqv->abpv', near_blocks[:, :, position].astype(jnp.float32), window)
    expansions = [jnp.einsum('abpk,abpv->abkv', leaf_basis.astype(jnp.float32), leaf_values.astype(jnp.float32)).astype(jnp.bfloat16)]
    for level_index in range(LEVELS - 1):
        expansions.append(lift_level(expansions[-1], transfer[level_index]).astype(jnp.bfloat16))
    far_terms = [far_sum(expansions[level_index], coupling[level_index]) for level_index in range(LEVELS)]
    downward = far_terms[-1].astype(jnp.bfloat16)
    for level_index in reversed(range(LEVELS - 1)):
        downward = (far_terms[level_index] + lower_level(downward, transfer[level_index])).astype(jnp.bfloat16)
    combined = jnp.einsum('abpk,abkv->abpv', leaf_basis.astype(jnp.float32), downward.astype(jnp.float32)) + near_field
    combined = combined.astype(jnp.bfloat16)
    box_rows = combined.reshape(N_GX, BOXES_X, N_GY, BOXES_Y, SITES_LEAF, VECTORS).transpose(0, 2, 1, 3, 4, 5).reshape(devices_all, SITES_DEV, VECTORS)
    scattered = jax.vmap(place_rows)(box_rows, box_order)
    return scattered.reshape(SITES, VECTORS)
```

```python
import jax
import jax.numpy as jnp
from jax import lax
from jax.experimental import pallas as pl
from jax.experimental.pallas import tpu as pltpu
from jax.sharding import PartitionSpec as P

BF = jnp.bfloat16
F32 = jnp.float32
AXES = ("gx", "gy")
VMEM_BYTES = 48 * 1024 * 1024

OWN_ROW, OWN_COL, OWN_E0, OWN_E1, OWN_E2, OWN_ROWS = 0, 64, 128, 256, 288, 320
FAR_X, FAR_E0, FAR_CORNER, FAR_E1, FAR_E1_SIDE, FAR_E2, FAR_ROWS = 0, 64, 128, 192, 224, 256, 288


def dot(a, b):
    return lax.dot_general(a, b, (((1,), (0,)), ((), ())), preferred_element_type=F32)


def dot_nt(a, b):
    return lax.dot_general(a, b, (((1,), (1,)), ((), ())), preferred_element_type=F32)


def roll(x, lanes):
    lanes = lanes % x.shape[1]
    if lanes == 0:
        return x
    if x.dtype == BF:
        return pltpu.roll(x.astype(F32), lanes, 1).astype(BF)
    return pltpu.roll(x, lanes, 1)


def lane_of(rows, lanes=128):
    return lax.broadcasted_iota(jnp.int32, (rows, lanes), 1)


def slot_of(rows, lanes=128):
    return lane_of(rows, lanes) // 32


def eye(n):
    row = lax.broadcasted_iota(jnp.int32, (n, n), 0)
    return jnp.where(row == lane_of(n, n), 1.0, 0.0).astype(BF)


def place():
    gx, gy = lax.axis_index("gx"), lax.axis_index("gy")
    return gx, gy, lax.rem(gx, 2), lax.rem(gy, 2)


def merge_diagonal(blocks, height):
    slot = slot_of(height)
    out = jnp.zeros((height, 128), F32)
    for b in range(4):
        out = jnp.where(slot == b, blocks[b * height : (b + 1) * height], out)
    return out


def upward_kernel(samples, order, basis, transfer, x_out, msg):
    _, _, pi, pj = place()
    slot = slot_of(64)
    spread = jnp.concatenate([samples[...]] * 4, axis=0)
    lane = lane_of(128)
    xs, e0s = [], []
    for a in range(4):
        picked = []
        for half in range(2):
            g = 2 * a + half
            line = order[g : g + 1, :].astype(F32)
            column = jnp.transpose(jnp.broadcast_to(line, (128, 128))).astype(jnp.int32)
            pick = jnp.concatenate(
                [jnp.where(column == lane + 128 * t, 1.0, 0.0).astype(BF) for t in range(8)],
                axis=1,
            )
            picked.append(dot_nt(pick, spread))
        x = merge_diagonal(jnp.concatenate(picked, axis=0), 64).astype(BF)
        x_out[a * 64 : (a + 1) * 64, :] = x
        e0 = merge_diagonal(dot(basis[a * 128 : (a + 1) * 128, :], x), 32).astype(BF)
        msg[OWN_E0 + a * 32 : OWN_E0 + (a + 1) * 32, :] = e0
        xs.append(x)
        e0s.append(e0)
    msg[OWN_ROW : OWN_ROW + 64, :] = jnp.where(pi == 0, xs[3], xs[0])
    column_slot = jnp.where(pj == 0, 3, 0)
    packed = jnp.zeros((64, 128), BF)
    for a in range(4):
        packed = jnp.where(slot == lax.rem(column_slot + a, 4), roll(xs[a], 32 * a), packed)
    msg[OWN_COL : OWN_COL + 64, :] = packed

    one = eye(32)
    slot = slot_of(32)
    turned = [dot_nt(one, transfer[n * 32 : (n + 1) * 32, :]).astype(BF) for n in range(8)]
    e1 = jnp.zeros((32, 128), F32)
    for x in range(2):
        parts = []
        for j in range(2):
            parts.append(dot(turned[j], e0s[2 * x]) + dot(turned[2 + j], e0s[2 * x + 1]))
        joined = parts[0] + roll(parts[1], -32)
        e1 = jnp.where(slot == 2 * x, roll(joined, 64 * x), e1)
        e1 = jnp.where(slot == 2 * x + 1, roll(joined, 64 * x - 32), e1)
    e1 = e1.astype(BF)
    msg[OWN_E1 : OWN_E1 + 32, :] = e1
    e2 = merge_diagonal(dot(jnp.concatenate(turned[4:], axis=0), e1), 32)
    e2 = e2 + roll(e2, 64)
    e2 = e2 + roll(e2, 32)
    msg[OWN_E2 : OWN_E2 + 32, :] = jnp.where(slot == 2 * pi + pj, e2, 0.0).astype(BF)


def cross_kernel(group, x, send):
    _, _, pi, pj = place()
    me, across_x, across_y = 2 * pi + pj, 2 * (1 - pi) + pj, 2 * pi + 1 - pj
    lane, slot = lane_of(64), slot_of(64)
    near_half = (lane < 64) == (pj == 0)
    e0 = group[me, OWN_E0 : OWN_E0 + 128, :]
    e0_rows = jnp.where(pi == 0, e0[:64], e0[64:])
    x_row = jnp.where(pi == 0, x[0:64, :], x[192:256, :])
    e1 = group[me, OWN_E1 : OWN_E1 + 32, :]
    e2 = group[0, OWN_E2 : OWN_ROWS, :]
    for m in range(1, 4):
        e2 = e2 + group[m, OWN_E2 : OWN_ROWS, :]
    for m in range(4):
        send[m, FAR_E2 : FAR_E2 + 32, :] = e2
        send[m, FAR_E1 : FAR_E1 + 32, :] = e1

    to = 2 * pi + 1 - pj
    send[to, FAR_X : FAR_X + 64, :] = x_row
    send[to, FAR_E0 : FAR_E0 + 64, :] = e0_rows
    column = group[across_y, OWN_COL : OWN_COL + 64, :]
    column = jnp.where(pi == 0, roll(column, 64), roll(column, -32))
    corner_e0 = group[across_y, pl.ds(OWN_E0 + 64 * pi, 64), :]
    send[to, FAR_CORNER : FAR_CORNER + 64, :] = jnp.where(near_half, corner_e0, column)
    send[to, FAR_E1_SIDE : FAR_E1_SIDE + 32, :] = group[across_y, OWN_E1 : OWN_E1 + 32, :]

    to = 2 * (1 - pi) + pj
    column_slot = jnp.where(pj == 0, 0, 3)
    packed = jnp.zeros((64, 128), BF)
    for a in range(4):
        moved = roll(x[a * 64 : (a + 1) * 64, :], 32 * a)
        packed = jnp.where(slot == lax.rem(column_slot + a, 4), moved, packed)
    send[to, FAR_X : FAR_X + 64, :] = packed
    send[to, FAR_E0 : FAR_E0 + 64, :] = jnp.where(near_half, e0[:64], roll(e0[64:], 64))
    corner_x = roll(group[across_x, OWN_ROW : OWN_ROW + 64, :], 64)
    corner_e0 = group[across_x, pl.ds(OWN_E0 + 64 * pi, 64), :]
    send[to, FAR_CORNER : FAR_CORNER + 64, :] = jnp.where(near_half, corner_e0, corner_x)
    send[to, FAR_E1_SIDE : FAR_E1_SIDE + 32, :] = group[across_x, OWN_E1 : OWN_E1 + 32, :]

    to = 2 * pi + pj
    send[to, FAR_X : FAR_X + 64, :] = jnp.zeros((64, 128), BF)
    send[to, FAR_E0 : FAR_E0 + 64, :] = jnp.zeros((64, 128), BF)
    send[to, FAR_CORNER : FAR_CORNER + 64, :] = jnp.where(near_half, e0_rows, roll(x_row, 64))
    send[to, FAR_E1_SIDE : FAR_E1_SIDE + 32, :] = jnp.zeros((32, 128), BF)

    to = 2 * (1 - pi) + 1 - pj
    send[to, 0:FAR_E1, :] = jnp.zeros((FAR_E1, 128), BF)
    send[to, FAR_E1_SIDE : FAR_E1_SIDE + 32, :] = jnp.zeros((32, 128), BF)


def store_row_of_tiles(halo, start, left, middle, right):
    lane = lane_of(32)
    low = lane < 64
    nothing = jnp.zeros((32, 128), BF)
    first = jnp.where(low, middle, roll(right, 64))
    second = jnp.where(low, roll(middle, 64), right)
    halo[pl.ds(start, 32), 0:128] = first
    halo[pl.ds(start, 32), 128:256] = jnp.where(low, nothing, roll(left, 64))
    halo[pl.ds(start + 32, 32), 0:128] = second
    halo[pl.ds(start + 32, 32), 128:256] = jnp.where(low, nothing, left)


def far_row(matrix, window, parity):
    lane = lane_of(224, 224)
    admitted = (lane >= 32 * (1 - parity)) & (lane < 224 - 32 * parity)
    product = dot(jnp.where(admitted, matrix, jnp.zeros((224, 224), BF)), window)
    odd = lax.rem(slot_of(32), 2) == 1
    out = jnp.zeros((32, 128), F32)
    for w in range(-3, 4):
        part = product[(w + 3) * 32 : (w + 4) * 32]
        part = part[:, :128] if w == 0 else pltpu.roll(part, (-32 * w) % 256, 1)[:, :128]
        if w == -3:
            part = jnp.where(odd, part, 0.0)
        if w == 3:
            part = jnp.where(odd, 0.0, part)
        out = out + part
    return out


def downward_kernel(count_x, count_y):
    def body(group, x, cross, shared, near, basis, transfer, coupling, order, out, far, h0, h1, h2):
        gx, gy, pi, pj = place()
        me, across_x, across_y = 2 * pi + pj, 2 * (1 - pi) + pj, 2 * pi + 1 - pj
        across = 2 * (1 - pi) + 1 - pj
        from_x, from_y, from_xy = 2 * pi + 1 - pj, 2 * (1 - pi) + pj, 2 * pi + pj
        has_x = jnp.where(pi == 0, gx > 0, gx < count_x - 1)
        has_y = jnp.where(pj == 0, gy > 0, gy < count_y - 1)
        has_xy = has_x & has_y

        def kept(keep, value):
            return jnp.where(keep, value, jnp.zeros_like(value))

        far[...] = jnp.zeros(far.shape, BF)
        for level in range(3):
            n = 0
            for u in range(-3, 4):
                for w in range(-3, 4):
                    if max(abs(u), abs(w)) >= 2:
                        start = (level * 40 + n) * 32
                        far[level, (w + 3) * 32 : (w + 4) * 32, (u + 3) * 32 : (u + 4) * 32] = (
                            coupling[start : start + 32, :]
                        )
                        n += 1

        lane = lane_of(64)
        near_half = (lane < 64) == (pj == 0)
        h0[0:32, :] = jnp.zeros((32, 256), BF)
        h0[288:320, :] = jnp.zeros((32, 256), BF)
        h0[96:224, 0:128] = group[me, OWN_E0 : OWN_E0 + 128, :]
        strip = kept(has_y, cross[from_y, FAR_E0 : FAR_E0 + 64, :])
        beside = group[across_y, OWN_E0 : OWN_E0 + 128, :]
        h0[96:160, 128:256] = jnp.where(near_half, beside[:64], strip)
        h0[160:224, 128:256] = jnp.where(near_half, beside[64:], roll(strip, 64))
        start = 32 + 192 * (1 - pi)
        h0[pl.ds(start, 64), 0:128] = group[across_x, pl.ds(OWN_E0 + 64 * pi, 64), :]
        h0[pl.ds(start, 64), 128:256] = jnp.where(
            near_half,
            group[across, pl.ds(OWN_E0 + 64 * pi, 64), :],
            kept(has_y, cross[from_y, FAR_CORNER : FAR_CORNER + 64, :]),
        )
        start = 32 + 192 * pi
        h0[pl.ds(start, 64), 0:128] = kept(has_x, cross[from_x, FAR_E0 : FAR_E0 + 64, :])
        h0[pl.ds(start, 64), 128:256] = jnp.where(
            near_half,
            kept(has_x, cross[from_x, FAR_CORNER : FAR_CORNER + 64, :]),
            kept(has_xy, cross[from_xy, FAR_CORNER : FAR_CORNER + 64, :]),
        )

        def store_sides(start, middle, inner, outer):
            left = jnp.where(pj == 0, outer, inner)
            right = jnp.where(pj == 0, inner, outer)
            store_row_of_tiles(h1, start, left, middle, right)

        for halo in (h1, h2):
            halo[0:32, :] = jnp.zeros((32, 256), BF)
            halo[224:256, :] = jnp.zeros((32, 256), BF)
        own_e1 = slice(OWN_E1, OWN_E1 + 32)
        far_e1, side_e1 = slice(FAR_E1, FAR_E1 + 32), slice(FAR_E1_SIDE, FAR_E1_SIDE + 32)
        store_sides(
            96, group[me, own_e1, :], group[across_y, own_e1, :], kept(has_y, cross[from_y, far_e1, :])
        )
        store_sides(
            32 + 128 * (1 - pi),
            group[across_x, own_e1, :],
            group[across, own_e1, :],
            kept(has_y, cross[from_y, side_e1, :]),
        )
        store_sides(
            32 + 128 * pi,
            kept(has_x, cross[from_x, far_e1, :]),
            kept(has_x, cross[from_x, side_e1, :]),
            kept(has_xy, cross[from_xy, far_e1, :]),
        )

        above, below = gx >= 2, gx < count_x - 2
        before, after = gy >= 2, gy < count_y - 2
        e2 = group[0, OWN_E2:OWN_ROWS, :]
        for m in range(1, 4):
            e2 = e2 + group[m, OWN_E2:OWN_ROWS, :]
        store_row_of_tiles(
            h2,
            32,
            kept(above & before, shared[0, 0]),
            kept(above, shared[0, 1]),
            kept(above & after, shared[1, 1]),
        )
        store_row_of_tiles(h2, 96, kept(before, shared[0, 2]), e2, kept(after, shared[1, 3]))
        store_row_of_tiles(
            h2,
            160,
            kept(below & before, shared[2, 2]),
            kept(below, shared[2, 3]),
            kept(below & after, shared[3, 3]),
        )

        slot = slot_of(32)
        local2 = far_row(far[2], h2[pl.ds(32 * pi, 224), :], pi)
        local2 = jnp.where(slot == pj, local2, 0.0)
        local2 = local2 + roll(local2, 64)
        local2 = (local2 + roll(local2, 32)).astype(BF)
        spread = dot(transfer[128:256, :], local2)
        local1 = []
        for i in range(2):
            down = far_row(far[1], h1[32 * i : 32 * i + 224, :], i)
            for j in range(2):
                n = 2 * i + j
                down = down + jnp.where(slot == j, spread[n * 32 : (n + 1) * 32], 0.0)
            down = jnp.where(slot < 2, down, 0.0)
            wide = jnp.where(slot == 0, down, 0.0) + jnp.where(slot == 2, roll(down, 32), 0.0)
            local1.append((wide + roll(wide, 32)).astype(BF))
        local0 = []
        for i in range(4):
            spread = dot(transfer[64 * (i % 2) : 64 * (i % 2) + 64, :], local1[i // 2])
            down = far_row(far[0], h0[32 * i : 32 * i + 224, :], i % 2)
            down = down + jnp.where(lax.rem(slot, 2) == 0, spread[:32], spread[32:])
            local0.append(down.astype(BF))

        slot = slot_of(64)
        column = kept(has_y, cross[from_y, FAR_X : FAR_X + 64, :])
        beside = group[across_y, OWN_COL : OWN_COL + 64, :]
        windows = {}

        def store_windows(a, middle, inner, outer):
            left = jnp.where(pj == 0, outer, inner)
            right = jnp.where(pj == 0, inner, outer)
            windows[a, 0] = middle
            windows[a, -1] = roll(jnp.where(slot == 3, left, middle), 32)
            windows[a, 1] = roll(jnp.where(slot == 0, right, middle), -32)

        for a in range(4):
            store_windows(
                a, x[a * 64 : (a + 1) * 64, :], roll(beside, -32 * a), roll(column, -32 * a)
            )
        inside = (
            group[across_x, OWN_ROW : OWN_ROW + 64, :],
            group[across, OWN_ROW : OWN_ROW + 64, :],
            kept(has_y, roll(cross[from_y, FAR_CORNER : FAR_CORNER + 64, :], 64)),
        )
        outside = (
            kept(has_x, cross[from_x, FAR_X : FAR_X + 64, :]),
            kept(has_x, roll(cross[from_x, FAR_CORNER : FAR_CORNER + 64, :], 64)),
            kept(has_xy, roll(cross[from_xy, FAR_CORNER : FAR_CORNER + 64, :], 64)),
        )
        store_windows(-1, *[jnp.where(pi == 0, o, i) for o, i in zip(outside, inside)])
        store_windows(4, *[jnp.where(pi == 0, i, o) for o, i in zip(outside, inside)])

        row = lax.broadcasted_iota(jnp.int32, (256, 128), 0)
        diagonal = row // 64 == slot_of(256)
        block = lax.broadcasted_iota(jnp.int32, (128, 128), 0) // 32 == slot_of(128)
        leaves = []
        for a in range(4):
            total = jnp.zeros((256, 128), F32)
            for n in range(9):
                r, c = n // 3 - 1, n % 3 - 1
                matrix = near[a, :, n].reshape(256, 64)
                total = total + dot(matrix, windows[a + r, c])
            leaf = jnp.transpose(basis[a * 128 : (a + 1) * 128, :].astype(F32)).astype(BF)
            local = jnp.concatenate([local0[a]] * 4, axis=0)
            lift = dot(leaf, jnp.where(block, local, jnp.zeros_like(local)))
            total = total + jnp.concatenate([lift] * 4, axis=0)
            leaves.append(jnp.where(diagonal, total, 0.0).astype(BF))
        leaves = jnp.concatenate(leaves, axis=0)
        line = jnp.concatenate([order[g : g + 1, :] for g in range(8)], axis=1)
        for t in range(8):
            site = lax.broadcasted_iota(jnp.int32, (128, 1024), 0) + 128 * t
            pick = jnp.where(site == line, 1.0, 0.0).astype(BF)
            done = jnp.transpose(dot(pick, leaves))
            done = (done[:32] + done[32:64]) + (done[64:96] + done[96:])
            out[:, 128 * t : 128 * (t + 1)] = done.astype(BF)

    return body


def call(kernel, shapes, scratch=()):
    return pl.pallas_call(
        kernel,
        out_shape=shapes,
        scratch_shapes=list(scratch),
        compiler_params=pltpu.CompilerParams(vmem_limit_bytes=VMEM_BYTES),
    )


def groups_of_four(count_x, count_y, offset):
    return [
        [
            ((i + di) % count_x) * count_y + (j + dj) % count_y
            for di in range(2)
            for dj in range(2)
        ]
        for i in range(offset, count_x + offset, 2)
        for j in range(offset, count_y + offset, 2)
    ]


def solution(mesh):
    count_x, count_y = mesh.shape["gx"], mesh.shape["gy"]
    aligned = groups_of_four(count_x, count_y, 0)
    shifted = groups_of_four(count_x, count_y, 1)

    def local(samples, site_order, leaf_basis, near_blocks, transfer, coupling):
        samples = samples.T
        order = site_order.reshape(8, 128)
        basis = leaf_basis.transpose(0, 1, 3, 2).reshape(512, 64)
        transfer = transfer.reshape(256, 32)
        coupling = coupling.reshape(3840, 32)
        x, message = call(
            upward_kernel,
            (jax.ShapeDtypeStruct((256, 128), BF), jax.ShapeDtypeStruct((OWN_ROWS, 128), BF)),
        )(samples, order, basis, transfer)
        group = lax.all_gather(message, AXES, axis_index_groups=aligned)
        send = call(cross_kernel, jax.ShapeDtypeStruct((4, FAR_ROWS, 128), BF))(group, x)
        cross = lax.all_to_all(send, AXES, 0, 0, axis_index_groups=shifted)
        shared = lax.all_gather(cross[:, FAR_E2 : FAR_E2 + 32], AXES, axis_index_groups=aligned)
        out = call(
            downward_kernel(count_x, count_y),
            jax.ShapeDtypeStruct((32, 1024), BF),
            (
                pltpu.VMEM((3, 224, 224), BF),
                pltpu.VMEM((320, 256), BF),
                pltpu.VMEM((256, 256), BF),
                pltpu.VMEM((256, 256), BF),
            ),
        )(group, x, cross, shared, near_blocks, basis, transfer, coupling, order)
        return out.T

    return jax.shard_map(
        local,
        mesh=mesh,
        in_specs=(
            P(("gx", "gy"), None),
            P(("gx", "gy")),
            P("gx", "gy", None, None),
            P("gx", "gy", None, None, None),
            P(),
            P(),
        ),
        out_specs=P(("gx", "gy"), None),
        check_vma=False,
    )
```

```python
import jax
import jax.numpy as jnp
from jax import lax
from jax.experimental import pallas as pl
from jax.experimental.pallas import tpu as pltpu
from jax.sharding import PartitionSpec as P

BF = jnp.bfloat16
F32 = jnp.float32
AXES = ("gx", "gy")
VMEM_BYTES = 32 * 1024 * 1024
VMEM, FAR_MEMORY = pltpu.VMEM, pltpu.HBM

OWN_ROW, OWN_COL, OWN_E0, OWN_E1, OWN_E2, OWN_ROWS = 0, 64, 128, 256, 288, 320
FAR_X, FAR_E0, FAR_CORNER, FAR_E1, FAR_E1_SIDE, FAR_E2, FAR_ROWS = 0, 64, 128, 192, 224, 256, 288


def dot(a, b):
    return lax.dot_general(a, b, (((1,), (0,)), ((), ())), preferred_element_type=F32)


def dot_nt(a, b):
    return lax.dot_general(a, b, (((1,), (1,)), ((), ())), preferred_element_type=F32)


def roll(x, lanes):
    lanes = lanes % x.shape[1]
    if lanes == 0:
        return x
    if x.dtype == BF:
        return pltpu.roll(x.astype(F32), lanes, 1).astype(BF)
    return pltpu.roll(x, lanes, 1)


def lane_of(rows, lanes=128):
    return lax.broadcasted_iota(jnp.int32, (rows, lanes), 1)


def slot_of(rows, lanes=128):
    return lane_of(rows, lanes) // 32


def eye(n):
    row = lax.broadcasted_iota(jnp.int32, (n, n), 0)
    return jnp.where(row == lane_of(n, n), 1.0, 0.0).astype(BF)


def place():
    gx, gy = lax.axis_index("gx"), lax.axis_index("gy")
    return gx, gy, lax.rem(gx, 2), lax.rem(gy, 2)


def merge_diagonal(blocks, height):
    slot = slot_of(height)
    out = jnp.zeros((height, 128), F32)
    for b in range(4):
        out = jnp.where(slot == b, blocks[b * height : (b + 1) * height], out)
    return out


def fetch(sources, targets, sems):
    copies = [
        pltpu.make_async_copy(source, target, sems.at[n])
        for n, (source, target) in enumerate(zip(sources, targets))
    ]
    for copy in copies:
        copy.start()
    return copies


def upward_kernel(
    samples_hbm, order_hbm, basis_hbm, transfer_hbm, x_out, msg, samples, order, basis, transfer, sems
):
    copies = fetch(
        (order_hbm, samples_hbm, basis_hbm, transfer_hbm), (order, samples, basis, transfer), sems
    )
    _, _, pi, pj = place()
    copies[0].wait()
    copies[1].wait()
    slot = slot_of(64)
    spread = jnp.concatenate([samples[...]] * 4, axis=0)
    lane = lane_of(128)
    xs, e0s = [], []
    for a in range(4):
        picked = []
        for half in range(2):
            g = 2 * a + half
            line = order[g : g + 1, :].astype(F32)
            column = jnp.transpose(jnp.broadcast_to(line, (128, 128))).astype(jnp.int32)
            pick = jnp.concatenate(
                [jnp.where(column == lane + 128 * t, 1.0, 0.0).astype(BF) for t in range(8)],
                axis=1,
            )
            picked.append(dot_nt(pick, spread))
        x = merge_diagonal(jnp.concatenate(picked, axis=0), 64).astype(BF)
        if a == 0:
            copies[2].wait()
        x_out[a * 64 : (a + 1) * 64, :] = x
        e0 = merge_diagonal(dot(basis[a * 128 : (a + 1) * 128, :], x), 32).astype(BF)
        msg[OWN_E0 + a * 32 : OWN_E0 + (a + 1) * 32, :] = e0
        xs.append(x)
        e0s.append(e0)
    msg[OWN_ROW : OWN_ROW + 64, :] = jnp.where(pi == 0, xs[3], xs[0])
    column_slot = jnp.where(pj == 0, 3, 0)
    packed = jnp.zeros((64, 128), BF)
    for a in range(4):
        packed = jnp.where(slot == lax.rem(column_slot + a, 4), roll(xs[a], 32 * a), packed)
    msg[OWN_COL : OWN_COL + 64, :] = packed

    one = eye(32)
    slot = slot_of(32)
    copies[3].wait()
    turned = [dot_nt(one, transfer[n * 32 : (n + 1) * 32, :]).astype(BF) for n in range(8)]
    e1 = jnp.zeros((32, 128), F32)
    for x in range(2):
        parts = []
        for j in range(2):
            parts.append(dot(turned[j], e0s[2 * x]) + dot(turned[2 + j], e0s[2 * x + 1]))
        joined = parts[0] + roll(parts[1], -32)
        e1 = jnp.where(slot == 2 * x, roll(joined, 64 * x), e1)
        e1 = jnp.where(slot == 2 * x + 1, roll(joined, 64 * x - 32), e1)
    e1 = e1.astype(BF)
    msg[OWN_E1 : OWN_E1 + 32, :] = e1
    e2 = merge_diagonal(dot(jnp.concatenate(turned[4:], axis=0), e1), 32)
    e2 = e2 + roll(e2, 64)
    e2 = e2 + roll(e2, 32)
    msg[OWN_E2 : OWN_E2 + 32, :] = jnp.where(slot == 2 * pi + pj, e2, 0.0).astype(BF)


def cross_kernel(group, x, send):
    _, _, pi, pj = place()
    me, across_x, across_y = 2 * pi + pj, 2 * (1 - pi) + pj, 2 * pi + 1 - pj
    lane, slot = lane_of(64), slot_of(64)
    near_half = (lane < 64) == (pj == 0)
    e0 = group[me, OWN_E0 : OWN_E0 + 128, :]
    e0_rows = jnp.where(pi == 0, e0[:64], e0[64:])
    x_row = jnp.where(pi == 0, x[0:64, :], x[192:256, :])
    e1 = group[me, OWN_E1 : OWN_E1 + 32, :]
    e2 = group[0, OWN_E2 : OWN_ROWS, :]
    for m in range(1, 4):
        e2 = e2 + group[m, OWN_E2 : OWN_ROWS, :]
    for m in range(4):
        send[m, FAR_E2 : FAR_E2 + 32, :] = e2
        send[m, FAR_E1 : FAR_E1 + 32, :] = e1

    to = 2 * pi + 1 - pj
    send[to, FAR_X : FAR_X + 64, :] = x_row
    send[to, FAR_E0 : FAR_E0 + 64, :] = e0_rows
    column = group[across_y, OWN_COL : OWN_COL + 64, :]
    column = jnp.where(pi == 0, roll(column, 64), roll(column, -32))
    corner_e0 = group[across_y, pl.ds(OWN_E0 + 64 * pi, 64), :]
    send[to, FAR_CORNER : FAR_CORNER + 64, :] = jnp.where(near_half, corner_e0, column)
    send[to, FAR_E1_SIDE : FAR_E1_SIDE + 32, :] = group[across_y, OWN_E1 : OWN_E1 + 32, :]

    to = 2 * (1 - pi) + pj
    column_slot = jnp.where(pj == 0, 0, 3)
    packed = jnp.zeros((64, 128), BF)
    for a in range(4):
        moved = roll(x[a * 64 : (a + 1) * 64, :], 32 * a)
        packed = jnp.where(slot == lax.rem(column_slot + a, 4), moved, packed)
    send[to, FAR_X : FAR_X + 64, :] = packed
    send[to, FAR_E0 : FAR_E0 + 64, :] = jnp.where(near_half, e0[:64], roll(e0[64:], 64))
    corner_x = roll(group[across_x, OWN_ROW : OWN_ROW + 64, :], 64)
    corner_e0 = group[across_x, pl.ds(OWN_E0 + 64 * pi, 64), :]
    send[to, FAR_CORNER : FAR_CORNER + 64, :] = jnp.where(near_half, corner_e0, corner_x)
    send[to, FAR_E1_SIDE : FAR_E1_SIDE + 32, :] = group[across_x, OWN_E1 : OWN_E1 + 32, :]

    to = 2 * pi + pj
    send[to, FAR_X : FAR_X + 64, :] = jnp.zeros((64, 128), BF)
    send[to, FAR_E0 : FAR_E0 + 64, :] = jnp.zeros((64, 128), BF)
    send[to, FAR_CORNER : FAR_CORNER + 64, :] = jnp.where(near_half, e0_rows, roll(x_row, 64))
    send[to, FAR_E1_SIDE : FAR_E1_SIDE + 32, :] = jnp.zeros((32, 128), BF)

    to = 2 * (1 - pi) + 1 - pj
    send[to, 0:FAR_E1, :] = jnp.zeros((FAR_E1, 128), BF)
    send[to, FAR_E1_SIDE : FAR_E1_SIDE + 32, :] = jnp.zeros((32, 128), BF)


def store_row_of_tiles(halo, start, left, middle, right):
    lane = lane_of(32)
    low = lane < 64
    nothing = jnp.zeros((32, 128), BF)
    first = jnp.where(low, middle, roll(right, 64))
    second = jnp.where(low, roll(middle, 64), right)
    halo[pl.ds(start, 32), 0:128] = first
    halo[pl.ds(start, 32), 128:256] = jnp.where(low, nothing, roll(left, 64))
    halo[pl.ds(start + 32, 32), 0:128] = second
    halo[pl.ds(start + 32, 32), 128:256] = jnp.where(low, nothing, left)


def far_row(matrix, window, parity):
    lane = lane_of(224, 224)
    admitted = (lane >= 32 * (1 - parity)) & (lane < 224 - 32 * parity)
    product = dot(jnp.where(admitted, matrix, jnp.zeros((224, 224), BF)), window)
    odd = lax.rem(slot_of(32), 2) == 1
    out = jnp.zeros((32, 128), F32)
    for w in range(-3, 4):
        part = product[(w + 3) * 32 : (w + 4) * 32]
        part = part[:, :128] if w == 0 else pltpu.roll(part, (-32 * w) % 256, 1)[:, :128]
        if w == -3:
            part = jnp.where(odd, part, 0.0)
        if w == 3:
            part = jnp.where(odd, 0.0, part)
        out = out + part
    return out


def inner_kernel(group, x, near_hbm, coupling, near_out, far, near, sems):
    copies = fetch([near_hbm.at[a] for a in range(4)], [near.at[a] for a in range(4)], sems)
    _, _, pi, pj = place()
    across_x, across_y, across = 2 * (1 - pi) + pj, 2 * pi + 1 - pj, 2 * (1 - pi) + 1 - pj
    far[...] = jnp.zeros(far.shape, BF)
    for level in range(3):
        n = 0
        for u in range(-3, 4):
            for w in range(-3, 4):
                if max(abs(u), abs(w)) >= 2:
                    start = (level * 40 + n) * 32
                    far[level, (w + 3) * 32 : (w + 4) * 32, (u + 3) * 32 : (u + 4) * 32] = (
                        coupling[start : start + 32, :]
                    )
                    n += 1


    slot = slot_of(64)
    windows = {}

    def store_windows(a, middle, inner):
        left = jnp.where(pj == 0, jnp.zeros_like(inner), inner)
        right = jnp.where(pj == 0, inner, jnp.zeros_like(inner))
        windows[a, 0] = middle
        windows[a, -1] = roll(jnp.where(slot == 3, left, middle), 32)
        windows[a, 1] = roll(jnp.where(slot == 0, right, middle), -32)

    beside = group[across_y, OWN_COL : OWN_COL + 64, :]
    for a in range(4):
        store_windows(a, x[a * 64 : (a + 1) * 64, :], roll(beside, -32 * a))
    middle = group[across_x, OWN_ROW : OWN_ROW + 64, :]
    inner = group[across, OWN_ROW : OWN_ROW + 64, :]
    nothing = jnp.zeros((64, 128), BF)
    store_windows(-1, jnp.where(pi == 0, nothing, middle), jnp.where(pi == 0, nothing, inner))
    store_windows(4, jnp.where(pi == 0, middle, nothing), jnp.where(pi == 0, inner, nothing))
    for a in range(4):
        copies[a].wait()
        total = jnp.zeros((256, 128), F32)
        for n in range(9):
            matrix = near[a, :, n].reshape(256, 64)
            total = total + dot(matrix, windows[a + n // 3 - 1, n % 3 - 1])
        near_out[a * 64 : (a + 1) * 64, :] = merge_diagonal(total, 64)


def downward_kernel(count_x, count_y):
    def body(
        group, near_part, far, cross, shared, near_hbm, basis_hbm, transfer_hbm, order_hbm, out,
        h0, h1, h2, near_row, near_col, basis, transfer, order, sems,
    ):
        gx, gy, pi, pj = place()
        copies = fetch(
            (
                transfer_hbm,
                near_hbm.at[3 * pi, :, pl.ds(6 * pi, 3)],
                near_hbm.at[:, 3 * pj],
                basis_hbm,
                order_hbm,
            ),
            (transfer, near_row, near_col, basis, order),
            sems,
        )
        me, across_x, across_y = 2 * pi + pj, 2 * (1 - pi) + pj, 2 * pi + 1 - pj
        across = 2 * (1 - pi) + 1 - pj
        from_x, from_y, from_xy = 2 * pi + 1 - pj, 2 * (1 - pi) + pj, 2 * pi + pj
        has_x = jnp.where(pi == 0, gx > 0, gx < count_x - 1)
        has_y = jnp.where(pj == 0, gy > 0, gy < count_y - 1)
        has_xy = has_x & has_y

        def kept(keep, value):
            return jnp.where(keep, value, jnp.zeros_like(value))

        lane = lane_of(64)
        near_half = (lane < 64) == (pj == 0)
        h0[0:32, :] = jnp.zeros((32, 256), BF)
        h0[288:320, :] = jnp.zeros((32, 256), BF)
        h0[96:224, 0:128] = group[me, OWN_E0 : OWN_E0 + 128, :]
        strip = kept(has_y, cross[from_y, FAR_E0 : FAR_E0 + 64, :])
        beside = group[across_y, OWN_E0 : OWN_E0 + 128, :]
        h0[96:160, 128:256] = jnp.where(near_half, beside[:64], strip)
        h0[160:224, 128:256] = jnp.where(near_half, beside[64:], roll(strip, 64))
        start = 32 + 192 * (1 - pi)
        h0[pl.ds(start, 64), 0:128] = group[across_x, pl.ds(OWN_E0 + 64 * pi, 64), :]
        h0[pl.ds(start, 64), 128:256] = jnp.where(
            near_half,
            group[across, pl.ds(OWN_E0 + 64 * pi, 64), :],
            kept(has_y, cross[from_y, FAR_CORNER : FAR_CORNER + 64, :]),
        )
        start = 32 + 192 * pi
        h0[pl.ds(start, 64), 0:128] = kept(has_x, cross[from_x, FAR_E0 : FAR_E0 + 64, :])
        h0[pl.ds(start, 64), 128:256] = jnp.where(
            near_half,
            kept(has_x, cross[from_x, FAR_CORNER : FAR_CORNER + 64, :]),
            kept(has_xy, cross[from_xy, FAR_CORNER : FAR_CORNER + 64, :]),
        )

        def store_sides(start, middle, inner, outer):
            left = jnp.where(pj == 0, outer, inner)
            right = jnp.where(pj == 0, inner, outer)
            store_row_of_tiles(h1, start, left, middle, right)

        for halo in (h1, h2):
            halo[0:32, :] = jnp.zeros((32, 256), BF)
            halo[224:256, :] = jnp.zeros((32, 256), BF)
        own_e1 = slice(OWN_E1, OWN_E1 + 32)
        far_e1, side_e1 = slice(FAR_E1, FAR_E1 + 32), slice(FAR_E1_SIDE, FAR_E1_SIDE + 32)
        store_sides(
            96, group[me, own_e1, :], group[across_y, own_e1, :], kept(has_y, cross[from_y, far_e1, :])
        )
        store_sides(
            32 + 128 * (1 - pi),
            group[across_x, own_e1, :],
            group[across, own_e1, :],
            kept(has_y, cross[from_y, side_e1, :]),
        )
        store_sides(
            32 + 128 * pi,
            kept(has_x, cross[from_x, far_e1, :]),
            kept(has_x, cross[from_x, side_e1, :]),
            kept(has_xy, cross[from_xy, far_e1, :]),
        )

        above, below = gx >= 2, gx < count_x - 2
        before, after = gy >= 2, gy < count_y - 2
        e2 = group[0, OWN_E2:OWN_ROWS, :]
        for m in range(1, 4):
            e2 = e2 + group[m, OWN_E2:OWN_ROWS, :]
        store_row_of_tiles(
            h2,
            32,
            kept(above & before, shared[0, 0]),
            kept(above, shared[0, 1]),
            kept(above & after, shared[1, 1]),
        )
        store_row_of_tiles(h2, 96, kept(before, shared[0, 2]), e2, kept(after, shared[1, 3]))
        store_row_of_tiles(
            h2,
            160,
            kept(below & before, shared[2, 2]),
            kept(below, shared[2, 3]),
            kept(below & after, shared[3, 3]),
        )

        slot = slot_of(32)
        local2 = far_row(far[2], h2[pl.ds(32 * pi, 224), :], pi)
        local2 = jnp.where(slot == pj, local2, 0.0)
        local2 = local2 + roll(local2, 64)
        local2 = (local2 + roll(local2, 32)).astype(BF)
        copies[0].wait()
        spread = dot(transfer[128:256, :], local2)
        local1 = []
        for i in range(2):
            down = far_row(far[1], h1[32 * i : 32 * i + 224, :], i)
            for j in range(2):
                n = 2 * i + j
                down = down + jnp.where(slot == j, spread[n * 32 : (n + 1) * 32], 0.0)
            down = jnp.where(slot < 2, down, 0.0)
            wide = jnp.where(slot == 0, down, 0.0) + jnp.where(slot == 2, roll(down, 32), 0.0)
            local1.append((wide + roll(wide, 32)).astype(BF))
        local0 = []
        for i in range(4):
            spread = dot(transfer[64 * (i % 2) : 64 * (i % 2) + 64, :], local1[i // 2])
            down = far_row(far[0], h0[32 * i : 32 * i + 224, :], i % 2)
            down = down + jnp.where(lax.rem(slot, 2) == 0, spread[:32], spread[32:])
            local0.append(down.astype(BF))


        slot = slot_of(64)
        copies[1].wait()
        copies[2].wait()
        column = kept(has_y, cross[from_y, FAR_X : FAR_X + 64, :])
        corner_in = kept(has_y, roll(cross[from_y, FAR_CORNER : FAR_CORNER + 64, :], 64))
        corner_out = kept(has_xy, roll(cross[from_xy, FAR_CORNER : FAR_CORNER + 64, :], 64))
        boxes = {a: roll(column, -32 * a) for a in range(4)}
        boxes[-1] = jnp.where(pi == 0, corner_out, corner_in)
        boxes[4] = jnp.where(pi == 0, corner_in, corner_out)
        edge = slot == 3 * pj
        for a in boxes:
            moved = jnp.where(pj == 0, roll(boxes[a], 32), roll(boxes[a], -32))
            boxes[a] = jnp.where(edge, moved, jnp.zeros_like(moved))
        middle = kept(has_x, cross[from_x, FAR_X : FAR_X + 64, :])
        inner = kept(has_x, roll(cross[from_x, FAR_CORNER : FAR_CORNER + 64, :], 64))
        nothing = jnp.zeros_like(inner)
        left = jnp.where(pj == 0, nothing, inner)
        right = jnp.where(pj == 0, inner, nothing)
        shifts = (
            roll(jnp.where(slot == 3, left, middle), 32),
            middle,
            roll(jnp.where(slot == 0, right, middle), -32),
        )
        beyond = jnp.zeros((256, 128), F32)
        for c in range(3):
            beyond = beyond + dot(near_row[:, c].reshape(256, 64), shifts[c])
        beyond = merge_diagonal(beyond, 64)

        row = lax.broadcasted_iota(jnp.int32, (256, 128), 0)
        diagonal = row // 64 == slot_of(256)
        block = lax.broadcasted_iota(jnp.int32, (128, 128), 0) // 32 == slot_of(128)
        leaves = []
        copies[3].wait()
        for a in range(4):
            total = near_part[a * 64 : (a + 1) * 64, :]
            if a == 0:
                total = total + jnp.where(pi == 0, beyond, 0.0)
            if a == 3:
                total = total + jnp.where(pi == 0, 0.0, beyond)
            for r in range(3):
                total = total + dot(near_col[a, 3 * r + 2 * pj], boxes[a + r - 1])
            leaf = jnp.transpose(basis[a * 128 : (a + 1) * 128, :].astype(F32)).astype(BF)
            local = jnp.concatenate([local0[a]] * 4, axis=0)
            total = total + dot(leaf, jnp.where(block, local, jnp.zeros_like(local)))
            total = jnp.concatenate([total] * 4, axis=0)
            leaves.append(jnp.where(diagonal, total, 0.0).astype(BF))
        leaves = jnp.concatenate(leaves, axis=0)
        copies[4].wait()
        line = jnp.concatenate([order[g : g + 1, :] for g in range(8)], axis=1)
        for t in range(8):
            site = lax.broadcasted_iota(jnp.int32, (128, 1024), 0) + 128 * t
            pick = jnp.where(site == line, 1.0, 0.0).astype(BF)
            done = jnp.transpose(dot(pick, leaves))
            done = (done[:32] + done[32:64]) + (done[64:96] + done[96:])
            out[:, 128 * t : 128 * (t + 1)] = done.astype(BF)

    return body


def call(kernel, in_spaces, shapes, scratch=(), flops=10**6):
    return pl.pallas_call(
        kernel,
        in_specs=[pl.BlockSpec(memory_space=space) for space in in_spaces],
        out_shape=shapes,
        scratch_shapes=list(scratch),
        cost_estimate=pl.CostEstimate(flops=flops, bytes_accessed=2**20, transcendentals=0),
        compiler_params=pltpu.CompilerParams(vmem_limit_bytes=VMEM_BYTES),
    )


def groups_of_four(count_x, count_y, offset):
    return [
        [
            ((i + di) % count_x) * count_y + (j + dj) % count_y
            for di in range(2)
            for dj in range(2)
        ]
        for i in range(offset, count_x + offset, 2)
        for j in range(offset, count_y + offset, 2)
    ]


def solution(mesh):
    count_x, count_y = mesh.shape["gx"], mesh.shape["gy"]
    aligned = groups_of_four(count_x, count_y, 0)
    shifted = groups_of_four(count_x, count_y, 1)

    def local(samples, site_order, leaf_basis, near_blocks, transfer, coupling):
        samples = samples.T
        order = site_order.reshape(8, 128)
        basis = leaf_basis.transpose(0, 1, 3, 2).reshape(512, 64)
        transfer = transfer.reshape(256, 32)
        coupling = coupling.reshape(3840, 32)
        x, message = call(
            upward_kernel,
            (FAR_MEMORY,) * 4,
            (jax.ShapeDtypeStruct((256, 128), BF), jax.ShapeDtypeStruct((OWN_ROWS, 128), BF)),
            (
                pltpu.VMEM((32, 1024), BF),
                pltpu.VMEM((8, 128), jnp.int32),
                pltpu.VMEM((512, 64), BF),
                pltpu.VMEM((256, 32), BF),
                pltpu.SemaphoreType.DMA((4,)),
            ),
        )(samples, order, basis, transfer)
        group = lax.all_gather(message, AXES, axis_index_groups=aligned)
        send = call(cross_kernel, (VMEM,) * 2, jax.ShapeDtypeStruct((4, FAR_ROWS, 128), BF))(group, x)
        cross = lax.all_to_all(send, AXES, 0, 0, axis_index_groups=shifted)
        near_part, far = call(
            inner_kernel,
            (VMEM, VMEM, FAR_MEMORY, VMEM),
            (jax.ShapeDtypeStruct((256, 128), F32), jax.ShapeDtypeStruct((3, 224, 224), BF)),
            (pltpu.VMEM((4, 4, 9, 64, 64), BF), pltpu.SemaphoreType.DMA((4,))),
            flops=10**9,
        )(group, x, near_blocks, coupling)
        shared = lax.all_gather(cross[:, FAR_E2 : FAR_E2 + 32], AXES, axis_index_groups=aligned)
        out = call(
            downward_kernel(count_x, count_y),
            (VMEM,) * 5 + (FAR_MEMORY,) * 4,
            jax.ShapeDtypeStruct((32, 1024), BF),
            (
                pltpu.VMEM((320, 256), BF),
                pltpu.VMEM((256, 256), BF),
                pltpu.VMEM((256, 256), BF),
                pltpu.VMEM((4, 3, 64, 64), BF),
                pltpu.VMEM((4, 9, 64, 64), BF),
                pltpu.VMEM((512, 64), BF),
                pltpu.VMEM((256, 32), BF),
                pltpu.VMEM((8, 128), jnp.int32),
                pltpu.SemaphoreType.DMA((5,)),
            ),
        )(group, near_part, far, cross, shared, near_blocks, basis, transfer, order)
        return out.T

    return jax.shard_map(
        local,
        mesh=mesh,
        in_specs=(
            P(("gx", "gy"), None),
            P(("gx", "gy")),
            P("gx", "gy", None, None),
            P("gx", "gy", None, None, None),
            P(),
            P(),
        ),
        out_specs=P(("gx", "gy"), None),
        check_vma=False,
    )
```

```python
import jax
import jax.numpy as jnp
from jax import lax
from jax.experimental import pallas as pl
from jax.experimental.pallas import tpu as pltpu
from jax.sharding import PartitionSpec as P

BF = jnp.bfloat16
F32 = jnp.float32
AXES = ("gx", "gy")
VMEM_BYTES = 32 * 1024 * 1024
VMEM = pltpu.VMEM

OWN_ROW, OWN_COL, OWN_E0, OWN_E1, OWN_E2, OWN_ROWS = 0, 64, 128, 256, 288, 320
FAR_X, FAR_E0, FAR_CORNER, FAR_E1, FAR_E1_SIDE, FAR_E2, FAR_ROWS = 0, 64, 128, 192, 224, 256, 288


def dot(a, b):
    return lax.dot_general(a, b, (((1,), (0,)), ((), ())), preferred_element_type=F32)


def dot_nt(a, b):
    return lax.dot_general(a, b, (((1,), (1,)), ((), ())), preferred_element_type=F32)


def roll(x, lanes):
    lanes = lanes % x.shape[1]
    if lanes == 0:
        return x
    if x.dtype == BF:
        return pltpu.roll(x.astype(F32), lanes, 1).astype(BF)
    return pltpu.roll(x, lanes, 1)


def lane_of(rows, lanes=128):
    return lax.broadcasted_iota(jnp.int32, (rows, lanes), 1)


def slot_of(rows, lanes=128):
    return lane_of(rows, lanes) // 32


def eye(n):
    row = lax.broadcasted_iota(jnp.int32, (n, n), 0)
    return jnp.where(row == lane_of(n, n), 1.0, 0.0).astype(BF)


def place():
    gx, gy = lax.axis_index("gx"), lax.axis_index("gy")
    return gx, gy, lax.rem(gx, 2), lax.rem(gy, 2)


def merge_diagonal(blocks, height):
    slot = slot_of(height)
    out = jnp.zeros((height, 128), F32)
    for b in range(4):
        out = jnp.where(slot == b, blocks[b * height : (b + 1) * height], out)
    return out


def fetch(sources, targets, sems):
    copies = [
        pltpu.make_async_copy(source, target, sems.at[n])
        for n, (source, target) in enumerate(zip(sources, targets))
    ]
    for copy in copies:
        copy.start()
    return copies


def upward_kernel(
    samples_hbm, order_hbm, basis_hbm, transfer_hbm, coupling_hbm, near_hbm,
    x_out, msg, order, basis, transfer, coupling, near, samples, sems,
):
    copies = fetch(
        (order_hbm, samples_hbm, basis_hbm, transfer_hbm, coupling_hbm, near_hbm),
        (order, samples, basis, transfer, coupling, near),
        sems,
    )
    _, _, pi, pj = place()
    copies[0].wait()
    copies[1].wait()
    slot = slot_of(64)
    spread = jnp.concatenate([samples[...]] * 4, axis=0)
    lane = lane_of(128)
    xs, e0s = [], []
    for a in range(4):
        picked = []
        for half in range(2):
            g = 2 * a + half
            line = order[g : g + 1, :].astype(F32)
            column = jnp.transpose(jnp.broadcast_to(line, (128, 128))).astype(jnp.int32)
            pick = jnp.concatenate(
                [jnp.where(column == lane + 128 * t, 1.0, 0.0).astype(BF) for t in range(8)],
                axis=1,
            )
            picked.append(dot_nt(pick, spread))
        x = merge_diagonal(jnp.concatenate(picked, axis=0), 64).astype(BF)
        if a == 0:
            copies[2].wait()
        x_out[a * 64 : (a + 1) * 64, :] = x
        e0 = merge_diagonal(dot(basis[a * 128 : (a + 1) * 128, :], x), 32).astype(BF)
        msg[OWN_E0 + a * 32 : OWN_E0 + (a + 1) * 32, :] = e0
        xs.append(x)
        e0s.append(e0)
    msg[OWN_ROW : OWN_ROW + 64, :] = jnp.where(pi == 0, xs[3], xs[0])
    column_slot = jnp.where(pj == 0, 3, 0)
    packed = jnp.zeros((64, 128), BF)
    for a in range(4):
        packed = jnp.where(slot == lax.rem(column_slot + a, 4), roll(xs[a], 32 * a), packed)
    msg[OWN_COL : OWN_COL + 64, :] = packed

    one = eye(32)
    slot = slot_of(32)
    copies[3].wait()
    turned = [dot_nt(one, transfer[n * 32 : (n + 1) * 32, :]).astype(BF) for n in range(8)]
    e1 = jnp.zeros((32, 128), F32)
    for x in range(2):
        parts = []
        for j in range(2):
            parts.append(dot(turned[j], e0s[2 * x]) + dot(turned[2 + j], e0s[2 * x + 1]))
        joined = parts[0] + roll(parts[1], -32)
        e1 = jnp.where(slot == 2 * x, roll(joined, 64 * x), e1)
        e1 = jnp.where(slot == 2 * x + 1, roll(joined, 64 * x - 32), e1)
    e1 = e1.astype(BF)
    msg[OWN_E1 : OWN_E1 + 32, :] = e1
    e2 = merge_diagonal(dot(jnp.concatenate(turned[4:], axis=0), e1), 32)
    e2 = e2 + roll(e2, 64)
    e2 = e2 + roll(e2, 32)
    msg[OWN_E2 : OWN_E2 + 32, :] = jnp.where(slot == 2 * pi + pj, e2, 0.0).astype(BF)
    copies[4].wait()
    copies[5].wait()


def cross_kernel(group, x, send):
    _, _, pi, pj = place()
    me, across_x, across_y = 2 * pi + pj, 2 * (1 - pi) + pj, 2 * pi + 1 - pj
    lane, slot = lane_of(64), slot_of(64)
    near_half = (lane < 64) == (pj == 0)
    e0 = group[me, OWN_E0 : OWN_E0 + 128, :]
    e0_rows = jnp.where(pi == 0, e0[:64], e0[64:])
    x_row = jnp.where(pi == 0, x[0:64, :], x[192:256, :])
    e1 = group[me, OWN_E1 : OWN_E1 + 32, :]
    e2 = group[0, OWN_E2 : OWN_ROWS, :]
    for m in range(1, 4):
        e2 = e2 + group[m, OWN_E2 : OWN_ROWS, :]
    for m in range(4):
        send[m, FAR_E2 : FAR_E2 + 32, :] = e2
        send[m, FAR_E1 : FAR_E1 + 32, :] = e1

    to = 2 * pi + 1 - pj
    send[to, FAR_X : FAR_X + 64, :] = x_row
    send[to, FAR_E0 : FAR_E0 + 64, :] = e0_rows
    column = group[across_y, OWN_COL : OWN_COL + 64, :]
    column = jnp.where(pi == 0, roll(column, 64), roll(column, -32))
    corner_e0 = group[across_y, pl.ds(OWN_E0 + 64 * pi, 64), :]
    send[to, FAR_CORNER : FAR_CORNER + 64, :] = jnp.where(near_half, corner_e0, column)
    send[to, FAR_E1_SIDE : FAR_E1_SIDE + 32, :] = group[across_y, OWN_E1 : OWN_E1 + 32, :]

    to = 2 * (1 - pi) + pj
    column_slot = jnp.where(pj == 0, 0, 3)
    packed = jnp.zeros((64, 128), BF)
    for a in range(4):
        moved = roll(x[a * 64 : (a + 1) * 64, :], 32 * a)
        packed = jnp.where(slot == lax.rem(column_slot + a, 4), moved, packed)
    send[to, FAR_X : FAR_X + 64, :] = packed
    send[to, FAR_E0 : FAR_E0 + 64, :] = jnp.where(near_half, e0[:64], roll(e0[64:], 64))
    corner_x = roll(group[across_x, OWN_ROW : OWN_ROW + 64, :], 64)
    corner_e0 = group[across_x, pl.ds(OWN_E0 + 64 * pi, 64), :]
    send[to, FAR_CORNER : FAR_CORNER + 64, :] = jnp.where(near_half, corner_e0, corner_x)
    send[to, FAR_E1_SIDE : FAR_E1_SIDE + 32, :] = group[across_x, OWN_E1 : OWN_E1 + 32, :]

    to = 2 * pi + pj
    send[to, FAR_X : FAR_X + 64, :] = jnp.zeros((64, 128), BF)
    send[to, FAR_E0 : FAR_E0 + 64, :] = jnp.zeros((64, 128), BF)
    send[to, FAR_CORNER : FAR_CORNER + 64, :] = jnp.where(near_half, e0_rows, roll(x_row, 64))
    send[to, FAR_E1_SIDE : FAR_E1_SIDE + 32, :] = jnp.zeros((32, 128), BF)

    to = 2 * (1 - pi) + 1 - pj
    send[to, 0:FAR_E1, :] = jnp.zeros((FAR_E1, 128), BF)
    send[to, FAR_E1_SIDE : FAR_E1_SIDE + 32, :] = jnp.zeros((32, 128), BF)


def store_row_of_tiles(halo, start, left, middle, right):
    lane = lane_of(32)
    low = lane < 64
    nothing = jnp.zeros((32, 128), BF)
    first = jnp.where(low, middle, roll(right, 64))
    second = jnp.where(low, roll(middle, 64), right)
    halo[pl.ds(start, 32), 0:128] = first
    halo[pl.ds(start, 32), 128:256] = jnp.where(low, nothing, roll(left, 64))
    halo[pl.ds(start + 32, 32), 0:128] = second
    halo[pl.ds(start + 32, 32), 128:256] = jnp.where(low, nothing, left)


def far_row(matrix, window, parity):
    lane = lane_of(224, 224)
    admitted = (lane >= 32 * (1 - parity)) & (lane < 224 - 32 * parity)
    product = dot(jnp.where(admitted, matrix, jnp.zeros((224, 224), BF)), window)
    odd = lax.rem(slot_of(32), 2) == 1
    out = jnp.zeros((32, 128), F32)
    for w in range(-3, 4):
        part = product[(w + 3) * 32 : (w + 4) * 32]
        part = part[:, :128] if w == 0 else pltpu.roll(part, (-32 * w) % 256, 1)[:, :128]
        if w == -3:
            part = jnp.where(odd, part, 0.0)
        if w == 3:
            part = jnp.where(odd, 0.0, part)
        out = out + part
    return out


def inner_kernel(group, x, near, coupling, basis, order, near_out, far, leaf, pick):
    _, _, pi, pj = place()
    across_x, across_y, across = 2 * (1 - pi) + pj, 2 * pi + 1 - pj, 2 * (1 - pi) + 1 - pj
    far[...] = jnp.zeros(far.shape, BF)
    for level in range(3):
        n = 0
        for u in range(-3, 4):
            for w in range(-3, 4):
                if max(abs(u), abs(w)) >= 2:
                    start = (level * 40 + n) * 32
                    far[level, (w + 3) * 32 : (w + 4) * 32, (u + 3) * 32 : (u + 4) * 32] = (
                        coupling[start : start + 32, :]
                    )
                    n += 1


    slot = slot_of(64)
    windows = {}

    def store_windows(a, middle, inner):
        left = jnp.where(pj == 0, jnp.zeros_like(inner), inner)
        right = jnp.where(pj == 0, inner, jnp.zeros_like(inner))
        windows[a, 0] = middle
        windows[a, -1] = roll(jnp.where(slot == 3, left, middle), 32)
        windows[a, 1] = roll(jnp.where(slot == 0, right, middle), -32)

    beside = group[across_y, OWN_COL : OWN_COL + 64, :]
    for a in range(4):
        store_windows(a, x[a * 64 : (a + 1) * 64, :], roll(beside, -32 * a))
    middle = group[across_x, OWN_ROW : OWN_ROW + 64, :]
    inner = group[across, OWN_ROW : OWN_ROW + 64, :]
    nothing = jnp.zeros((64, 128), BF)
    store_windows(-1, jnp.where(pi == 0, nothing, middle), jnp.where(pi == 0, nothing, inner))
    store_windows(4, jnp.where(pi == 0, middle, nothing), jnp.where(pi == 0, inner, nothing))
    for a in range(4):
        total = jnp.zeros((256, 128), F32)
        for n in range(9):
            matrix = near[a, :, n].reshape(256, 64)
            total = total + dot(matrix, windows[a + n // 3 - 1, n % 3 - 1])
        near_out[a * 64 : (a + 1) * 64, :] = merge_diagonal(total, 64)
        turned = jnp.transpose(basis[a * 128 : (a + 1) * 128, :].astype(F32))
        leaf[a * 64 : (a + 1) * 64, :] = turned.astype(BF)
    line = jnp.concatenate([order[g : g + 1, :] for g in range(8)], axis=1)
    for t in range(8):
        site = lax.broadcasted_iota(jnp.int32, (128, 1024), 0) + 128 * t
        pick[128 * t : 128 * (t + 1), :] = jnp.where(site == line, 1.0, 0.0).astype(BF)


def downward_kernel(count_x, count_y):
    def body(
        group, near_part, far, leaf, pick, cross, shared, near, transfer, out, h0, h1, h2
    ):
        gx, gy, pi, pj = place()
        me, across_x, across_y = 2 * pi + pj, 2 * (1 - pi) + pj, 2 * pi + 1 - pj
        across = 2 * (1 - pi) + 1 - pj
        from_x, from_y, from_xy = 2 * pi + 1 - pj, 2 * (1 - pi) + pj, 2 * pi + pj
        has_x = jnp.where(pi == 0, gx > 0, gx < count_x - 1)
        has_y = jnp.where(pj == 0, gy > 0, gy < count_y - 1)
        has_xy = has_x & has_y

        def kept(keep, value):
            return jnp.where(keep, value, jnp.zeros_like(value))

        lane = lane_of(64)
        near_half = (lane < 64) == (pj == 0)
        h0[0:32, :] = jnp.zeros((32, 256), BF)
        h0[288:320, :] = jnp.zeros((32, 256), BF)
        h0[96:224, 0:128] = group[me, OWN_E0 : OWN_E0 + 128, :]
        strip = kept(has_y, cross[from_y, FAR_E0 : FAR_E0 + 64, :])
        beside = group[across_y, OWN_E0 : OWN_E0 + 128, :]
        h0[96:160, 128:256] = jnp.where(near_half, beside[:64], strip)
        h0[160:224, 128:256] = jnp.where(near_half, beside[64:], roll(strip, 64))
        start = 32 + 192 * (1 - pi)
        h0[pl.ds(start, 64), 0:128] = group[across_x, pl.ds(OWN_E0 + 64 * pi, 64), :]
        h0[pl.ds(start, 64), 128:256] = jnp.where(
            near_half,
            group[across, pl.ds(OWN_E0 + 64 * pi, 64), :],
            kept(has_y, cross[from_y, FAR_CORNER : FAR_CORNER + 64, :]),
        )
        start = 32 + 192 * pi
        h0[pl.ds(start, 64), 0:128] = kept(has_x, cross[from_x, FAR_E0 : FAR_E0 + 64, :])
        h0[pl.ds(start, 64), 128:256] = jnp.where(
            near_half,
            kept(has_x, cross[from_x, FAR_CORNER : FAR_CORNER + 64, :]),
            kept(has_xy, cross[from_xy, FAR_CORNER : FAR_CORNER + 64, :]),
        )

        def store_sides(start, middle, inner, outer):
            left = jnp.where(pj == 0, outer, inner)
            right = jnp.where(pj == 0, inner, outer)
            store_row_of_tiles(h1, start, left, middle, right)

        for halo in (h1, h2):
            halo[0:32, :] = jnp.zeros((32, 256), BF)
            halo[224:256, :] = jnp.zeros((32, 256), BF)
        own_e1 = slice(OWN_E1, OWN_E1 + 32)
        far_e1, side_e1 = slice(FAR_E1, FAR_E1 + 32), slice(FAR_E1_SIDE, FAR_E1_SIDE + 32)
        store_sides(
            96, group[me, own_e1, :], group[across_y, own_e1, :], kept(has_y, cross[from_y, far_e1, :])
        )
        store_sides(
            32 + 128 * (1 - pi),
            group[across_x, own_e1, :],
            group[across, own_e1, :],
            kept(has_y, cross[from_y, side_e1, :]),
        )
        store_sides(
            32 + 128 * pi,
            kept(has_x, cross[from_x, far_e1, :]),
            kept(has_x, cross[from_x, side_e1, :]),
            kept(has_xy, cross[from_xy, far_e1, :]),
        )

        above, below = gx >= 2, gx < count_x - 2
        before, after = gy >= 2, gy < count_y - 2
        e2 = group[0, OWN_E2:OWN_ROWS, :]
        for m in range(1, 4):
            e2 = e2 + group[m, OWN_E2:OWN_ROWS, :]
        store_row_of_tiles(
            h2,
            32,
            kept(above & before, shared[0, 0]),
            kept(above, shared[0, 1]),
            kept(above & after, shared[1, 1]),
        )
        store_row_of_tiles(h2, 96, kept(before, shared[0, 2]), e2, kept(after, shared[1, 3]))
        store_row_of_tiles(
            h2,
            160,
            kept(below & before, shared[2, 2]),
            kept(below, shared[2, 3]),
            kept(below & after, shared[3, 3]),
        )

        slot = slot_of(32)
        local2 = far_row(far[2], h2[pl.ds(32 * pi, 224), :], pi)
        local2 = jnp.where(slot == pj, local2, 0.0)
        local2 = local2 + roll(local2, 64)
        local2 = (local2 + roll(local2, 32)).astype(BF)
        spread = dot(transfer[128:256, :], local2)
        local1 = []
        for i in range(2):
            down = far_row(far[1], h1[32 * i : 32 * i + 224, :], i)
            for j in range(2):
                n = 2 * i + j
                down = down + jnp.where(slot == j, spread[n * 32 : (n + 1) * 32], 0.0)
            down = jnp.where(slot < 2, down, 0.0)
            wide = jnp.where(slot == 0, down, 0.0) + jnp.where(slot == 2, roll(down, 32), 0.0)
            local1.append((wide + roll(wide, 32)).astype(BF))
        local0 = []
        for i in range(4):
            spread = dot(transfer[64 * (i % 2) : 64 * (i % 2) + 64, :], local1[i // 2])
            down = far_row(far[0], h0[32 * i : 32 * i + 224, :], i % 2)
            down = down + jnp.where(lax.rem(slot, 2) == 0, spread[:32], spread[32:])
            local0.append(down.astype(BF))


        slot = slot_of(64)
        column = kept(has_y, cross[from_y, FAR_X : FAR_X + 64, :])
        corner_in = kept(has_y, roll(cross[from_y, FAR_CORNER : FAR_CORNER + 64, :], 64))
        corner_out = kept(has_xy, roll(cross[from_xy, FAR_CORNER : FAR_CORNER + 64, :], 64))
        boxes = {a: roll(column, -32 * a) for a in range(4)}
        boxes[-1] = jnp.where(pi == 0, corner_out, corner_in)
        boxes[4] = jnp.where(pi == 0, corner_in, corner_out)
        edge = slot == 3 * pj
        for a in boxes:
            moved = jnp.where(pj == 0, roll(boxes[a], 32), roll(boxes[a], -32))
            boxes[a] = jnp.where(edge, moved, jnp.zeros_like(moved))
        middle = kept(has_x, cross[from_x, FAR_X : FAR_X + 64, :])
        inner = kept(has_x, roll(cross[from_x, FAR_CORNER : FAR_CORNER + 64, :], 64))
        nothing = jnp.zeros_like(inner)
        left = jnp.where(pj == 0, nothing, inner)
        right = jnp.where(pj == 0, inner, nothing)
        shifts = (
            roll(jnp.where(slot == 3, left, middle), 32),
            middle,
            roll(jnp.where(slot == 0, right, middle), -32),
        )
        beyond = jnp.zeros((256, 128), F32)
        for c in range(3):
            beyond = beyond + dot(near[3 * pi, :, 6 * pi + c].reshape(256, 64), shifts[c])
        beyond = merge_diagonal(beyond, 64)

        row = lax.broadcasted_iota(jnp.int32, (256, 128), 0)
        diagonal = row // 64 == slot_of(256)
        block = lax.broadcasted_iota(jnp.int32, (128, 128), 0) // 32 == slot_of(128)
        leaves = []
        for a in range(4):
            total = near_part[a * 64 : (a + 1) * 64, :]
            if a == 0:
                total = total + jnp.where(pi == 0, beyond, 0.0)
            if a == 3:
                total = total + jnp.where(pi == 0, 0.0, beyond)
            for r in range(3):
                total = total + dot(near[a, 3 * pj, 3 * r + 2 * pj], boxes[a + r - 1])
            local = jnp.concatenate([local0[a]] * 4, axis=0)
            total = total + dot(leaf[a * 64 : (a + 1) * 64, :], jnp.where(block, local, jnp.zeros_like(local)))
            total = jnp.concatenate([total] * 4, axis=0)
            leaves.append(jnp.where(diagonal, total, 0.0).astype(BF))
        leaves = jnp.concatenate(leaves, axis=0)
        for t in range(8):
            done = jnp.transpose(dot(pick[128 * t : 128 * (t + 1), :], leaves))
            done = (done[:32] + done[32:64]) + (done[64:96] + done[96:])
            out[:, 128 * t : 128 * (t + 1)] = done.astype(BF)

    return body


def call(kernel, shapes, scratch=(), inputs=VMEM, flops=10**6):
    def run(*args):
        return pl.pallas_call(
            kernel,
            out_shape=shapes,
            in_specs=[pl.BlockSpec(memory_space=inputs)] * len(args),
            scratch_shapes=list(scratch),
            cost_estimate=pl.CostEstimate(flops=flops, bytes_accessed=2**20, transcendentals=0),
            compiler_params=pltpu.CompilerParams(vmem_limit_bytes=VMEM_BYTES),
        )(*[pltpu.with_memory_space_constraint(arg, inputs) for arg in args])

    return run


def groups_of_four(count_x, count_y, offset):
    return [
        [
            ((i + di) % count_x) * count_y + (j + dj) % count_y
            for di in range(2)
            for dj in range(2)
        ]
        for i in range(offset, count_x + offset, 2)
        for j in range(offset, count_y + offset, 2)
    ]


def solution(mesh):
    count_x, count_y = mesh.shape["gx"], mesh.shape["gy"]
    aligned = groups_of_four(count_x, count_y, 0)
    shifted = groups_of_four(count_x, count_y, 1)

    def local(samples, site_order, leaf_basis, near_blocks, transfer, coupling):
        samples = samples.T
        order = site_order.reshape(8, 128)
        basis = leaf_basis.transpose(0, 1, 3, 2).reshape(512, 64)
        transfer = transfer.reshape(256, 32)
        coupling = coupling.transpose(0, 2, 3, 1)
        x, message, order, basis, transfer, coupling, near = call(
            upward_kernel,
            (
                VMEM((256, 128), BF),
                VMEM((OWN_ROWS, 128), BF),
                VMEM((8, 128), jnp.int32),
                VMEM((512, 64), BF),
                VMEM((256, 32), BF),
                VMEM((3, 32, 32, 40), BF),
                VMEM((4, 4, 9, 64, 64), BF),
            ),
            (VMEM((32, 1024), BF), pltpu.SemaphoreType.DMA((6,))),
            inputs=pltpu.HBM,
        )(samples, order, basis, transfer, coupling, near_blocks)
        group = lax.all_gather(message, AXES, axis_index_groups=aligned)
        send = call(cross_kernel, VMEM((4, FAR_ROWS, 128), BF))(group, x)
        cross = lax.all_to_all(send, AXES, 0, 0, axis_index_groups=shifted)
        coupling = coupling.transpose(0, 3, 1, 2).reshape(3840, 32)
        near_part, far, leaf, pick = call(
            inner_kernel,
            (
                VMEM((256, 128), F32),
                VMEM((3, 224, 224), BF),
                VMEM((256, 128), BF),
                VMEM((1024, 1024), BF),
            ),
            flops=10**9,
        )(group, x, near, coupling, basis, order)
        shared = lax.all_gather(cross[:, FAR_E2 : FAR_E2 + 32], AXES, axis_index_groups=aligned)
        out = call(
            downward_kernel(count_x, count_y),
            jax.ShapeDtypeStruct((32, 1024), BF),
            (VMEM((320, 256), BF), VMEM((256, 256), BF), VMEM((256, 256), BF)),
        )(group, near_part, far, leaf, pick, cross, shared, near, transfer)
        return out.T

    return jax.shard_map(
        local,
        mesh=mesh,
        in_specs=(
            P(("gx", "gy"), None),
            P(("gx", "gy")),
            P("gx", "gy", None, None),
            P("gx", "gy", None, None, None),
            P(),
            P(),
        ),
        out_specs=P(("gx", "gy"), None),
        check_vma=False,
    )
```

```python
import functools

import jax
import jax.numpy as jnp
from jax import lax
from jax.experimental import pallas as pl
from jax.experimental.pallas import tpu as pltpu
from jax.sharding import PartitionSpec as P

BF = jnp.bfloat16
F32 = jnp.float32
AXES = ("gx", "gy")
VMEM_BYTES = 32 * 1024 * 1024
VMEM, HBM = pltpu.VMEM, pltpu.HBM

OWN_ROW, OWN_COL, OWN_E0, OWN_E1, OWN_E2, OWN_ROWS = 0, 64, 128, 256, 288, 320
FAR_X, FAR_E0, FAR_CORNER, FAR_E1, FAR_E1_SIDE, FAR_E2, FAR_ROWS = 0, 64, 128, 192, 224, 256, 288


def dot(a, b):
    return lax.dot_general(a, b, (((1,), (0,)), ((), ())), preferred_element_type=F32)


def dot_nt(a, b):
    return lax.dot_general(a, b, (((1,), (1,)), ((), ())), preferred_element_type=F32)


def roll(x, lanes):
    lanes = lanes % x.shape[1]
    if lanes == 0:
        return x
    if x.dtype == BF:
        return pltpu.roll(x.astype(F32), lanes, 1).astype(BF)
    return pltpu.roll(x, lanes, 1)


def lane_of(rows, lanes=128):
    return lax.broadcasted_iota(jnp.int32, (rows, lanes), 1)


def slot_of(rows, lanes=128):
    return lane_of(rows, lanes) // 32


def eye(n):
    row = lax.broadcasted_iota(jnp.int32, (n, n), 0)
    return jnp.where(row == lane_of(n, n), 1.0, 0.0).astype(BF)


def place():
    gx, gy = lax.axis_index("gx"), lax.axis_index("gy")
    return gx, gy, lax.rem(gx, 2), lax.rem(gy, 2)


def swap_of(gx, gy, count_x, count_y):
    end_x = (gx == 0) | (gx == count_x - 1)
    end_y = (gy == 0) | (gy == count_y - 1)
    along_y = jnp.where(lax.rem(gy + 3, 4) >= 2, 2, 0)
    along_x = jnp.where(lax.rem(gx + 3, 4) >= 2, 1, 0)
    return jnp.where(end_x & ~end_y, along_y, jnp.where(end_y & ~end_x, along_x, 0))


def merge_diagonal(blocks, height):
    slot = slot_of(height)
    out = jnp.zeros((height, 128), F32)
    for b in range(4):
        out = jnp.where(slot == b, blocks[b * height : (b + 1) * height], out)
    return out


def fetch(sources, targets, sems):
    copies = [
        pltpu.make_async_copy(source, target, sems.at[n])
        for n, (source, target) in enumerate(zip(sources, targets))
    ]
    for copy in copies:
        copy.start()
    return copies


def upward_kernel(
    samples_hbm, order_hbm, basis_hbm, transfer_hbm, x_out, msg, order, samples, basis, transfer, sems
):
    copies = fetch(
        (order_hbm, samples_hbm, basis_hbm, transfer_hbm), (order, samples, basis, transfer), sems
    )
    _, _, pi, pj = place()
    copies[0].wait()
    copies[1].wait()
    slot = slot_of(64)
    spread = jnp.concatenate([samples[...]] * 4, axis=0)
    lane = lane_of(128)
    xs, e0s = [], []
    for a in range(4):
        picked = []
        for half in range(2):
            g = 2 * a + half
            line = order[g : g + 1, :].astype(F32)
            column = jnp.transpose(jnp.broadcast_to(line, (128, 128))).astype(jnp.int32)
            pick = jnp.concatenate(
                [jnp.where(column == lane + 128 * t, 1.0, 0.0).astype(BF) for t in range(8)],
                axis=1,
            )
            picked.append(dot_nt(pick, spread))
        x = merge_diagonal(jnp.concatenate(picked, axis=0), 64).astype(BF)
        if a == 0:
            copies[2].wait()
        x_out[a * 64 : (a + 1) * 64, :] = x
        e0 = merge_diagonal(dot(basis[a * 128 : (a + 1) * 128, :], x), 32).astype(BF)
        msg[OWN_E0 + a * 32 : OWN_E0 + (a + 1) * 32, :] = e0
        xs.append(x)
        e0s.append(e0)
    msg[OWN_ROW : OWN_ROW + 64, :] = jnp.where(pi == 0, xs[3], xs[0])
    column_slot = jnp.where(pj == 0, 3, 0)
    packed = jnp.zeros((64, 128), BF)
    for a in range(4):
        packed = jnp.where(slot == lax.rem(column_slot + a, 4), roll(xs[a], 32 * a), packed)
    msg[OWN_COL : OWN_COL + 64, :] = packed

    one = eye(32)
    slot = slot_of(32)
    copies[3].wait()
    turned = [dot_nt(one, transfer[n * 32 : (n + 1) * 32, :]).astype(BF) for n in range(8)]
    e1 = jnp.zeros((32, 128), F32)
    for x in range(2):
        parts = []
        for j in range(2):
            parts.append(dot(turned[j], e0s[2 * x]) + dot(turned[2 + j], e0s[2 * x + 1]))
        joined = parts[0] + roll(parts[1], -32)
        e1 = jnp.where(slot == 2 * x, roll(joined, 64 * x), e1)
        e1 = jnp.where(slot == 2 * x + 1, roll(joined, 64 * x - 32), e1)
    e1 = e1.astype(BF)
    msg[OWN_E1 : OWN_E1 + 32, :] = e1
    e2 = merge_diagonal(dot(jnp.concatenate(turned[4:], axis=0), e1), 32)
    e2 = e2 + roll(e2, 64)
    e2 = e2 + roll(e2, 32)
    msg[OWN_E2 : OWN_E2 + 32, :] = jnp.where(slot == 2 * pi + pj, e2, 0.0).astype(BF)


def cross_kernel(group, x, send, *, count_x, count_y):
    gx, gy, pi, pj = place()
    swap = swap_of(gx, gy, count_x, count_y)
    me, across_x, across_y = 2 * pi + pj, 2 * (1 - pi) + pj, 2 * pi + 1 - pj
    lane, slot = lane_of(64), slot_of(64)
    near_half = (lane < 64) == (pj == 0)
    e0 = group[me, OWN_E0 : OWN_E0 + 128, :]
    e0_rows = jnp.where(pi == 0, e0[:64], e0[64:])
    x_row = jnp.where(pi == 0, x[0:64, :], x[192:256, :])
    e1 = group[me, OWN_E1 : OWN_E1 + 32, :]
    e2 = group[0, OWN_E2 : OWN_ROWS, :]
    for m in range(1, 4):
        e2 = e2 + group[m, OWN_E2 : OWN_ROWS, :]
    for m in range(4):
        send[m, FAR_E2 : FAR_E2 + 32, :] = e2
        send[m, FAR_E1 : FAR_E1 + 32, :] = e1

    to = (2 * pi + 1 - pj) ^ swap
    send[to, FAR_X : FAR_X + 64, :] = x_row
    send[to, FAR_E0 : FAR_E0 + 64, :] = e0_rows
    column = group[across_y, OWN_COL : OWN_COL + 64, :]
    column = jnp.where(pi == 0, roll(column, 64), roll(column, -32))
    corner_e0 = group[across_y, pl.ds(OWN_E0 + 64 * pi, 64), :]
    send[to, FAR_CORNER : FAR_CORNER + 64, :] = jnp.where(near_half, corner_e0, column)
    send[to, FAR_E1_SIDE : FAR_E1_SIDE + 32, :] = group[across_y, OWN_E1 : OWN_E1 + 32, :]

    to = (2 * (1 - pi) + pj) ^ swap
    column_slot = jnp.where(pj == 0, 0, 3)
    packed = jnp.zeros((64, 128), BF)
    for a in range(4):
        moved = roll(x[a * 64 : (a + 1) * 64, :], 32 * a)
        packed = jnp.where(slot == lax.rem(column_slot + a, 4), moved, packed)
    send[to, FAR_X : FAR_X + 64, :] = packed
    send[to, FAR_E0 : FAR_E0 + 64, :] = jnp.where(near_half, e0[:64], roll(e0[64:], 64))
    corner_x = roll(group[across_x, OWN_ROW : OWN_ROW + 64, :], 64)
    corner_e0 = group[across_x, pl.ds(OWN_E0 + 64 * pi, 64), :]
    send[to, FAR_CORNER : FAR_CORNER + 64, :] = jnp.where(near_half, corner_e0, corner_x)
    send[to, FAR_E1_SIDE : FAR_E1_SIDE + 32, :] = group[across_x, OWN_E1 : OWN_E1 + 32, :]

    to = (2 * pi + pj) ^ swap
    send[to, FAR_X : FAR_X + 64, :] = jnp.zeros((64, 128), BF)
    send[to, FAR_E0 : FAR_E0 + 64, :] = jnp.zeros((64, 128), BF)
    send[to, FAR_CORNER : FAR_CORNER + 64, :] = jnp.where(near_half, e0_rows, roll(x_row, 64))
    send[to, FAR_E1_SIDE : FAR_E1_SIDE + 32, :] = jnp.zeros((32, 128), BF)

    to = (2 * (1 - pi) + 1 - pj) ^ swap
    send[to, 0:FAR_E1, :] = jnp.zeros((FAR_E1, 128), BF)
    send[to, FAR_E1_SIDE : FAR_E1_SIDE + 32, :] = jnp.zeros((32, 128), BF)


def store_row_of_tiles(halo, start, left, middle, right):
    lane = lane_of(32)
    low = lane < 64
    nothing = jnp.zeros((32, 128), BF)
    first = jnp.where(low, middle, roll(right, 64))
    second = jnp.where(low, roll(middle, 64), right)
    halo[pl.ds(start, 32), 0:128] = first
    halo[pl.ds(start, 32), 128:256] = jnp.where(low, nothing, roll(left, 64))
    halo[pl.ds(start + 32, 32), 0:128] = second
    halo[pl.ds(start + 32, 32), 128:256] = jnp.where(low, nothing, left)


def far_row(matrix, window, parity):
    lane = lane_of(224, 224)
    admitted = (lane >= 32 * (1 - parity)) & (lane < 224 - 32 * parity)
    product = dot(jnp.where(admitted, matrix, jnp.zeros((224, 224), BF)), window)
    odd = lax.rem(slot_of(32), 2) == 1
    out = jnp.zeros((32, 128), F32)
    for w in range(-3, 4):
        part = product[(w + 3) * 32 : (w + 4) * 32]
        part = part[:, :128] if w == 0 else pltpu.roll(part, (-32 * w) % 256, 1)[:, :128]
        if w == -3:
            part = jnp.where(odd, part, 0.0)
        if w == 3:
            part = jnp.where(odd, 0.0, part)
        out = out + part
    return out


def turn_coupling(coupling, turned, far):
    row = lax.broadcasted_iota(jnp.int32, (56, 40), 0)
    number = lane_of(56, 40)
    u, w = row // 8 - 3, row % 8 - 3
    outer = (abs(u) >= 2) & (w <= 3)
    inner = (abs(u) < 2) & (abs(w) >= 2) & (w <= 3)
    index = jnp.where(u < -1, (u + 3) * 7 + w + 3, 26 + (u - 2) * 7 + w + 3)
    index = jnp.where(abs(u) < 2, 14 + (u + 1) * 4 + jnp.where(w < 0, w + 3, w), index)
    choose = jnp.where((outer | inner) & (number == index), 1.0, 0.0).astype(BF)
    slot = slot_of(8)
    for level in range(3):
        for block in range(8):
            lines = coupling[level, 4 * block : 4 * block + 4].reshape(128, 40)
            part = dot_nt(choose, lines)
            moved = [part] + [pltpu.roll(part, 32 * q, 1) for q in range(1, 4)]
            for q in range(4):
                i = 4 * block + q
                for half in range(2):
                    out = jnp.zeros((8, 128), F32)
                    for u in range(4 * half, min(4 * half + 4, 7)):
                        piece = moved[(u - q) % 4][8 * u : 8 * u + 8]
                        out = jnp.where(slot == u % 4, piece, out)
                    turned[half][pl.ds(i, 8, stride=32), :] = out
        for half in range(2):
            lines = turned[half][0:224, :].astype(BF)
            far[level, :, 128 * half : 128 * half + 128] = lines


def inner_kernel(
    group, x, near_hbm, coupling_hbm, basis_hbm, order_hbm,
    near_out, far, leaf_hbm, pick_hbm,
    near, coupling, basis, order, turned_low, turned_high, leaf, pick, sems,
):
    copies = fetch(
        [order_hbm, basis_hbm, coupling_hbm] + [near_hbm.at[a] for a in range(4)],
        [order, basis, coupling] + [near.at[a] for a in range(4)],
        sems,
    )
    _, _, pi, pj = place()
    across_x, across_y, across = 2 * (1 - pi) + pj, 2 * pi + 1 - pj, 2 * (1 - pi) + 1 - pj
    copies[0].wait()
    line = jnp.concatenate([order[g : g + 1, :] for g in range(8)], axis=1)
    for t in range(8):
        site = lax.broadcasted_iota(jnp.int32, (128, 1024), 0) + 128 * t
        pick[128 * t : 128 * (t + 1), :] = jnp.where(site == line, 1.0, 0.0).astype(BF)
    pick_copy = pltpu.make_async_copy(pick, pick_hbm, sems.at[7])
    pick_copy.start()
    copies[1].wait()
    for a in range(4):
        flat = jnp.transpose(basis[a * 128 : (a + 1) * 128, :].astype(F32))
        leaf[a * 64 : (a + 1) * 64, :] = flat.astype(BF)
    leaf_copy = pltpu.make_async_copy(leaf, leaf_hbm, sems.at[8])
    leaf_copy.start()
    copies[2].wait()
    turn_coupling(coupling, (turned_low, turned_high), far)

    slot = slot_of(64)
    windows = {}

    def store_windows(a, middle, inner):
        left = jnp.where(pj == 0, jnp.zeros_like(inner), inner)
        right = jnp.where(pj == 0, inner, jnp.zeros_like(inner))
        windows[a, 0] = middle
        windows[a, -1] = roll(jnp.where(slot == 3, left, middle), 32)
        windows[a, 1] = roll(jnp.where(slot == 0, right, middle), -32)

    beside = group[across_y, OWN_COL : OWN_COL + 64, :]
    for a in range(4):
        store_windows(a, x[a * 64 : (a + 1) * 64, :], roll(beside, -32 * a))
    middle = group[across_x, OWN_ROW : OWN_ROW + 64, :]
    inner = group[across, OWN_ROW : OWN_ROW + 64, :]
    nothing = jnp.zeros((64, 128), BF)
    store_windows(-1, jnp.where(pi == 0, nothing, middle), jnp.where(pi == 0, nothing, inner))
    store_windows(4, jnp.where(pi == 0, middle, nothing), jnp.where(pi == 0, inner, nothing))
    for a in range(4):
        copies[3 + a].wait()
        total = jnp.zeros((256, 128), F32)
        for n in range(9):
            matrix = near[a, :, n].reshape(256, 64)
            total = total + dot(matrix, windows[a + n // 3 - 1, n % 3 - 1])
        near_out[a * 64 : (a + 1) * 64, :] = merge_diagonal(total, 64)
    pick_copy.wait()
    leaf_copy.wait()


def downward_kernel(count_x, count_y):
    def body(
        group, near_part, far, cross, shared, transfer_hbm, near_hbm, leaf_hbm, pick_hbm, out,
        h0, h1, h2, transfer, near_row, near_col, leaf, pick, sems,
    ):
        gx, gy, pi, pj = place()
        copies = fetch(
            (
                transfer_hbm,
                near_hbm.at[3 * pi, :, pl.ds(6 * pi, 3)],
                near_hbm.at[:, 3 * pj],
                leaf_hbm,
                pick_hbm,
            ),
            (transfer, near_row, near_col, leaf, pick),
            sems,
        )
        swap = swap_of(gx, gy, count_x, count_y)
        me, across_x, across_y = 2 * pi + pj, 2 * (1 - pi) + pj, 2 * pi + 1 - pj
        across = 2 * (1 - pi) + 1 - pj
        from_x, from_y = (2 * pi + 1 - pj) ^ swap, (2 * (1 - pi) + pj) ^ swap
        from_xy = (2 * pi + pj) ^ swap
        has_x = jnp.where(pi == 0, gx > 0, gx < count_x - 1)
        has_y = jnp.where(pj == 0, gy > 0, gy < count_y - 1)
        has_xy = has_x & has_y

        def kept(keep, value):
            return jnp.where(keep, value, jnp.zeros_like(value))

        lane = lane_of(64)
        near_half = (lane < 64) == (pj == 0)
        h0[0:32, :] = jnp.zeros((32, 256), BF)
        h0[288:320, :] = jnp.zeros((32, 256), BF)
        h0[96:224, 0:128] = group[me, OWN_E0 : OWN_E0 + 128, :]
        strip = kept(has_y, cross[from_y, FAR_E0 : FAR_E0 + 64, :])
        beside = group[across_y, OWN_E0 : OWN_E0 + 128, :]
        h0[96:160, 128:256] = jnp.where(near_half, beside[:64], strip)
        h0[160:224, 128:256] = jnp.where(near_half, beside[64:], roll(strip, 64))
        start = 32 + 192 * (1 - pi)
        h0[pl.ds(start, 64), 0:128] = group[across_x, pl.ds(OWN_E0 + 64 * pi, 64), :]
        h0[pl.ds(start, 64), 128:256] = jnp.where(
            near_half,
            group[across, pl.ds(OWN_E0 + 64 * pi, 64), :],
            kept(has_y, cross[from_y, FAR_CORNER : FAR_CORNER + 64, :]),
        )
        start = 32 + 192 * pi
        h0[pl.ds(start, 64), 0:128] = kept(has_x, cross[from_x, FAR_E0 : FAR_E0 + 64, :])
        h0[pl.ds(start, 64), 128:256] = jnp.where(
            near_half,
            kept(has_x, cross[from_x, FAR_CORNER : FAR_CORNER + 64, :]),
            kept(has_xy, cross[from_xy, FAR_CORNER : FAR_CORNER + 64, :]),
        )

        def store_sides(start, middle, inner, outer):
            left = jnp.where(pj == 0, outer, inner)
            right = jnp.where(pj == 0, inner, outer)
            store_row_of_tiles(h1, start, left, middle, right)

        for halo in (h1, h2):
            halo[0:32, :] = jnp.zeros((32, 256), BF)
            halo[224:256, :] = jnp.zeros((32, 256), BF)
        own_e1 = slice(OWN_E1, OWN_E1 + 32)
        far_e1, side_e1 = slice(FAR_E1, FAR_E1 + 32), slice(FAR_E1_SIDE, FAR_E1_SIDE + 32)
        store_sides(
            96, group[me, own_e1, :], group[across_y, own_e1, :], kept(has_y, cross[from_y, far_e1, :])
        )
        store_sides(
            32 + 128 * (1 - pi),
            group[across_x, own_e1, :],
            group[across, own_e1, :],
            kept(has_y, cross[from_y, side_e1, :]),
        )
        store_sides(
            32 + 128 * pi,
            kept(has_x, cross[from_x, far_e1, :]),
            kept(has_x, cross[from_x, side_e1, :]),
            kept(has_xy, cross[from_xy, far_e1, :]),
        )

        above, below = gx >= 2, gx < count_x - 2
        before, after = gy >= 2, gy < count_y - 2
        e2 = group[0, OWN_E2:OWN_ROWS, :]
        for m in range(1, 4):
            e2 = e2 + group[m, OWN_E2:OWN_ROWS, :]

        def brought(m, slot, keep):
            other = swap_of(gx - pi + m // 2, gy - pj + m % 2, count_x, count_y)
            return kept(keep, shared[m, slot ^ other])

        store_row_of_tiles(
            h2, 32, brought(0, 0, above & before), brought(0, 1, above), brought(1, 1, above & after)
        )
        store_row_of_tiles(h2, 96, brought(0, 2, before), e2, brought(1, 3, after))
        store_row_of_tiles(
            h2, 160, brought(2, 2, below & before), brought(2, 3, below), brought(3, 3, below & after)
        )

        slot = slot_of(32)
        local2 = far_row(far[2, :, :224], h2[pl.ds(32 * pi, 224), :], pi)
        local2 = jnp.where(slot == pj, local2, 0.0)
        local2 = local2 + roll(local2, 64)
        local2 = (local2 + roll(local2, 32)).astype(BF)
        copies[0].wait()
        spread = dot(transfer[128:256, :], local2)
        local1 = []
        for i in range(2):
            down = far_row(far[1, :, :224], h1[32 * i : 32 * i + 224, :], i)
            for j in range(2):
                n = 2 * i + j
                down = down + jnp.where(slot == j, spread[n * 32 : (n + 1) * 32], 0.0)
            down = jnp.where(slot < 2, down, 0.0)
            wide = jnp.where(slot == 0, down, 0.0) + jnp.where(slot == 2, roll(down, 32), 0.0)
            local1.append((wide + roll(wide, 32)).astype(BF))
        local0 = []
        for i in range(4):
            spread = dot(transfer[64 * (i % 2) : 64 * (i % 2) + 64, :], local1[i // 2])
            down = far_row(far[0, :, :224], h0[32 * i : 32 * i + 224, :], i % 2)
            down = down + jnp.where(lax.rem(slot, 2) == 0, spread[:32], spread[32:])
            local0.append(down.astype(BF))


        slot = slot_of(64)
        copies[1].wait()
        copies[2].wait()
        column = kept(has_y, cross[from_y, FAR_X : FAR_X + 64, :])
        corner_in = kept(has_y, roll(cross[from_y, FAR_CORNER : FAR_CORNER + 64, :], 64))
        corner_out = kept(has_xy, roll(cross[from_xy, FAR_CORNER : FAR_CORNER + 64, :], 64))
        boxes = {a: roll(column, -32 * a) for a in range(4)}
        boxes[-1] = jnp.where(pi == 0, corner_out, corner_in)
        boxes[4] = jnp.where(pi == 0, corner_in, corner_out)
        edge = slot == 3 * pj
        for a in boxes:
            moved = jnp.where(pj == 0, roll(boxes[a], 32), roll(boxes[a], -32))
            boxes[a] = jnp.where(edge, moved, jnp.zeros_like(moved))
        middle = kept(has_x, cross[from_x, FAR_X : FAR_X + 64, :])
        inner = kept(has_x, roll(cross[from_x, FAR_CORNER : FAR_CORNER + 64, :], 64))
        nothing = jnp.zeros_like(inner)
        left = jnp.where(pj == 0, nothing, inner)
        right = jnp.where(pj == 0, inner, nothing)
        shifts = (
            roll(jnp.where(slot == 3, left, middle), 32),
            middle,
            roll(jnp.where(slot == 0, right, middle), -32),
        )
        beyond = jnp.zeros((256, 128), F32)
        for c in range(3):
            beyond = beyond + dot(near_row[:, c].reshape(256, 64), shifts[c])
        beyond = merge_diagonal(beyond, 64)

        row = lax.broadcasted_iota(jnp.int32, (256, 128), 0)
        diagonal = row // 64 == slot_of(256)
        block = lax.broadcasted_iota(jnp.int32, (128, 128), 0) // 32 == slot_of(128)
        leaves = []
        copies[3].wait()
        for a in range(4):
            total = near_part[a * 64 : (a + 1) * 64, :]
            if a == 0:
                total = total + jnp.where(pi == 0, beyond, 0.0)
            if a == 3:
                total = total + jnp.where(pi == 0, 0.0, beyond)
            for r in range(3):
                total = total + dot(near_col[a, 3 * r + 2 * pj], boxes[a + r - 1])
            local = jnp.concatenate([local0[a]] * 4, axis=0)
            total = total + dot(leaf[a * 64 : (a + 1) * 64, :], jnp.where(block, local, jnp.zeros_like(local)))
            total = jnp.concatenate([total] * 4, axis=0)
            leaves.append(jnp.where(diagonal, total, 0.0).astype(BF))
        leaves = jnp.concatenate(leaves, axis=0)
        copies[4].wait()
        for t in range(8):
            done = jnp.transpose(dot(pick[128 * t : 128 * (t + 1), :], leaves))
            done = (done[:32] + done[32:64]) + (done[64:96] + done[96:])
            out[:, 128 * t : 128 * (t + 1)] = done.astype(BF)

    return body


def call(kernel, spaces, shapes, scratch=(), flops=10**6):
    def run(*args):
        return pl.pallas_call(
            kernel,
            out_shape=shapes,
            in_specs=[pl.BlockSpec(memory_space=space) for space in spaces],
            out_specs=jax.tree.map(lambda shape: pl.BlockSpec(memory_space=shape.memory_space), shapes),
            scratch_shapes=list(scratch),
            cost_estimate=pl.CostEstimate(flops=flops, bytes_accessed=2**20, transcendentals=0),
            compiler_params=pltpu.CompilerParams(vmem_limit_bytes=VMEM_BYTES),
        )(*map(pltpu.with_memory_space_constraint, args, spaces))

    return run


def aligned_groups(count_x, count_y):
    return [
        [(i + di) * count_y + j + dj for di in range(2) for dj in range(2)]
        for i in range(0, count_x, 2)
        for j in range(0, count_y, 2)
    ]


def shifted_groups(count_x, count_y):
    last_x, last_y = count_x - 1, count_y - 1
    groups = [
        [(i, j), (i, j + 1), (i + 1, j), (i + 1, j + 1)]
        for i in range(1, last_x, 2)
        for j in range(1, last_y, 2)
    ]
    for i in (0, last_x):
        for j in range(1, last_y, 4):
            second = [(i, j + 2), (i, j + 3)] if j + 3 < last_y else [(i, last_y), (i, 0)]
            first = [(i, j), (i, j + 1)]
            groups.append(second + first if i == 0 else first + second)
    for i in range(1, last_x, 4):
        if i + 3 < last_x:
            for j in (0, last_y):
                lanes = (i + 2, i) if j == 0 else (i, i + 2)
                groups.append([(g + d, j) for d in range(2) for g in lanes])
        else:
            groups.append([(i + d, j) for d in range(2) for j in (last_y, 0)])
    return [[i * count_y + j for i, j in group] for group in groups]


def solution(mesh):
    count_x, count_y = mesh.shape["gx"], mesh.shape["gy"]
    aligned = aligned_groups(count_x, count_y)
    shifted = shifted_groups(count_x, count_y)

    def local(samples, site_order, leaf_basis, near_blocks, transfer, coupling):
        samples = samples.T
        order = site_order.reshape(8, 128)
        basis = leaf_basis.transpose(0, 1, 3, 2).reshape(512, 64)
        transfer = transfer.reshape(256, 32)
        coupling = coupling.transpose(0, 2, 3, 1)
        x, message = call(
            upward_kernel,
            (HBM,) * 4,
            (VMEM((256, 128), BF), VMEM((OWN_ROWS, 128), BF)),
            (
                VMEM((8, 128), jnp.int32),
                VMEM((32, 1024), BF),
                VMEM((512, 64), BF),
                VMEM((256, 32), BF),
                pltpu.SemaphoreType.DMA((4,)),
            ),
        )(samples, order, basis, transfer)
        group = lax.all_gather(message, AXES, axis_index_groups=aligned)
        cross_body = functools.partial(cross_kernel, count_x=count_x, count_y=count_y)
        send = call(cross_body, (VMEM,) * 2, VMEM((4, FAR_ROWS, 128), BF))(group, x)
        cross = lax.all_to_all(send, AXES, 0, 0, axis_index_groups=shifted)
        near_part, far, leaf, pick = call(
            inner_kernel,
            (VMEM,) * 2 + (HBM,) * 4,
            (
                VMEM((256, 128), F32),
                VMEM((3, 224, 256), BF),
                HBM((256, 128), BF),
                HBM((1024, 1024), BF),
            ),
            (
                VMEM((4, 4, 9, 64, 64), BF),
                VMEM((3, 32, 32, 40), BF),
                VMEM((512, 64), BF),
                VMEM((8, 128), jnp.int32),
                VMEM((256, 128), F32),
                VMEM((256, 128), F32),
                VMEM((256, 128), BF),
                VMEM((1024, 1024), BF),
                pltpu.SemaphoreType.DMA((9,)),
            ),
            flops=10**9,
        )(group, x, near_blocks, coupling, basis, order)
        shared = lax.all_gather(cross[:, FAR_E2 : FAR_E2 + 32], AXES, axis_index_groups=aligned)
        out = call(
            downward_kernel(count_x, count_y),
            (VMEM,) * 5 + (HBM,) * 4,
            VMEM((32, 1024), BF),
            (
                VMEM((320, 256), BF),
                VMEM((256, 256), BF),
                VMEM((256, 256), BF),
                VMEM((256, 32), BF),
                VMEM((4, 3, 64, 64), BF),
                VMEM((4, 9, 64, 64), BF),
                VMEM((256, 128), BF),
                VMEM((1024, 1024), BF),
                pltpu.SemaphoreType.DMA((5,)),
            ),
        )(group, near_part, far, cross, shared, transfer, near_blocks, leaf, pick)
        return out.T

    return jax.shard_map(
        local,
        mesh=mesh,
        in_specs=(
            P(("gx", "gy"), None),
            P(("gx", "gy")),
            P("gx", "gy", None, None),
            P("gx", "gy", None, None, None),
            P(),
            P(),
        ),
        out_specs=P(("gx", "gy"), None),
        check_vma=False,
    )
```

```python
import functools

import jax
import jax.numpy as jnp
from jax import lax
from jax.experimental import pallas as pl
from jax.experimental.pallas import tpu as pltpu
from jax.sharding import PartitionSpec as P

BF = jnp.bfloat16
F32 = jnp.float32
AXES = ("gx", "gy")
VMEM_BYTES = 32 * 1024 * 1024
VMEM, HBM = pltpu.VMEM, pltpu.HBM

OWN_ROW, OWN_COL, OWN_E0, OWN_E1, OWN_E2, OWN_ROWS = 0, 64, 128, 256, 288, 320
FAR_X, FAR_E0, FAR_CORNER, FAR_E1, FAR_E1_SIDE, FAR_E2, FAR_ROWS = 0, 64, 128, 192, 224, 256, 288


def dot(a, b):
    return lax.dot_general(a, b, (((1,), (0,)), ((), ())), preferred_element_type=F32)


def dot_nt(a, b):
    return lax.dot_general(a, b, (((1,), (1,)), ((), ())), preferred_element_type=F32)


def roll(x, lanes):
    lanes = lanes % x.shape[1]
    if lanes == 0:
        return x
    if x.dtype == BF:
        return pltpu.roll(x.astype(F32), lanes, 1).astype(BF)
    return pltpu.roll(x, lanes, 1)


def lane_of(rows, lanes=128):
    return lax.broadcasted_iota(jnp.int32, (rows, lanes), 1)


def slot_of(rows, lanes=128):
    return lane_of(rows, lanes) // 32


def eye(n):
    row = lax.broadcasted_iota(jnp.int32, (n, n), 0)
    return jnp.where(row == lane_of(n, n), 1.0, 0.0).astype(BF)


def place():
    gx, gy = lax.axis_index("gx"), lax.axis_index("gy")
    return gx, gy, lax.rem(gx, 2), lax.rem(gy, 2)


def swap_of(gx, gy, count_x, count_y):
    end_x = (gx == 0) | (gx == count_x - 1)
    end_y = (gy == 0) | (gy == count_y - 1)
    along_y = jnp.where((lax.rem(gy + 3, 4) < 2) & (gy > 2), 2, 0)
    along_x = jnp.where(lax.rem(gx + 3, 4) >= 2, 1, 0)
    return jnp.where(end_x & ~end_y, along_y, jnp.where(end_y & ~end_x, along_x, 0))


def merge_diagonal(blocks, height):
    slot = slot_of(height)
    out = jnp.zeros((height, 128), F32)
    for b in range(4):
        out = jnp.where(slot == b, blocks[b * height : (b + 1) * height], out)
    return out


def split_order(order):
    lane = lane_of(1)
    lines = []
    for pair in range(2):
        for b in range(4):
            low = order[4 * pair + b // 2 : 4 * pair + b // 2 + 1, :]
            high = order[4 * pair + 2 + b // 2 : 4 * pair + 3 + b // 2, :]
            if b % 2 == 0:
                lines.append(jnp.where(lane < 64, low, pltpu.roll(high, 64, 1)))
            else:
                lines.append(jnp.where(lane < 64, pltpu.roll(low, 64, 1), high))
    lines = jnp.concatenate(lines, axis=0)
    return lines // 128, lines % 128


def pick_sites(within):
    row = lax.broadcasted_iota(jnp.int32, (128, 128), 0)
    return jnp.where(within == row, 1.0, 0.0).astype(BF)


def fetch(sources, targets, sems):
    copies = [
        pltpu.make_async_copy(source, target, sems.at[n])
        for n, (source, target) in enumerate(zip(sources, targets))
    ]
    for copy in copies:
        copy.start()
    return copies


def upward_kernel(
    samples_hbm, order_hbm, basis_hbm, transfer_hbm, x_out, msg, order, samples, basis, transfer, sems
):
    copies = fetch(
        (order_hbm, samples_hbm, basis_hbm, transfer_hbm), (order, samples, basis, transfer), sems
    )
    _, _, pi, pj = place()
    copies[0].wait()
    block, within = split_order(order[...])
    picks = [pick_sites(within[n : n + 1, :]) for n in range(8)]
    copies[1].wait()
    table = jnp.concatenate([samples[:, 128 * t : 128 * t + 128] for t in range(8)], axis=0)
    xs, e0s = [], []
    for pair in range(2):
        columns = []
        for b in range(4):
            n = 4 * pair + b
            found = dot(table, picks[n])
            columns.append(
                sum(
                    jnp.where(block[n : n + 1, :] == t, found[32 * t : 32 * t + 32], 0.0)
                    for t in range(8)
                )
            )
        both = jnp.transpose(jnp.concatenate(columns, axis=0)).astype(BF)
        x_out[128 * pair : 128 * pair + 128, :] = both
        xs += [both[:64], both[64:]]
    slot = slot_of(64)
    copies[2].wait()
    for a in range(4):
        e0 = merge_diagonal(dot(basis[a * 128 : (a + 1) * 128, :], xs[a]), 32).astype(BF)
        msg[OWN_E0 + a * 32 : OWN_E0 + (a + 1) * 32, :] = e0
        e0s.append(e0)
    msg[OWN_ROW : OWN_ROW + 64, :] = jnp.where(pi == 0, xs[3], xs[0])
    column_slot = jnp.where(pj == 0, 3, 0)
    packed = jnp.zeros((64, 128), BF)
    for a in range(4):
        packed = jnp.where(slot == lax.rem(column_slot + a, 4), roll(xs[a], 32 * a), packed)
    msg[OWN_COL : OWN_COL + 64, :] = packed

    one = eye(32)
    slot = slot_of(32)
    copies[3].wait()
    turned = [dot_nt(one, transfer[n * 32 : (n + 1) * 32, :]).astype(BF) for n in range(8)]
    e1 = jnp.zeros((32, 128), F32)
    for x in range(2):
        parts = []
        for j in range(2):
            parts.append(dot(turned[j], e0s[2 * x]) + dot(turned[2 + j], e0s[2 * x + 1]))
        joined = parts[0] + roll(parts[1], -32)
        e1 = jnp.where(slot == 2 * x, roll(joined, 64 * x), e1)
        e1 = jnp.where(slot == 2 * x + 1, roll(joined, 64 * x - 32), e1)
    e1 = e1.astype(BF)
    msg[OWN_E1 : OWN_E1 + 32, :] = e1
    e2 = merge_diagonal(dot(jnp.concatenate(turned[4:], axis=0), e1), 32)
    e2 = e2 + roll(e2, 64)
    e2 = e2 + roll(e2, 32)
    msg[OWN_E2 : OWN_E2 + 32, :] = jnp.where(slot == 2 * pi + pj, e2, 0.0).astype(BF)


def cross_kernel(group, x, send, *, count_x, count_y):
    gx, gy, pi, pj = place()
    swap = swap_of(gx, gy, count_x, count_y)
    me, across_x, across_y = 2 * pi + pj, 2 * (1 - pi) + pj, 2 * pi + 1 - pj
    lane, slot = lane_of(64), slot_of(64)
    near_half = (lane < 64) == (pj == 0)
    e0 = group[me, OWN_E0 : OWN_E0 + 128, :]
    e0_rows = jnp.where(pi == 0, e0[:64], e0[64:])
    x_row = jnp.where(pi == 0, x[0:64, :], x[192:256, :])
    e1 = group[me, OWN_E1 : OWN_E1 + 32, :]
    e2 = group[0, OWN_E2 : OWN_ROWS, :]
    for m in range(1, 4):
        e2 = e2 + group[m, OWN_E2 : OWN_ROWS, :]
    for m in range(4):
        send[m, FAR_E2 : FAR_E2 + 32, :] = e2
        send[m, FAR_E1 : FAR_E1 + 32, :] = e1

    to = (2 * pi + 1 - pj) ^ swap
    send[to, FAR_X : FAR_X + 64, :] = x_row
    send[to, FAR_E0 : FAR_E0 + 64, :] = e0_rows
    column = group[across_y, OWN_COL : OWN_COL + 64, :]
    column = jnp.where(pi == 0, roll(column, 64), roll(column, -32))
    corner_e0 = group[across_y, pl.ds(OWN_E0 + 64 * pi, 64), :]
    send[to, FAR_CORNER : FAR_CORNER + 64, :] = jnp.where(near_half, corner_e0, column)
    send[to, FAR_E1_SIDE : FAR_E1_SIDE + 32, :] = group[across_y, OWN_E1 : OWN_E1 + 32, :]

    to = (2 * (1 - pi) + pj) ^ swap
    column_slot = jnp.where(pj == 0, 0, 3)
    packed = jnp.zeros((64, 128), BF)
    for a in range(4):
        moved = roll(x[a * 64 : (a + 1) * 64, :], 32 * a)
        packed = jnp.where(slot == lax.rem(column_slot + a, 4), moved, packed)
    send[to, FAR_X : FAR_X + 64, :] = packed
    send[to, FAR_E0 : FAR_E0 + 64, :] = jnp.where(near_half, e0[:64], roll(e0[64:], 64))
    corner_x = roll(group[across_x, OWN_ROW : OWN_ROW + 64, :], 64)
    corner_e0 = group[across_x, pl.ds(OWN_E0 + 64 * pi, 64), :]
    send[to, FAR_CORNER : FAR_CORNER + 64, :] = jnp.where(near_half, corner_e0, corner_x)
    send[to, FAR_E1_SIDE : FAR_E1_SIDE + 32, :] = group[across_x, OWN_E1 : OWN_E1 + 32, :]

    to = (2 * pi + pj) ^ swap
    send[to, FAR_X : FAR_X + 64, :] = jnp.zeros((64, 128), BF)
    send[to, FAR_E0 : FAR_E0 + 64, :] = jnp.zeros((64, 128), BF)
    send[to, FAR_CORNER : FAR_CORNER + 64, :] = jnp.where(near_half, e0_rows, roll(x_row, 64))
    send[to, FAR_E1_SIDE : FAR_E1_SIDE + 32, :] = jnp.zeros((32, 128), BF)

    to = (2 * (1 - pi) + 1 - pj) ^ swap
    send[to, 0:FAR_E1, :] = jnp.zeros((FAR_E1, 128), BF)
    send[to, FAR_E1_SIDE : FAR_E1_SIDE + 32, :] = jnp.zeros((32, 128), BF)


def store_row_of_tiles(halo, start, left, middle, right):
    lane = lane_of(32)
    low = lane < 64
    nothing = jnp.zeros((32, 128), BF)
    first = jnp.where(low, middle, roll(right, 64))
    second = jnp.where(low, roll(middle, 64), right)
    halo[pl.ds(start, 32), 0:128] = first
    halo[pl.ds(start, 32), 128:256] = jnp.where(low, nothing, roll(left, 64))
    halo[pl.ds(start + 32, 32), 0:128] = second
    halo[pl.ds(start + 32, 32), 128:256] = jnp.where(low, nothing, left)


def far_row(matrix, window, parity):
    lane = lane_of(224, 224)
    admitted = (lane >= 32 * (1 - parity)) & (lane < 224 - 32 * parity)
    product = dot(jnp.where(admitted, matrix, jnp.zeros((224, 224), BF)), window)
    odd = lax.rem(slot_of(32), 2) == 1
    out = jnp.zeros((32, 128), F32)
    for w in range(-3, 4):
        part = product[(w + 3) * 32 : (w + 4) * 32]
        part = part[:, :128] if w == 0 else pltpu.roll(part, (-32 * w) % 256, 1)[:, :128]
        if w == -3:
            part = jnp.where(odd, part, 0.0)
        if w == 3:
            part = jnp.where(odd, 0.0, part)
        out = out + part
    return out


def turn_coupling(coupling, turned, far):
    row = lax.broadcasted_iota(jnp.int32, (56, 40), 0)
    number = lane_of(56, 40)
    u, w = row // 8 - 3, row % 8 - 3
    outer = (abs(u) >= 2) & (w <= 3)
    inner = (abs(u) < 2) & (abs(w) >= 2) & (w <= 3)
    index = jnp.where(u < -1, (u + 3) * 7 + w + 3, 26 + (u - 2) * 7 + w + 3)
    index = jnp.where(abs(u) < 2, 14 + (u + 1) * 4 + jnp.where(w < 0, w + 3, w), index)
    choose = jnp.where((outer | inner) & (number == index), 1.0, 0.0).astype(BF)
    slot = slot_of(8)
    for level in range(3):
        for block in range(8):
            lines = coupling[level, 4 * block : 4 * block + 4].reshape(128, 40)
            part = dot_nt(choose, lines)
            moved = [part] + [pltpu.roll(part, 32 * q, 1) for q in range(1, 4)]
            for q in range(4):
                i = 4 * block + q
                for half in range(2):
                    out = jnp.zeros((8, 128), F32)
                    for u in range(4 * half, min(4 * half + 4, 7)):
                        piece = moved[(u - q) % 4][8 * u : 8 * u + 8]
                        out = jnp.where(slot == u % 4, piece, out)
                    turned[half][pl.ds(i, 8, stride=32), :] = out
        for half in range(2):
            lines = turned[half][0:224, :].astype(BF)
            far[level, :, 128 * half : 128 * half + 128] = lines


def inner_kernel(
    group, x, near_hbm, coupling_hbm, basis_hbm,
    near_out, far, leaf_hbm,
    near, coupling, basis, turned_low, turned_high, leaf, sems,
):
    copies = fetch(
        [basis_hbm, coupling_hbm] + [near_hbm.at[a] for a in range(4)],
        [basis, coupling] + [near.at[a] for a in range(4)],
        sems,
    )
    _, _, pi, pj = place()
    across_x, across_y, across = 2 * (1 - pi) + pj, 2 * pi + 1 - pj, 2 * (1 - pi) + 1 - pj
    copies[0].wait()
    for a in range(4):
        flat = jnp.transpose(basis[a * 128 : (a + 1) * 128, :].astype(F32))
        leaf[a * 64 : (a + 1) * 64, :] = flat.astype(BF)
    leaf_copy = pltpu.make_async_copy(leaf, leaf_hbm, sems.at[6])
    leaf_copy.start()
    copies[1].wait()
    turn_coupling(coupling, (turned_low, turned_high), far)

    slot = slot_of(64)
    windows = {}

    def store_windows(a, middle, inner):
        left = jnp.where(pj == 0, jnp.zeros_like(inner), inner)
        right = jnp.where(pj == 0, inner, jnp.zeros_like(inner))
        windows[a, 0] = middle
        windows[a, -1] = roll(jnp.where(slot == 3, left, middle), 32)
        windows[a, 1] = roll(jnp.where(slot == 0, right, middle), -32)

    beside = group[across_y, OWN_COL : OWN_COL + 64, :]
    for a in range(4):
        store_windows(a, x[a * 64 : (a + 1) * 64, :], roll(beside, -32 * a))
    middle = group[across_x, OWN_ROW : OWN_ROW + 64, :]
    inner = group[across, OWN_ROW : OWN_ROW + 64, :]
    nothing = jnp.zeros((64, 128), BF)
    store_windows(-1, jnp.where(pi == 0, nothing, middle), jnp.where(pi == 0, nothing, inner))
    store_windows(4, jnp.where(pi == 0, middle, nothing), jnp.where(pi == 0, inner, nothing))
    for a in range(4):
        copies[2 + a].wait()
        total = jnp.zeros((256, 128), F32)
        for n in range(9):
            matrix = near[a, :, n].reshape(256, 64)
            total = total + dot(matrix, windows[a + n // 3 - 1, n % 3 - 1])
        near_out[a * 64 : (a + 1) * 64, :] = merge_diagonal(total, 64)
    leaf_copy.wait()


def downward_kernel(count_x, count_y):
    def body(
        group, near_part, far, cross, shared, transfer_hbm, near_hbm, leaf_hbm, order_hbm, out_hbm,
        h0, h1, h2, transfer, near_row, near_col, leaf, order, out, sems,
    ):
        gx, gy, pi, pj = place()
        copies = fetch(
            (
                transfer_hbm,
                near_hbm.at[3 * pi, :, pl.ds(6 * pi, 3)],
                near_hbm.at[:, 3 * pj],
                leaf_hbm,
                order_hbm,
            ),
            (transfer, near_row, near_col, leaf, order),
            sems,
        )
        swap = swap_of(gx, gy, count_x, count_y)
        me, across_x, across_y = 2 * pi + pj, 2 * (1 - pi) + pj, 2 * pi + 1 - pj
        across = 2 * (1 - pi) + 1 - pj
        from_x, from_y = (2 * pi + 1 - pj) ^ swap, (2 * (1 - pi) + pj) ^ swap
        from_xy = (2 * pi + pj) ^ swap
        has_x = jnp.where(pi == 0, gx > 0, gx < count_x - 1)
        has_y = jnp.where(pj == 0, gy > 0, gy < count_y - 1)
        has_xy = has_x & has_y

        def kept(keep, value):
            return jnp.where(keep, value, jnp.zeros_like(value))

        lane = lane_of(64)
        near_half = (lane < 64) == (pj == 0)
        h0[0:32, :] = jnp.zeros((32, 256), BF)
        h0[288:320, :] = jnp.zeros((32, 256), BF)
        h0[96:224, 0:128] = group[me, OWN_E0 : OWN_E0 + 128, :]
        strip = kept(has_y, cross[from_y, FAR_E0 : FAR_E0 + 64, :])
        beside = group[across_y, OWN_E0 : OWN_E0 + 128, :]
        h0[96:160, 128:256] = jnp.where(near_half, beside[:64], strip)
        h0[160:224, 128:256] = jnp.where(near_half, beside[64:], roll(strip, 64))
        start = 32 + 192 * (1 - pi)
        h0[pl.ds(start, 64), 0:128] = group[across_x, pl.ds(OWN_E0 + 64 * pi, 64), :]
        h0[pl.ds(start, 64), 128:256] = jnp.where(
            near_half,
            group[across, pl.ds(OWN_E0 + 64 * pi, 64), :],
            kept(has_y, cross[from_y, FAR_CORNER : FAR_CORNER + 64, :]),
        )
        start = 32 + 192 * pi
        h0[pl.ds(start, 64), 0:128] = kept(has_x, cross[from_x, FAR_E0 : FAR_E0 + 64, :])
        h0[pl.ds(start, 64), 128:256] = jnp.where(
            near_half,
            kept(has_x, cross[from_x, FAR_CORNER : FAR_CORNER + 64, :]),
            kept(has_xy, cross[from_xy, FAR_CORNER : FAR_CORNER + 64, :]),
        )

        def store_sides(start, middle, inner, outer):
            left = jnp.where(pj == 0, outer, inner)
            right = jnp.where(pj == 0, inner, outer)
            store_row_of_tiles(h1, start, left, middle, right)

        for halo in (h1, h2):
            halo[0:32, :] = jnp.zeros((32, 256), BF)
            halo[224:256, :] = jnp.zeros((32, 256), BF)
        own_e1 = slice(OWN_E1, OWN_E1 + 32)
        far_e1, side_e1 = slice(FAR_E1, FAR_E1 + 32), slice(FAR_E1_SIDE, FAR_E1_SIDE + 32)
        store_sides(
            96, group[me, own_e1, :], group[across_y, own_e1, :], kept(has_y, cross[from_y, far_e1, :])
        )
        store_sides(
            32 + 128 * (1 - pi),
            group[across_x, own_e1, :],
            group[across, own_e1, :],
            kept(has_y, cross[from_y, side_e1, :]),
        )
        store_sides(
            32 + 128 * pi,
            kept(has_x, cross[from_x, far_e1, :]),
            kept(has_x, cross[from_x, side_e1, :]),
            kept(has_xy, cross[from_xy, far_e1, :]),
        )

        above, below = gx >= 2, gx < count_x - 2
        before, after = gy >= 2, gy < count_y - 2
        e2 = group[0, OWN_E2:OWN_ROWS, :]
        for m in range(1, 4):
            e2 = e2 + group[m, OWN_E2:OWN_ROWS, :]

        def brought(m, slot, keep):
            other = swap_of(gx - pi + m // 2, gy - pj + m % 2, count_x, count_y)
            return kept(keep, shared[m, slot ^ other])

        store_row_of_tiles(
            h2, 32, brought(0, 0, above & before), brought(0, 1, above), brought(1, 1, above & after)
        )
        store_row_of_tiles(h2, 96, brought(0, 2, before), e2, brought(1, 3, after))
        store_row_of_tiles(
            h2, 160, brought(2, 2, below & before), brought(2, 3, below), brought(3, 3, below & after)
        )

        slot = slot_of(32)
        local2 = far_row(far[2, :, :224], h2[pl.ds(32 * pi, 224), :], pi)
        local2 = jnp.where(slot == pj, local2, 0.0)
        local2 = local2 + roll(local2, 64)
        local2 = (local2 + roll(local2, 32)).astype(BF)
        copies[0].wait()
        spread = dot(transfer[128:256, :], local2)
        local1 = []
        for i in range(2):
            down = far_row(far[1, :, :224], h1[32 * i : 32 * i + 224, :], i)
            for j in range(2):
                n = 2 * i + j
                down = down + jnp.where(slot == j, spread[n * 32 : (n + 1) * 32], 0.0)
            down = jnp.where(slot < 2, down, 0.0)
            wide = jnp.where(slot == 0, down, 0.0) + jnp.where(slot == 2, roll(down, 32), 0.0)
            local1.append((wide + roll(wide, 32)).astype(BF))
        local0 = []
        for i in range(4):
            spread = dot(transfer[64 * (i % 2) : 64 * (i % 2) + 64, :], local1[i // 2])
            down = far_row(far[0, :, :224], h0[32 * i : 32 * i + 224, :], i % 2)
            down = down + jnp.where(lax.rem(slot, 2) == 0, spread[:32], spread[32:])
            local0.append(down.astype(BF))


        slot = slot_of(64)
        copies[1].wait()
        copies[2].wait()
        column = kept(has_y, cross[from_y, FAR_X : FAR_X + 64, :])
        corner_in = kept(has_y, roll(cross[from_y, FAR_CORNER : FAR_CORNER + 64, :], 64))
        corner_out = kept(has_xy, roll(cross[from_xy, FAR_CORNER : FAR_CORNER + 64, :], 64))
        boxes = {a: roll(column, -32 * a) for a in range(4)}
        boxes[-1] = jnp.where(pi == 0, corner_out, corner_in)
        boxes[4] = jnp.where(pi == 0, corner_in, corner_out)
        edge = slot == 3 * pj
        for a in boxes:
            moved = jnp.where(pj == 0, roll(boxes[a], 32), roll(boxes[a], -32))
            boxes[a] = jnp.where(edge, moved, jnp.zeros_like(moved))
        middle = kept(has_x, cross[from_x, FAR_X : FAR_X + 64, :])
        inner = kept(has_x, roll(cross[from_x, FAR_CORNER : FAR_CORNER + 64, :], 64))
        nothing = jnp.zeros_like(inner)
        left = jnp.where(pj == 0, nothing, inner)
        right = jnp.where(pj == 0, inner, nothing)
        shifts = (
            roll(jnp.where(slot == 3, left, middle), 32),
            middle,
            roll(jnp.where(slot == 0, right, middle), -32),
        )
        beyond = jnp.zeros((256, 128), F32)
        for c in range(3):
            beyond = beyond + dot(near_row[:, c].reshape(256, 64), shifts[c])
        beyond = merge_diagonal(beyond, 64)

        block = lax.broadcasted_iota(jnp.int32, (128, 128), 0) // 32 == slot_of(128)
        copies[4].wait()
        part, within = split_order(order[...])
        pick = jnp.concatenate([pick_sites(within[n : n + 1, :]) for n in range(8)], axis=1)
        leaves = []
        copies[3].wait()
        for a in range(4):
            total = near_part[a * 64 : (a + 1) * 64, :]
            if a == 0:
                total = total + jnp.where(pi == 0, beyond, 0.0)
            if a == 3:
                total = total + jnp.where(pi == 0, 0.0, beyond)
            for r in range(3):
                total = total + dot(near_col[a, 3 * r + 2 * pj], boxes[a + r - 1])
            local = jnp.concatenate([local0[a]] * 4, axis=0)
            total = total + dot(leaf[a * 64 : (a + 1) * 64, :], jnp.where(block, local, jnp.zeros_like(local)))
            leaves.append(total)
        spread = []
        for pair in range(2):
            turned = jnp.transpose(jnp.concatenate(leaves[2 * pair : 2 * pair + 2], axis=0))
            for b in range(4):
                n = 4 * pair + b
                line = turned[32 * b : 32 * b + 32]
                parts = [jnp.where(part[n : n + 1, :] == t, line, 0.0) for t in range(8)]
                spread.append(jnp.concatenate(parts, axis=0).astype(BF))
        done = dot_nt(jnp.concatenate(spread, axis=1), pick).astype(BF)
        for t in range(8):
            out[:, 128 * t : 128 * (t + 1)] = done[32 * t : 32 * t + 32]
        last = pltpu.make_async_copy(out, out_hbm, sems.at[5])
        last.start()
        last.wait()

    return body


def call(kernel, spaces, shapes, scratch=(), flops=10**6):
    def run(*args):
        return pl.pallas_call(
            kernel,
            out_shape=shapes,
            in_specs=[pl.BlockSpec(memory_space=space) for space in spaces],
            out_specs=jax.tree.map(lambda shape: pl.BlockSpec(memory_space=shape.memory_space), shapes),
            scratch_shapes=list(scratch),
            cost_estimate=pl.CostEstimate(flops=flops, bytes_accessed=2**20, transcendentals=0),
            compiler_params=pltpu.CompilerParams(vmem_limit_bytes=VMEM_BYTES),
        )(*map(pltpu.with_memory_space_constraint, args, spaces))

    return run


def aligned_groups(count_x, count_y):
    return [
        [(i + di) * count_y + j + dj for di in range(2) for dj in range(2)]
        for i in range(0, count_x, 2)
        for j in range(0, count_y, 2)
    ]


def shifted_groups(count_x, count_y):
    last_x, last_y = count_x - 1, count_y - 1
    groups = [
        [(i, j), (i, j + 1), (i + 1, j), (i + 1, j + 1)]
        for i in range(1, last_x, 2)
        for j in range(1, last_y, 2)
    ]
    for i in (0, last_x):
        for j in range(-1, last_y, 4):
            first = [(i, j), (i, j + 1)] if j > 0 else [(i, last_y), (i, 0)]
            second = [(i, j + 2), (i, j + 3)]
            if j < 0:
                first, second = second, first
            groups.append(second + first if i == 0 else first + second)
    for i in range(1, last_x, 4):
        if i + 3 < last_x:
            for j in (0, last_y):
                lanes = (i + 2, i) if j == 0 else (i, i + 2)
                groups.append([(g + d, j) for d in range(2) for g in lanes])
        else:
            groups.append([(i + d, j) for d in range(2) for j in (last_y, 0)])
    return [[i * count_y + j for i, j in group] for group in groups]


def run_upward(samples, order, basis, transfer):
    return call(
        upward_kernel,
        (HBM,) * 4,
        (VMEM((256, 128), BF), VMEM((OWN_ROWS, 128), BF)),
        (
            VMEM((8, 128), jnp.int32),
            VMEM((32, 1024), BF),
            VMEM((512, 64), BF),
            VMEM((256, 32), BF),
            pltpu.SemaphoreType.DMA((4,)),
        ),
    )(samples, order, basis, transfer)


def run_cross(group, x, count_x, count_y):
    body = functools.partial(cross_kernel, count_x=count_x, count_y=count_y)
    return call(body, (VMEM,) * 2, VMEM((4, FAR_ROWS, 128), BF))(group, x)


def run_inner(group, x, near_blocks, coupling, basis):
    return call(
        inner_kernel,
        (VMEM,) * 2 + (HBM,) * 3,
        (VMEM((256, 128), F32), VMEM((3, 224, 256), BF), HBM((256, 128), BF)),
        (
            VMEM((4, 4, 9, 64, 64), BF),
            VMEM((3, 32, 32, 40), BF),
            VMEM((512, 64), BF),
            VMEM((256, 128), F32),
            VMEM((256, 128), F32),
            VMEM((256, 128), BF),
            pltpu.SemaphoreType.DMA((7,)),
        ),
        flops=10**9,
    )(group, x, near_blocks, coupling, basis)


def run_downward(group, inner, cross, shared, transfer, near_blocks, order, count_x, count_y):
    near_part, far, leaf = inner
    return call(
        downward_kernel(count_x, count_y),
        (VMEM,) * 5 + (HBM,) * 4,
        HBM((32, 1024), BF),
        (
            VMEM((320, 256), BF),
            VMEM((256, 256), BF),
            VMEM((256, 256), BF),
            VMEM((256, 32), BF),
            VMEM((4, 3, 64, 64), BF),
            VMEM((4, 9, 64, 64), BF),
            VMEM((256, 128), BF),
            VMEM((8, 128), jnp.int32),
            VMEM((32, 1024), BF),
            pltpu.SemaphoreType.DMA((6,)),
        ),
    )(group, near_part, far, cross, shared, transfer, near_blocks, leaf, order)


def solution(mesh):
    count_x, count_y = mesh.shape["gx"], mesh.shape["gy"]
    aligned = aligned_groups(count_x, count_y)
    shifted = shifted_groups(count_x, count_y)

    def local(samples, site_order, leaf_basis, near_blocks, transfer, coupling):
        samples = samples.T
        order = site_order.reshape(8, 128)
        basis = leaf_basis.transpose(0, 1, 3, 2).reshape(512, 64)
        transfer = transfer.reshape(256, 32)
        coupling = coupling.transpose(0, 2, 3, 1)
        x, message = run_upward(samples, order, basis, transfer)
        group = lax.all_gather(message, AXES, axis_index_groups=aligned)
        send = run_cross(group, x, count_x, count_y)
        cross = lax.all_to_all(send, AXES, 0, 0, axis_index_groups=shifted)
        inner = run_inner(group, x, near_blocks, coupling, basis)
        shared = lax.all_gather(cross[:, FAR_E2 : FAR_E2 + 32], AXES, axis_index_groups=aligned)
        out = run_downward(
            group, inner, cross, shared, transfer, near_blocks, order, count_x, count_y
        )
        return out.T

    return jax.shard_map(
        local,
        mesh=mesh,
        in_specs=(
            P(("gx", "gy"), None),
            P(("gx", "gy")),
            P("gx", "gy", None, None),
            P("gx", "gy", None, None, None),
            P(),
            P(),
        ),
        out_specs=P(("gx", "gy"), None),
        check_vma=False,
    )
```

```python
import functools

import jax
import jax.numpy as jnp
from jax import lax
from jax.experimental import pallas as pl
from jax.experimental.pallas import tpu as pltpu
from jax.sharding import PartitionSpec as P

BF = jnp.bfloat16
F32 = jnp.float32
AXES = ("gx", "gy")
LEAF, TABLE_ROWS = 672, 928
VMEM_BYTES = 32 * 1024 * 1024
VMEM, HBM = pltpu.VMEM, pltpu.HBM

OWN_ROW, OWN_COL, OWN_E0, OWN_E1, OWN_E2, OWN_ROWS = 0, 64, 128, 256, 288, 320
FAR_X, FAR_E0, FAR_CORNER, FAR_E1, FAR_E1_SIDE, FAR_E2, FAR_ROWS = 0, 64, 128, 192, 224, 256, 288


def dot(a, b):
    return lax.dot_general(a, b, (((1,), (0,)), ((), ())), preferred_element_type=F32)


def dot_nt(a, b):
    return lax.dot_general(a, b, (((1,), (1,)), ((), ())), preferred_element_type=F32)


def roll(x, lanes):
    lanes = lanes % x.shape[1]
    if lanes == 0:
        return x
    if x.dtype == BF:
        return pltpu.roll(x.astype(F32), lanes, 1).astype(BF)
    return pltpu.roll(x, lanes, 1)


def lane_of(rows, lanes=128):
    return lax.broadcasted_iota(jnp.int32, (rows, lanes), 1)


def slot_of(rows, lanes=128):
    return lane_of(rows, lanes) // 32


def eye(n):
    row = lax.broadcasted_iota(jnp.int32, (n, n), 0)
    return jnp.where(row == lane_of(n, n), 1.0, 0.0).astype(BF)


def place():
    gx, gy = lax.axis_index("gx"), lax.axis_index("gy")
    return gx, gy, lax.rem(gx, 2), lax.rem(gy, 2)


def swap_of(gx, gy, count_x, count_y):
    end_x = (gx == 0) | (gx == count_x - 1)
    end_y = (gy == 0) | (gy == count_y - 1)
    along_y = jnp.where((lax.rem(gy + 3, 4) < 2) == (gx == 0), 2, 0)
    along_x = jnp.where(lax.rem(gx + 3, 4) >= 2, 1, 0)
    return jnp.where(end_x & ~end_y, along_y, jnp.where(end_y & ~end_x, along_x, 0))


def merge_diagonal(blocks, height):
    slot = slot_of(height)
    out = jnp.zeros((height, 128), F32)
    for b in range(4):
        out = jnp.where(slot == b, blocks[b * height : (b + 1) * height], out)
    return out


def split_order(order):
    lane = lane_of(1)
    lines = []
    for pair in range(2):
        for b in range(4):
            low = order[4 * pair + b // 2 : 4 * pair + b // 2 + 1, :]
            high = order[4 * pair + 2 + b // 2 : 4 * pair + 3 + b // 2, :]
            if b % 2 == 0:
                lines.append(jnp.where(lane < 64, low, pltpu.roll(high, 64, 1)))
            else:
                lines.append(jnp.where(lane < 64, pltpu.roll(low, 64, 1), high))
    lines = jnp.concatenate(lines, axis=0)
    return lines // 128, lines % 128


def pick_sites(within):
    row = lax.broadcasted_iota(jnp.int32, (128, 128), 0)
    return jnp.where(within == row, 1.0, 0.0).astype(BF)


def fetch(sources, targets, sems):
    copies = [
        pltpu.make_async_copy(source, target, sems.at[n])
        for n, (source, target) in enumerate(zip(sources, targets))
    ]
    for copy in copies:
        copy.start()
    return copies


def upward_kernel(
    samples_hbm, order_hbm, basis_hbm, transfer_hbm, near_hbm,
    x_out, msg, near, order, samples, basis, transfer, sems,
):
    copies = fetch(
        (order_hbm, samples_hbm, basis_hbm, transfer_hbm, near_hbm.at[0:2]),
        (order, samples, basis, transfer, near),
        sems,
    )
    _, _, pi, pj = place()
    copies[0].wait()
    block, within = split_order(order[...])
    picks = [pick_sites(within[n : n + 1, :]) for n in range(8)]
    copies[1].wait()
    table = jnp.concatenate([samples[:, 128 * t : 128 * t + 128] for t in range(8)], axis=0)
    xs, e0s = [], []
    for pair in range(2):
        columns = []
        for b in range(4):
            n = 4 * pair + b
            found = dot(table, picks[n])
            columns.append(
                sum(
                    jnp.where(block[n : n + 1, :] == t, found[32 * t : 32 * t + 32], 0.0)
                    for t in range(8)
                )
            )
        both = jnp.transpose(jnp.concatenate(columns, axis=0)).astype(BF)
        x_out[128 * pair : 128 * pair + 128, :] = both
        xs += [both[:64], both[64:]]
    slot = slot_of(64)
    copies[2].wait()
    for a in range(4):
        e0 = merge_diagonal(dot(basis[a * 128 : (a + 1) * 128, :], xs[a]), 32).astype(BF)
        msg[OWN_E0 + a * 32 : OWN_E0 + (a + 1) * 32, :] = e0
        e0s.append(e0)
    msg[OWN_ROW : OWN_ROW + 64, :] = jnp.where(pi == 0, xs[3], xs[0])
    column_slot = jnp.where(pj == 0, 3, 0)
    packed = jnp.zeros((64, 128), BF)
    for a in range(4):
        packed = jnp.where(slot == lax.rem(column_slot + a, 4), roll(xs[a], 32 * a), packed)
    msg[OWN_COL : OWN_COL + 64, :] = packed

    one = eye(32)
    slot = slot_of(32)
    copies[3].wait()
    turned = [dot_nt(one, transfer[n * 32 : (n + 1) * 32, :]).astype(BF) for n in range(8)]
    e1 = jnp.zeros((32, 128), F32)
    for x in range(2):
        parts = []
        for j in range(2):
            parts.append(dot(turned[j], e0s[2 * x]) + dot(turned[2 + j], e0s[2 * x + 1]))
        joined = parts[0] + roll(parts[1], -32)
        e1 = jnp.where(slot == 2 * x, roll(joined, 64 * x), e1)
        e1 = jnp.where(slot == 2 * x + 1, roll(joined, 64 * x - 32), e1)
    e1 = e1.astype(BF)
    msg[OWN_E1 : OWN_E1 + 32, :] = e1
    e2 = merge_diagonal(dot(jnp.concatenate(turned[4:], axis=0), e1), 32)
    e2 = e2 + roll(e2, 64)
    e2 = e2 + roll(e2, 32)
    msg[OWN_E2 : OWN_E2 + 32, :] = jnp.where(slot == 2 * pi + pj, e2, 0.0).astype(BF)
    copies[4].wait()


def cross_kernel(group, x, send, *, count_x, count_y):
    gx, gy, pi, pj = place()
    swap = swap_of(gx, gy, count_x, count_y)
    me, across_x, across_y = 2 * pi + pj, 2 * (1 - pi) + pj, 2 * pi + 1 - pj
    lane, slot = lane_of(64), slot_of(64)
    near_half = (lane < 64) == (pj == 0)
    e0 = group[me, OWN_E0 : OWN_E0 + 128, :]
    e0_rows = jnp.where(pi == 0, e0[:64], e0[64:])
    x_row = jnp.where(pi == 0, x[0:64, :], x[192:256, :])
    e1 = group[me, OWN_E1 : OWN_E1 + 32, :]
    e2 = group[0, OWN_E2 : OWN_ROWS, :]
    for m in range(1, 4):
        e2 = e2 + group[m, OWN_E2 : OWN_ROWS, :]
    for m in range(4):
        send[m, FAR_E2 : FAR_E2 + 32, :] = e2
        send[m, FAR_E1 : FAR_E1 + 32, :] = e1

    to = (2 * pi + 1 - pj) ^ swap
    send[to, FAR_X : FAR_X + 64, :] = x_row
    send[to, FAR_E0 : FAR_E0 + 64, :] = e0_rows
    column = group[across_y, OWN_COL : OWN_COL + 64, :]
    column = jnp.where(pi == 0, roll(column, 64), roll(column, -32))
    corner_e0 = group[across_y, pl.ds(OWN_E0 + 64 * pi, 64), :]
    send[to, FAR_CORNER : FAR_CORNER + 64, :] = jnp.where(near_half, corner_e0, column)
    send[to, FAR_E1_SIDE : FAR_E1_SIDE + 32, :] = group[across_y, OWN_E1 : OWN_E1 + 32, :]

    to = (2 * (1 - pi) + pj) ^ swap
    column_slot = jnp.where(pj == 0, 0, 3)
    packed = jnp.zeros((64, 128), BF)
    for a in range(4):
        moved = roll(x[a * 64 : (a + 1) * 64, :], 32 * a)
        packed = jnp.where(slot == lax.rem(column_slot + a, 4), moved, packed)
    send[to, FAR_X : FAR_X + 64, :] = packed
    send[to, FAR_E0 : FAR_E0 + 64, :] = jnp.where(near_half, e0[:64], roll(e0[64:], 64))
    corner_x = roll(group[across_x, OWN_ROW : OWN_ROW + 64, :], 64)
    corner_e0 = group[across_x, pl.ds(OWN_E0 + 64 * pi, 64), :]
    send[to, FAR_CORNER : FAR_CORNER + 64, :] = jnp.where(near_half, corner_e0, corner_x)
    send[to, FAR_E1_SIDE : FAR_E1_SIDE + 32, :] = group[across_x, OWN_E1 : OWN_E1 + 32, :]

    to = (2 * pi + pj) ^ swap
    send[to, FAR_X : FAR_X + 64, :] = jnp.zeros((64, 128), BF)
    send[to, FAR_E0 : FAR_E0 + 64, :] = jnp.zeros((64, 128), BF)
    send[to, FAR_CORNER : FAR_CORNER + 64, :] = jnp.where(near_half, e0_rows, roll(x_row, 64))
    send[to, FAR_E1_SIDE : FAR_E1_SIDE + 32, :] = jnp.zeros((32, 128), BF)

    to = (2 * (1 - pi) + 1 - pj) ^ swap
    send[to, 0:FAR_E1, :] = jnp.zeros((FAR_E1, 128), BF)
    send[to, FAR_E1_SIDE : FAR_E1_SIDE + 32, :] = jnp.zeros((32, 128), BF)


def store_row_of_tiles(halo, start, left, middle, right):
    lane = lane_of(32)
    low = lane < 64
    nothing = jnp.zeros((32, 128), BF)
    first = jnp.where(low, middle, roll(right, 64))
    second = jnp.where(low, roll(middle, 64), right)
    halo[pl.ds(start, 32), 0:128] = first
    halo[pl.ds(start, 32), 128:256] = jnp.where(low, nothing, roll(left, 64))
    halo[pl.ds(start + 32, 32), 0:128] = second
    halo[pl.ds(start + 32, 32), 128:256] = jnp.where(low, nothing, left)


def far_row(matrix, window, parity):
    lane = lane_of(224, 224)
    admitted = (lane >= 32 * (1 - parity)) & (lane < 224 - 32 * parity)
    product = dot(jnp.where(admitted, matrix, jnp.zeros((224, 224), BF)), window)
    odd = lax.rem(slot_of(32), 2) == 1
    out = jnp.zeros((32, 128), F32)
    for w in range(-3, 4):
        part = product[(w + 3) * 32 : (w + 4) * 32]
        part = part[:, :128] if w == 0 else pltpu.roll(part, (-32 * w) % 256, 1)[:, :128]
        if w == -3:
            part = jnp.where(odd, part, 0.0)
        if w == 3:
            part = jnp.where(odd, 0.0, part)
        out = out + part
    return out


def turn_coupling(coupling, turned, tables):
    row = lax.broadcasted_iota(jnp.int32, (56, 40), 0)
    number = lane_of(56, 40)
    u, w = row // 8 - 3, row % 8 - 3
    outer = (abs(u) >= 2) & (w <= 3)
    inner = (abs(u) < 2) & (abs(w) >= 2) & (w <= 3)
    index = jnp.where(u < -1, (u + 3) * 7 + w + 3, 26 + (u - 2) * 7 + w + 3)
    index = jnp.where(abs(u) < 2, 14 + (u + 1) * 4 + jnp.where(w < 0, w + 3, w), index)
    choose = jnp.where((outer | inner) & (number == index), 1.0, 0.0).astype(BF)
    slot = slot_of(8)
    for level in range(3):
        for block in range(8):
            lines = coupling[level, 4 * block : 4 * block + 4].reshape(128, 40)
            part = dot_nt(choose, lines)
            moved = [part] + [pltpu.roll(part, 32 * q, 1) for q in range(1, 4)]
            for q in range(4):
                i = 4 * block + q
                for half in range(2):
                    out = jnp.zeros((8, 128), F32)
                    for u in range(4 * half, min(4 * half + 4, 7)):
                        piece = moved[(u - q) % 4][8 * u : 8 * u + 8]
                        out = jnp.where(slot == u % 4, piece, out)
                    turned[half][pl.ds(i, 8, stride=32), :] = out
        for half in range(2):
            lines = turned[half][0:224, :].astype(BF)
            tables[224 * level : 224 * level + 224, 128 * half : 128 * half + 128] = lines


def inner_kernel(
    group, x, near_low, near_hbm, coupling_hbm, basis_hbm, transfer_hbm, order_hbm,
    near_out, tables, edges,
    near_high, coupling, basis, transfer, order, turned_low, turned_high, sems,
):
    copies = fetch(
        (coupling_hbm, near_hbm.at[2:4], basis_hbm, transfer_hbm, order_hbm),
        (coupling, near_high, basis, transfer, order),
        sems,
    )
    _, _, pi, pj = place()
    across_x, across_y, across = 2 * (1 - pi) + pj, 2 * pi + 1 - pj, 2 * (1 - pi) + 1 - pj
    slot = slot_of(64)
    windows = {}

    def store_windows(a, middle, inner):
        left = jnp.where(pj == 0, jnp.zeros_like(inner), inner)
        right = jnp.where(pj == 0, inner, jnp.zeros_like(inner))
        windows[a, 0] = middle
        windows[a, -1] = roll(jnp.where(slot == 3, left, middle), 32)
        windows[a, 1] = roll(jnp.where(slot == 0, right, middle), -32)

    beside = group[across_y, OWN_COL : OWN_COL + 64, :]
    for a in range(4):
        store_windows(a, x[a * 64 : (a + 1) * 64, :], roll(beside, -32 * a))
    middle = group[across_x, OWN_ROW : OWN_ROW + 64, :]
    inner = group[across, OWN_ROW : OWN_ROW + 64, :]
    nothing = jnp.zeros((64, 128), BF)
    store_windows(-1, jnp.where(pi == 0, nothing, middle), jnp.where(pi == 0, nothing, inner))
    store_windows(4, jnp.where(pi == 0, middle, nothing), jnp.where(pi == 0, inner, nothing))
    def add_near(a):
        near = near_low if a < 2 else near_high
        total = jnp.zeros((256, 128), F32)
        for n in range(9):
            matrix = near[a % 2, :, n].reshape(256, 64)
            total = total + dot(matrix, windows[a + n // 3 - 1, n % 3 - 1])
        near_out[a * 64 : (a + 1) * 64, :] = merge_diagonal(total, 64)
        for r in range(3):
            row = 768 + 64 * (3 * a + r)
            edges[row : row + 64, :] = near[a % 2, 3 * pj, 3 * r + 2 * pj]

    add_near(0)
    add_near(1)
    copies[0].wait()
    turn_coupling(coupling, (turned_low, turned_high), tables)
    copies[1].wait()
    add_near(2)
    add_near(3)
    for c in range(3):
        above, below = near_low[0, :, c], near_high[1, :, 6 + c]
        edges[256 * c : 256 * c + 256, :] = jnp.where(pi == 0, above, below).reshape(256, 64)
    for copy in copies[2:]:
        copy.wait()
    for a in range(4):
        flat = jnp.transpose(basis[a * 128 : (a + 1) * 128, :].astype(F32))
        tables[LEAF + a * 64 : LEAF + (a + 1) * 64, 0:128] = flat.astype(BF)
    tables[LEAF : LEAF + 256, 128:160] = transfer[...]
    near_out[256:264, :] = order[...].astype(F32)


def downward_kernel(count_x, count_y):
    def body(group, near_part, tables, edges, cross, shared, out_hbm, h0, h1, h2, out, sem):
        gx, gy, pi, pj = place()
        swap = swap_of(gx, gy, count_x, count_y)
        me, across_x, across_y = 2 * pi + pj, 2 * (1 - pi) + pj, 2 * pi + 1 - pj
        across = 2 * (1 - pi) + 1 - pj
        from_x, from_y = (2 * pi + 1 - pj) ^ swap, (2 * (1 - pi) + pj) ^ swap
        from_xy = (2 * pi + pj) ^ swap
        has_x = jnp.where(pi == 0, gx > 0, gx < count_x - 1)
        has_y = jnp.where(pj == 0, gy > 0, gy < count_y - 1)
        has_xy = has_x & has_y

        def kept(keep, value):
            return jnp.where(keep, value, jnp.zeros_like(value))

        lane = lane_of(64)
        near_half = (lane < 64) == (pj == 0)
        h0[0:32, :] = jnp.zeros((32, 256), BF)
        h0[288:320, :] = jnp.zeros((32, 256), BF)
        h0[96:224, 0:128] = group[me, OWN_E0 : OWN_E0 + 128, :]
        strip = kept(has_y, cross[from_y, FAR_E0 : FAR_E0 + 64, :])
        beside = group[across_y, OWN_E0 : OWN_E0 + 128, :]
        h0[96:160, 128:256] = jnp.where(near_half, beside[:64], strip)
        h0[160:224, 128:256] = jnp.where(near_half, beside[64:], roll(strip, 64))
        start = 32 + 192 * (1 - pi)
        h0[pl.ds(start, 64), 0:128] = group[across_x, pl.ds(OWN_E0 + 64 * pi, 64), :]
        h0[pl.ds(start, 64), 128:256] = jnp.where(
            near_half,
            group[across, pl.ds(OWN_E0 + 64 * pi, 64), :],
            kept(has_y, cross[from_y, FAR_CORNER : FAR_CORNER + 64, :]),
        )
        start = 32 + 192 * pi
        h0[pl.ds(start, 64), 0:128] = kept(has_x, cross[from_x, FAR_E0 : FAR_E0 + 64, :])
        h0[pl.ds(start, 64), 128:256] = jnp.where(
            near_half,
            kept(has_x, cross[from_x, FAR_CORNER : FAR_CORNER + 64, :]),
            kept(has_xy, cross[from_xy, FAR_CORNER : FAR_CORNER + 64, :]),
        )

        def store_sides(start, middle, inner, outer):
            left = jnp.where(pj == 0, outer, inner)
            right = jnp.where(pj == 0, inner, outer)
            store_row_of_tiles(h1, start, left, middle, right)

        for halo in (h1, h2):
            halo[0:32, :] = jnp.zeros((32, 256), BF)
            halo[224:256, :] = jnp.zeros((32, 256), BF)
        own_e1 = slice(OWN_E1, OWN_E1 + 32)
        far_e1, side_e1 = slice(FAR_E1, FAR_E1 + 32), slice(FAR_E1_SIDE, FAR_E1_SIDE + 32)
        store_sides(
            96, group[me, own_e1, :], group[across_y, own_e1, :], kept(has_y, cross[from_y, far_e1, :])
        )
        store_sides(
            32 + 128 * (1 - pi),
            group[across_x, own_e1, :],
            group[across, own_e1, :],
            kept(has_y, cross[from_y, side_e1, :]),
        )
        store_sides(
            32 + 128 * pi,
            kept(has_x, cross[from_x, far_e1, :]),
            kept(has_x, cross[from_x, side_e1, :]),
            kept(has_xy, cross[from_xy, far_e1, :]),
        )

        above, below = gx >= 2, gx < count_x - 2
        before, after = gy >= 2, gy < count_y - 2
        e2 = group[0, OWN_E2:OWN_ROWS, :]
        for m in range(1, 4):
            e2 = e2 + group[m, OWN_E2:OWN_ROWS, :]

        def brought(m, slot, keep):
            other = swap_of(gx - pi + m // 2, gy - pj + m % 2, count_x, count_y)
            return kept(keep, shared[m, slot ^ other])

        store_row_of_tiles(
            h2, 32, brought(0, 0, above & before), brought(0, 1, above), brought(1, 1, above & after)
        )
        store_row_of_tiles(h2, 96, brought(0, 2, before), e2, brought(1, 3, after))
        store_row_of_tiles(
            h2, 160, brought(2, 2, below & before), brought(2, 3, below), brought(3, 3, below & after)
        )

        slot = slot_of(32)
        local2 = far_row(tables[448 : 672, 0:224], h2[pl.ds(32 * pi, 224), :], pi)
        local2 = jnp.where(slot == pj, local2, 0.0)
        local2 = local2 + roll(local2, 64)
        local2 = (local2 + roll(local2, 32)).astype(BF)
        transfer = tables[LEAF : LEAF + 256, 128:160]
        spread = dot(transfer[128:256], local2)
        local1 = []
        for i in range(2):
            down = far_row(tables[224 : 448, 0:224], h1[32 * i : 32 * i + 224, :], i)
            for j in range(2):
                n = 2 * i + j
                down = down + jnp.where(slot == j, spread[n * 32 : (n + 1) * 32], 0.0)
            down = jnp.where(slot < 2, down, 0.0)
            wide = jnp.where(slot == 0, down, 0.0) + jnp.where(slot == 2, roll(down, 32), 0.0)
            local1.append((wide + roll(wide, 32)).astype(BF))
        local0 = []
        for i in range(4):
            spread = dot(transfer[64 * (i % 2) : 64 * (i % 2) + 64], local1[i // 2])
            down = far_row(tables[0 : 224, 0:224], h0[32 * i : 32 * i + 224, :], i % 2)
            down = down + jnp.where(lax.rem(slot, 2) == 0, spread[:32], spread[32:])
            local0.append(down.astype(BF))


        slot = slot_of(64)
        column = kept(has_y, cross[from_y, FAR_X : FAR_X + 64, :])
        corner_in = kept(has_y, roll(cross[from_y, FAR_CORNER : FAR_CORNER + 64, :], 64))
        corner_out = kept(has_xy, roll(cross[from_xy, FAR_CORNER : FAR_CORNER + 64, :], 64))
        boxes = {a: roll(column, -32 * a) for a in range(4)}
        boxes[-1] = jnp.where(pi == 0, corner_out, corner_in)
        boxes[4] = jnp.where(pi == 0, corner_in, corner_out)
        edge = slot == 3 * pj
        for a in boxes:
            moved = jnp.where(pj == 0, roll(boxes[a], 32), roll(boxes[a], -32))
            boxes[a] = jnp.where(edge, moved, jnp.zeros_like(moved))
        middle = kept(has_x, cross[from_x, FAR_X : FAR_X + 64, :])
        inner = kept(has_x, roll(cross[from_x, FAR_CORNER : FAR_CORNER + 64, :], 64))
        nothing = jnp.zeros_like(inner)
        left = jnp.where(pj == 0, nothing, inner)
        right = jnp.where(pj == 0, inner, nothing)
        shifts = (
            roll(jnp.where(slot == 3, left, middle), 32),
            middle,
            roll(jnp.where(slot == 0, right, middle), -32),
        )
        beyond = jnp.zeros((256, 128), F32)
        for c in range(3):
            beyond = beyond + dot(edges[256 * c : 256 * c + 256, :], shifts[c])
        beyond = merge_diagonal(beyond, 64)

        block = lax.broadcasted_iota(jnp.int32, (128, 128), 0) // 32 == slot_of(128)
        part, within = split_order(near_part[256:264, :].astype(jnp.int32))
        pick = jnp.concatenate([pick_sites(within[n : n + 1, :]) for n in range(8)], axis=1)
        leaves = []
        for a in range(4):
            total = near_part[a * 64 : (a + 1) * 64, :]
            if a == 0:
                total = total + jnp.where(pi == 0, beyond, 0.0)
            if a == 3:
                total = total + jnp.where(pi == 0, 0.0, beyond)
            for r in range(3):
                row = 768 + 64 * (3 * a + r)
                total = total + dot(edges[row : row + 64, :], boxes[a + r - 1])
            leaf = tables[LEAF + a * 64 : LEAF + (a + 1) * 64, 0:128]
            local = jnp.concatenate([local0[a]] * 4, axis=0)
            total = total + dot(leaf, jnp.where(block, local, jnp.zeros_like(local)))
            leaves.append(total)
        spread = []
        for pair in range(2):
            turned = jnp.transpose(jnp.concatenate(leaves[2 * pair : 2 * pair + 2], axis=0))
            for b in range(4):
                n = 4 * pair + b
                line = turned[32 * b : 32 * b + 32]
                parts = [jnp.where(part[n : n + 1, :] == t, line, 0.0) for t in range(8)]
                spread.append(jnp.concatenate(parts, axis=0).astype(BF))
        done = dot_nt(jnp.concatenate(spread, axis=1), pick).astype(BF)
        for t in range(8):
            out[:, 128 * t : 128 * (t + 1)] = done[32 * t : 32 * t + 32]
        last = pltpu.make_async_copy(out, out_hbm, sem)
        last.start()
        last.wait()

    return body


def call(kernel, spaces, shapes, scratch=(), flops=10**6):
    def run(*args):
        return pl.pallas_call(
            kernel,
            out_shape=shapes,
            in_specs=[pl.BlockSpec(memory_space=space) for space in spaces],
            out_specs=jax.tree.map(lambda shape: pl.BlockSpec(memory_space=shape.memory_space), shapes),
            scratch_shapes=list(scratch),
            cost_estimate=pl.CostEstimate(flops=flops, bytes_accessed=2**20, transcendentals=0),
            compiler_params=pltpu.CompilerParams(vmem_limit_bytes=VMEM_BYTES),
        )(*map(pltpu.with_memory_space_constraint, args, spaces))

    return run


def aligned_groups(count_x, count_y):
    return [
        [(i + di) * count_y + j + dj for di in range(2) for dj in range(2)]
        for i in range(0, count_x, 2)
        for j in range(0, count_y, 2)
    ]


def shifted_groups(count_x, count_y):
    last_x, last_y = count_x - 1, count_y - 1
    groups = [
        [(i, j), (i, j + 1), (i + 1, j), (i + 1, j + 1)]
        for i in range(1, last_x, 2)
        for j in range(1, last_y, 2)
    ]
    for i in (0, last_x):
        groups.append([(i, 1), (i, 2), (i, last_y), (i, 0)])
        groups += [[(i, j + d) for d in (2, 3, 0, 1)] for j in range(3, last_y, 4)]
    for i in range(1, last_x, 4):
        if i + 3 < last_x:
            for j in (0, last_y):
                lanes = (i + 2, i) if j == 0 else (i, i + 2)
                groups.append([(g + d, j) for d in range(2) for g in lanes])
        else:
            groups.append([(i + d, j) for d in range(2) for j in (last_y, 0)])
    return [[i * count_y + j for i, j in group] for group in groups]


def run_upward(samples, order, basis, transfer, near_blocks):
    return call(
        upward_kernel,
        (HBM,) * 5,
        (VMEM((256, 128), BF), VMEM((OWN_ROWS, 128), BF), VMEM((2, 4, 9, 64, 64), BF)),
        (
            VMEM((8, 128), jnp.int32),
            VMEM((32, 1024), BF),
            VMEM((512, 64), BF),
            VMEM((256, 32), BF),
            pltpu.SemaphoreType.DMA((5,)),
        ),
    )(samples, order, basis, transfer, near_blocks)


def run_cross(group, x, count_x, count_y):
    body = functools.partial(cross_kernel, count_x=count_x, count_y=count_y)
    return call(body, (VMEM,) * 2, VMEM((4, FAR_ROWS, 128), BF))(group, x)


def run_inner(group, x, near, near_blocks, coupling, basis, transfer, order):
    return call(
        inner_kernel,
        (VMEM,) * 3 + (HBM,) * 5,
        (VMEM((264, 128), F32), VMEM((TABLE_ROWS, 256), BF), VMEM((1536, 64), BF)),
        (
            VMEM((2, 4, 9, 64, 64), BF),
            VMEM((3, 32, 32, 40), BF),
            VMEM((512, 64), BF),
            VMEM((256, 32), BF),
            VMEM((8, 128), jnp.int32),
            VMEM((256, 128), F32),
            VMEM((256, 128), F32),
            pltpu.SemaphoreType.DMA((5,)),
        ),
        flops=10**9,
    )(group, x, near, near_blocks, coupling, basis, transfer, order)


def run_downward(group, inner, cross, shared, count_x, count_y):
    return call(
        downward_kernel(count_x, count_y),
        (VMEM,) * 6,
        HBM((32, 1024), BF),
        (
            VMEM((320, 256), BF),
            VMEM((256, 256), BF),
            VMEM((256, 256), BF),
            VMEM((32, 1024), BF),
            pltpu.SemaphoreType.DMA,
        ),
    )(group, *inner, cross, shared)


def solution(mesh):
    count_x, count_y = mesh.shape["gx"], mesh.shape["gy"]
    aligned = aligned_groups(count_x, count_y)
    shifted = shifted_groups(count_x, count_y)

    def local(samples, site_order, leaf_basis, near_blocks, transfer, coupling):
        samples = samples.T
        order = site_order.reshape(8, 128)
        basis = leaf_basis.transpose(0, 1, 3, 2).reshape(512, 64)
        transfer = transfer.reshape(256, 32)
        coupling = coupling.transpose(0, 2, 3, 1)
        x, message, near = run_upward(samples, order, basis, transfer, near_blocks)
        group = lax.all_gather(message, AXES, axis_index_groups=aligned)
        send = run_cross(group, x, count_x, count_y)
        cross = lax.all_to_all(send, AXES, 0, 0, axis_index_groups=shifted)
        inner = run_inner(
            group, x, near, near_blocks, coupling, basis, transfer, order
        )
        shared = lax.all_gather(cross[:, FAR_E2 : FAR_E2 + 32], AXES, axis_index_groups=aligned)
        out = run_downward(group, inner, cross, shared, count_x, count_y)
        return out.T

    return jax.shard_map(
        local,
        mesh=mesh,
        in_specs=(
            P(("gx", "gy"), None),
            P(("gx", "gy")),
            P("gx", "gy", None, None),
            P("gx", "gy", None, None, None),
            P(),
            P(),
        ),
        out_specs=P(("gx", "gy"), None),
        check_vma=False,
    )
```

```python
import functools

import jax
import jax.numpy as jnp
from jax import lax
from jax.experimental import pallas as pl
from jax.experimental.pallas import tpu as pltpu
from jax.sharding import PartitionSpec as P

BF = jnp.bfloat16
F32 = jnp.float32
AXES = ("gx", "gy")
LEAF, TABLE_ROWS = 672, 928
VMEM_BYTES = 32 * 1024 * 1024
VMEM, HBM = pltpu.VMEM, pltpu.HBM

OWN_ROW, OWN_COL, OWN_E0, OWN_ROWS = 0, 64, 128, 256
FAR_X, FAR_E0, FAR_CORNER, FAR_E1, FAR_E1_SIDE, FAR_E2, FAR_ROWS = 0, 64, 128, 192, 224, 256, 288


def dot(a, b):
    return lax.dot_general(a, b, (((1,), (0,)), ((), ())), preferred_element_type=F32)


def dot_nt(a, b):
    return lax.dot_general(a, b, (((1,), (1,)), ((), ())), preferred_element_type=F32)


def roll(x, lanes):
    lanes = lanes % x.shape[1]
    if lanes == 0:
        return x
    if x.dtype == BF:
        return pltpu.roll(x.astype(F32), lanes, 1).astype(BF)
    return pltpu.roll(x, lanes, 1)


def lane_of(rows, lanes=128):
    return lax.broadcasted_iota(jnp.int32, (rows, lanes), 1)


def slot_of(rows, lanes=128):
    return lane_of(rows, lanes) // 32


def eye(n):
    row = lax.broadcasted_iota(jnp.int32, (n, n), 0)
    return jnp.where(row == lane_of(n, n), 1.0, 0.0).astype(BF)


def place():
    gx, gy = lax.axis_index("gx"), lax.axis_index("gy")
    return gx, gy, lax.rem(gx, 2), lax.rem(gy, 2)


def corner_pair(count_y):
    return (count_y - 8) // 2 if count_y > 8 else 0


def swap_of(gx, gy, count_x, count_y):
    end_x = (gx == 0) | (gx == count_x - 1)
    end_y = (gy == 0) | (gy == count_y - 1)
    corner = corner_pair(count_y)
    pair = lax.div(gy + 1, 2) - 1
    first = (pair == corner) | (lax.rem(jnp.where(pair > corner, pair + 1, pair), 2) == 0)
    along_y = jnp.where(first == (gx == 0), 2, 0)
    along_x = jnp.where(lax.rem(gx + 3, 4) >= 2, 1, 0)
    return jnp.where(end_x & ~end_y, along_y, jnp.where(end_y & ~end_x, along_x, 0))


def merge_diagonal(blocks, height):
    slot = slot_of(height)
    out = jnp.zeros((height, 128), F32)
    for b in range(4):
        out = jnp.where(slot == b, blocks[b * height : (b + 1) * height], out)
    return out


def split_order(order):
    lane = lane_of(1)
    lines = []
    for pair in range(2):
        for b in range(4):
            low = order[4 * pair + b // 2 : 4 * pair + b // 2 + 1, :]
            high = order[4 * pair + 2 + b // 2 : 4 * pair + 3 + b // 2, :]
            if b % 2 == 0:
                lines.append(jnp.where(lane < 64, low, pltpu.roll(high, 64, 1)))
            else:
                lines.append(jnp.where(lane < 64, pltpu.roll(low, 64, 1), high))
    lines = jnp.concatenate(lines, axis=0)
    return lines // 128, lines % 128


def pick_sites(within):
    row = lax.broadcasted_iota(jnp.int32, (128, 128), 0)
    return jnp.where(within == row, 1.0, 0.0).astype(BF)


def fetch(sources, targets, sems):
    copies = [
        pltpu.make_async_copy(source, target, sems.at[n])
        for n, (source, target) in enumerate(zip(sources, targets))
    ]
    for copy in copies:
        copy.start()
    return copies


def upward_kernel(
    samples_hbm, order_hbm, basis_hbm, transfer_hbm, near_hbm,
    x_out, msg, near, turned, order, samples, basis, transfer, sems,
):
    copies = fetch(
        (order_hbm, samples_hbm, basis_hbm, transfer_hbm, near_hbm.at[0:2]),
        (order, samples, basis, transfer, near),
        sems,
    )
    _, _, pi, pj = place()
    copies[0].wait()
    block, within = split_order(order[...])
    picks = [pick_sites(within[n : n + 1, :]) for n in range(8)]
    copies[1].wait()
    table = jnp.concatenate([samples[:, 128 * t : 128 * t + 128] for t in range(8)], axis=0)
    xs, e0s = [], []
    for pair in range(2):
        columns = []
        for b in range(4):
            n = 4 * pair + b
            found = dot(table, picks[n])
            columns.append(
                sum(
                    jnp.where(block[n : n + 1, :] == t, found[32 * t : 32 * t + 32], 0.0)
                    for t in range(8)
                )
            )
        both = jnp.transpose(jnp.concatenate(columns, axis=0)).astype(BF)
        x_out[128 * pair : 128 * pair + 128, :] = both
        xs += [both[:64], both[64:]]
    slot = slot_of(64)
    copies[2].wait()
    for a in range(4):
        e0 = merge_diagonal(dot(basis[a * 128 : (a + 1) * 128, :], xs[a]), 32).astype(BF)
        msg[OWN_E0 + a * 32 : OWN_E0 + (a + 1) * 32, :] = e0
        e0s.append(e0)
    msg[OWN_ROW : OWN_ROW + 64, :] = jnp.where(pi == 0, xs[3], xs[0])
    column_slot = jnp.where(pj == 0, 3, 0)
    packed = jnp.zeros((64, 128), BF)
    for a in range(4):
        packed = jnp.where(slot == lax.rem(column_slot + a, 4), roll(xs[a], 32 * a), packed)
    msg[OWN_COL : OWN_COL + 64, :] = packed

    one = eye(32)
    copies[3].wait()
    for n in range(8):
        block = slice(n * 32, (n + 1) * 32)
        turned[block, :] = dot_nt(one, transfer[block, :]).astype(BF)
    copies[4].wait()


def lift(group, turned, tiles):
    slot = lax.rem(slot_of(32, 512), 4)
    lines = [
        jnp.concatenate(
            [group[m, OWN_E0 + 32 * x : OWN_E0 + 32 * x + 32, :] for m in range(4)], axis=1
        )
        for x in range(4)
    ]
    matrices = [turned[32 * n : 32 * n + 32, :] for n in range(4)]
    e1 = jnp.zeros((32, 512), F32)
    for x in range(2):
        parts = []
        for j in range(2):
            parts.append(dot(matrices[j], lines[2 * x]) + dot(matrices[2 + j], lines[2 * x + 1]))
        joined = parts[0] + roll(parts[1], -32)
        e1 = jnp.where(slot == 2 * x, roll(joined, 64 * x), e1)
        e1 = jnp.where(slot == 2 * x + 1, roll(joined, 64 * x - 32), e1)
    e1 = e1.astype(BF)
    product = dot(turned[128:256, :], e1)
    slot = slot_of(32)
    top = jnp.zeros((32, 128), F32)
    for m in range(4):
        tiles[m] = e1[:, 128 * m : 128 * m + 128]
        e2 = merge_diagonal(product[:, 128 * m : 128 * m + 128], 32)
        e2 = e2 + roll(e2, 64)
        e2 = e2 + roll(e2, 32)
        top = jnp.where(slot == m, e2, top)
    tiles[4] = top.astype(BF)


def cross_kernel(group, x, turned, send_hbm, tiles, send, sems, *, count_x, count_y):
    gx, gy, pi, pj = place()
    swap = swap_of(gx, gy, count_x, count_y)
    me, across_x, across_y = 2 * pi + pj, 2 * (1 - pi) + pj, 2 * pi + 1 - pj
    lane, slot = lane_of(64), slot_of(64)
    near_half = (lane < 64) == (pj == 0)
    e0 = group[me, OWN_E0 : OWN_E0 + 128, :]
    e0_rows = jnp.where(pi == 0, e0[:64], e0[64:])
    x_row = jnp.where(pi == 0, x[0:64, :], x[192:256, :])
    to = (2 * pi + 1 - pj) ^ swap
    send[to, FAR_X : FAR_X + 64, :] = x_row
    send[to, FAR_E0 : FAR_E0 + 64, :] = e0_rows
    column = group[across_y, OWN_COL : OWN_COL + 64, :]
    column = jnp.where(pi == 0, roll(column, 64), roll(column, -32))
    corner_e0 = group[across_y, pl.ds(OWN_E0 + 64 * pi, 64), :]
    send[to, FAR_CORNER : FAR_CORNER + 64, :] = jnp.where(near_half, corner_e0, column)
    side_y = to

    to = (2 * (1 - pi) + pj) ^ swap
    column_slot = jnp.where(pj == 0, 0, 3)
    packed = jnp.zeros((64, 128), BF)
    for a in range(4):
        moved = roll(x[a * 64 : (a + 1) * 64, :], 32 * a)
        packed = jnp.where(slot == lax.rem(column_slot + a, 4), moved, packed)
    send[to, FAR_X : FAR_X + 64, :] = packed
    send[to, FAR_E0 : FAR_E0 + 64, :] = jnp.where(near_half, e0[:64], roll(e0[64:], 64))
    corner_x = roll(group[across_x, OWN_ROW : OWN_ROW + 64, :], 64)
    corner_e0 = group[across_x, pl.ds(OWN_E0 + 64 * pi, 64), :]
    send[to, FAR_CORNER : FAR_CORNER + 64, :] = jnp.where(near_half, corner_e0, corner_x)
    side_x = to

    to = (2 * pi + pj) ^ swap
    send[to, 0:FAR_CORNER, :] = jnp.zeros((FAR_CORNER, 128), BF)
    send[to, FAR_CORNER : FAR_CORNER + 64, :] = jnp.where(near_half, e0_rows, roll(x_row, 64))
    send[(2 * (1 - pi) + 1 - pj) ^ swap, 0:FAR_E1, :] = jnp.zeros((FAR_E1, 128), BF)
    strips = pltpu.make_async_copy(
        send.at[:, 0:FAR_E1, :], send_hbm.at[:, 0:FAR_E1, :], sems.at[0]
    )
    strips.start()

    lift(group, turned, tiles)
    for m in range(4):
        send[m, FAR_E1 : FAR_E1 + 32, :] = tiles[me]
        send[m, FAR_E1_SIDE : FAR_E1_SIDE + 32, :] = jnp.zeros((32, 128), BF)
        send[m, FAR_E2 : FAR_E2 + 32, :] = tiles[4]
    send[side_y, FAR_E1_SIDE : FAR_E1_SIDE + 32, :] = tiles[across_y]
    send[side_x, FAR_E1_SIDE : FAR_E1_SIDE + 32, :] = tiles[across_x]
    levels = pltpu.make_async_copy(
        send.at[:, FAR_E1:FAR_ROWS, :], send_hbm.at[:, FAR_E1:FAR_ROWS, :], sems.at[1]
    )
    levels.start()
    strips.wait()
    levels.wait()


def store_row_of_tiles(halo, start, left, middle, right):
    lane = lane_of(32)
    low = lane < 64
    nothing = jnp.zeros((32, 128), BF)
    first = jnp.where(low, middle, roll(right, 64))
    second = jnp.where(low, roll(middle, 64), right)
    halo[pl.ds(start, 32), 0:128] = first
    halo[pl.ds(start, 32), 128:256] = jnp.where(low, nothing, roll(left, 64))
    halo[pl.ds(start + 32, 32), 0:128] = second
    halo[pl.ds(start + 32, 32), 128:256] = jnp.where(low, nothing, left)


def far_row(matrix, window, parity):
    lane = lane_of(224, 224)
    admitted = (lane >= 32 * (1 - parity)) & (lane < 224 - 32 * parity)
    product = dot(jnp.where(admitted, matrix, jnp.zeros((224, 224), BF)), window)
    odd = lax.rem(slot_of(32), 2) == 1
    out = jnp.zeros((32, 128), F32)
    for w in range(-3, 4):
        part = product[(w + 3) * 32 : (w + 4) * 32]
        part = part[:, :128] if w == 0 else pltpu.roll(part, (-32 * w) % 256, 1)[:, :128]
        if w == -3:
            part = jnp.where(odd, part, 0.0)
        if w == 3:
            part = jnp.where(odd, 0.0, part)
        out = out + part
    return out


def turn_coupling(coupling, turned, tables):
    row = lax.broadcasted_iota(jnp.int32, (56, 40), 0)
    number = lane_of(56, 40)
    u, w = row // 8 - 3, row % 8 - 3
    outer = (abs(u) >= 2) & (w <= 3)
    inner = (abs(u) < 2) & (abs(w) >= 2) & (w <= 3)
    index = jnp.where(u < -1, (u + 3) * 7 + w + 3, 26 + (u - 2) * 7 + w + 3)
    index = jnp.where(abs(u) < 2, 14 + (u + 1) * 4 + jnp.where(w < 0, w + 3, w), index)
    choose = jnp.where((outer | inner) & (number == index), 1.0, 0.0).astype(BF)
    slot = slot_of(8)
    for level in range(3):
        for block in range(8):
            lines = coupling[level, 4 * block : 4 * block + 4].reshape(128, 40)
            part = dot_nt(choose, lines)
            moved = [part] + [pltpu.roll(part, 32 * q, 1) for q in range(1, 4)]
            for q in range(4):
                i = 4 * block + q
                for half in range(2):
                    out = jnp.zeros((8, 128), F32)
                    for u in range(4 * half, min(4 * half + 4, 7)):
                        piece = moved[(u - q) % 4][8 * u : 8 * u + 8]
                        out = jnp.where(slot == u % 4, piece, out)
                    turned[half][pl.ds(i, 8, stride=32), :] = out
        for half in range(2):
            lines = turned[half][0:224, :].astype(BF)
            tables[224 * level : 224 * level + 224, 128 * half : 128 * half + 128] = lines


def inner_kernel(
    group, x, near_low, near_hbm, coupling_hbm, basis_hbm, transfer_hbm, order_hbm,
    near_out, tables, edges,
    near_high, coupling, basis, transfer, order, turned_low, turned_high, sems,
):
    copies = fetch(
        (coupling_hbm, near_hbm.at[2:4], basis_hbm, transfer_hbm, order_hbm),
        (coupling, near_high, basis, transfer, order),
        sems,
    )
    _, _, pi, pj = place()
    across_x, across_y, across = 2 * (1 - pi) + pj, 2 * pi + 1 - pj, 2 * (1 - pi) + 1 - pj
    slot = slot_of(64)
    windows = {}

    def store_windows(a, middle, inner):
        left = jnp.where(pj == 0, jnp.zeros_like(inner), inner)
        right = jnp.where(pj == 0, inner, jnp.zeros_like(inner))
        windows[a, 0] = middle
        windows[a, -1] = roll(jnp.where(slot == 3, left, middle), 32)
        windows[a, 1] = roll(jnp.where(slot == 0, right, middle), -32)

    beside = group[across_y, OWN_COL : OWN_COL + 64, :]
    for a in range(4):
        store_windows(a, x[a * 64 : (a + 1) * 64, :], roll(beside, -32 * a))
    middle = group[across_x, OWN_ROW : OWN_ROW + 64, :]
    inner = group[across, OWN_ROW : OWN_ROW + 64, :]
    nothing = jnp.zeros((64, 128), BF)
    store_windows(-1, jnp.where(pi == 0, nothing, middle), jnp.where(pi == 0, nothing, inner))
    store_windows(4, jnp.where(pi == 0, middle, nothing), jnp.where(pi == 0, inner, nothing))
    def add_near(a):
        near = near_low if a < 2 else near_high
        total = jnp.zeros((256, 128), F32)
        for n in range(9):
            matrix = near[a % 2, :, n].reshape(256, 64)
            total = total + dot(matrix, windows[a + n // 3 - 1, n % 3 - 1])
        near_out[a * 64 : (a + 1) * 64, :] = merge_diagonal(total, 64)
        for r in range(3):
            row = 768 + 64 * (3 * a + r)
            edges[row : row + 64, :] = near[a % 2, 3 * pj, 3 * r + 2 * pj]

    add_near(0)
    add_near(1)
    copies[0].wait()
    turn_coupling(coupling, (turned_low, turned_high), tables)
    copies[1].wait()
    add_near(2)
    add_near(3)
    for c in range(3):
        above, below = near_low[0, :, c], near_high[1, :, 6 + c]
        edges[256 * c : 256 * c + 256, :] = jnp.where(pi == 0, above, below).reshape(256, 64)
    for copy in copies[2:]:
        copy.wait()
    for a in range(4):
        flat = jnp.transpose(basis[a * 128 : (a + 1) * 128, :].astype(F32))
        tables[LEAF + a * 64 : LEAF + (a + 1) * 64, 0:128] = flat.astype(BF)
    tables[LEAF : LEAF + 256, 128:160] = transfer[...]
    near_out[256:264, :] = order[...].astype(F32)


def downward_kernel(count_x, count_y):
    def body(group, tiles, near_part, tables, edges, cross, shared, out_hbm, h0, h1, h2, out, sem):
        gx, gy, pi, pj = place()
        swap = swap_of(gx, gy, count_x, count_y)
        me, across_x, across_y = 2 * pi + pj, 2 * (1 - pi) + pj, 2 * pi + 1 - pj
        across = 2 * (1 - pi) + 1 - pj
        from_x, from_y = (2 * pi + 1 - pj) ^ swap, (2 * (1 - pi) + pj) ^ swap
        from_xy = (2 * pi + pj) ^ swap
        has_x = jnp.where(pi == 0, gx > 0, gx < count_x - 1)
        has_y = jnp.where(pj == 0, gy > 0, gy < count_y - 1)
        has_xy = has_x & has_y

        def kept(keep, value):
            return jnp.where(keep, value, jnp.zeros_like(value))

        lane = lane_of(64)
        near_half = (lane < 64) == (pj == 0)
        h0[0:32, :] = jnp.zeros((32, 256), BF)
        h0[288:320, :] = jnp.zeros((32, 256), BF)
        h0[96:224, 0:128] = group[me, OWN_E0 : OWN_E0 + 128, :]
        strip = kept(has_y, cross[from_y, FAR_E0 : FAR_E0 + 64, :])
        beside = group[across_y, OWN_E0 : OWN_E0 + 128, :]
        h0[96:160, 128:256] = jnp.where(near_half, beside[:64], strip)
        h0[160:224, 128:256] = jnp.where(near_half, beside[64:], roll(strip, 64))
        start = 32 + 192 * (1 - pi)
        h0[pl.ds(start, 64), 0:128] = group[across_x, pl.ds(OWN_E0 + 64 * pi, 64), :]
        h0[pl.ds(start, 64), 128:256] = jnp.where(
            near_half,
            group[across, pl.ds(OWN_E0 + 64 * pi, 64), :],
            kept(has_y, cross[from_y, FAR_CORNER : FAR_CORNER + 64, :]),
        )
        start = 32 + 192 * pi
        h0[pl.ds(start, 64), 0:128] = kept(has_x, cross[from_x, FAR_E0 : FAR_E0 + 64, :])
        h0[pl.ds(start, 64), 128:256] = jnp.where(
            near_half,
            kept(has_x, cross[from_x, FAR_CORNER : FAR_CORNER + 64, :]),
            kept(has_xy, cross[from_xy, FAR_CORNER : FAR_CORNER + 64, :]),
        )

        def store_sides(start, middle, inner, outer):
            left = jnp.where(pj == 0, outer, inner)
            right = jnp.where(pj == 0, inner, outer)
            store_row_of_tiles(h1, start, left, middle, right)

        for halo in (h1, h2):
            halo[0:32, :] = jnp.zeros((32, 256), BF)
            halo[224:256, :] = jnp.zeros((32, 256), BF)
        far_e1, side_e1 = slice(FAR_E1, FAR_E1 + 32), slice(FAR_E1_SIDE, FAR_E1_SIDE + 32)
        store_sides(
            96, tiles[me], tiles[across_y], kept(has_y, cross[from_y, far_e1, :])
        )
        store_sides(
            32 + 128 * (1 - pi),
            tiles[across_x],
            tiles[across],
            kept(has_y, cross[from_y, side_e1, :]),
        )
        store_sides(
            32 + 128 * pi,
            kept(has_x, cross[from_x, far_e1, :]),
            kept(has_x, cross[from_x, side_e1, :]),
            kept(has_xy, cross[from_xy, far_e1, :]),
        )

        above, below = gx >= 2, gx < count_x - 2
        before, after = gy >= 2, gy < count_y - 2

        def brought(m, slot, keep):
            other = swap_of(gx - pi + m // 2, gy - pj + m % 2, count_x, count_y)
            return kept(keep, shared[m, slot ^ other])

        store_row_of_tiles(
            h2, 32, brought(0, 0, above & before), brought(0, 1, above), brought(1, 1, above & after)
        )
        store_row_of_tiles(h2, 96, brought(0, 2, before), tiles[4], brought(1, 3, after))
        store_row_of_tiles(
            h2, 160, brought(2, 2, below & before), brought(2, 3, below), brought(3, 3, below & after)
        )

        slot = slot_of(32)
        local2 = far_row(tables[448 : 672, 0:224], h2[pl.ds(32 * pi, 224), :], pi)
        local2 = jnp.where(slot == pj, local2, 0.0)
        local2 = local2 + roll(local2, 64)
        local2 = (local2 + roll(local2, 32)).astype(BF)
        transfer = tables[LEAF : LEAF + 256, 128:160]
        spread = dot(transfer[128:256], local2)
        local1 = []
        for i in range(2):
            down = far_row(tables[224 : 448, 0:224], h1[32 * i : 32 * i + 224, :], i)
            for j in range(2):
                n = 2 * i + j
                down = down + jnp.where(slot == j, spread[n * 32 : (n + 1) * 32], 0.0)
            down = jnp.where(slot < 2, down, 0.0)
            wide = jnp.where(slot == 0, down, 0.0) + jnp.where(slot == 2, roll(down, 32), 0.0)
            local1.append((wide + roll(wide, 32)).astype(BF))
        local0 = []
        for i in range(4):
            spread = dot(transfer[64 * (i % 2) : 64 * (i % 2) + 64], local1[i // 2])
            down = far_row(tables[0 : 224, 0:224], h0[32 * i : 32 * i + 224, :], i % 2)
            down = down + jnp.where(lax.rem(slot, 2) == 0, spread[:32], spread[32:])
            local0.append(down.astype(BF))


        slot = slot_of(64)
        column = kept(has_y, cross[from_y, FAR_X : FAR_X + 64, :])
        corner_in = kept(has_y, roll(cross[from_y, FAR_CORNER : FAR_CORNER + 64, :], 64))
        corner_out = kept(has_xy, roll(cross[from_xy, FAR_CORNER : FAR_CORNER + 64, :], 64))
        boxes = {a: roll(column, -32 * a) for a in range(4)}
        boxes[-1] = jnp.where(pi == 0, corner_out, corner_in)
        boxes[4] = jnp.where(pi == 0, corner_in, corner_out)
        edge = slot == 3 * pj
        for a in boxes:
            moved = jnp.where(pj == 0, roll(boxes[a], 32), roll(boxes[a], -32))
            boxes[a] = jnp.where(edge, moved, jnp.zeros_like(moved))
        middle = kept(has_x, cross[from_x, FAR_X : FAR_X + 64, :])
        inner = kept(has_x, roll(cross[from_x, FAR_CORNER : FAR_CORNER + 64, :], 64))
        nothing = jnp.zeros_like(inner)
        left = jnp.where(pj == 0, nothing, inner)
        right = jnp.where(pj == 0, inner, nothing)
        shifts = (
            roll(jnp.where(slot == 3, left, middle), 32),
            middle,
            roll(jnp.where(slot == 0, right, middle), -32),
        )
        beyond = jnp.zeros((256, 128), F32)
        for c in range(3):
            beyond = beyond + dot(edges[256 * c : 256 * c + 256, :], shifts[c])
        beyond = merge_diagonal(beyond, 64)

        block = lax.broadcasted_iota(jnp.int32, (128, 128), 0) // 32 == slot_of(128)
        part, within = split_order(near_part[256:264, :].astype(jnp.int32))
        pick = jnp.concatenate([pick_sites(within[n : n + 1, :]) for n in range(8)], axis=1)
        leaves = []
        for a in range(4):
            total = near_part[a * 64 : (a + 1) * 64, :]
            if a == 0:
                total = total + jnp.where(pi == 0, beyond, 0.0)
            if a == 3:
                total = total + jnp.where(pi == 0, 0.0, beyond)
            for r in range(3):
                row = 768 + 64 * (3 * a + r)
                total = total + dot(edges[row : row + 64, :], boxes[a + r - 1])
            leaf = tables[LEAF + a * 64 : LEAF + (a + 1) * 64, 0:128]
            local = jnp.concatenate([local0[a]] * 4, axis=0)
            total = total + dot(leaf, jnp.where(block, local, jnp.zeros_like(local)))
            leaves.append(total)
        spread = []
        for pair in range(2):
            turned = jnp.transpose(jnp.concatenate(leaves[2 * pair : 2 * pair + 2], axis=0))
            for b in range(4):
                n = 4 * pair + b
                line = turned[32 * b : 32 * b + 32]
                parts = [jnp.where(part[n : n + 1, :] == t, line, 0.0) for t in range(8)]
                spread.append(jnp.concatenate(parts, axis=0).astype(BF))
        done = dot_nt(jnp.concatenate(spread, axis=1), pick).astype(BF)
        for t in range(8):
            out[:, 128 * t : 128 * (t + 1)] = done[32 * t : 32 * t + 32]
        last = pltpu.make_async_copy(out, out_hbm, sem)
        last.start()
        last.wait()

    return body


def call(kernel, spaces, shapes, scratch=(), flops=10**6):
    def run(*args):
        return pl.pallas_call(
            kernel,
            out_shape=shapes,
            in_specs=[pl.BlockSpec(memory_space=space) for space in spaces],
            out_specs=jax.tree.map(lambda shape: pl.BlockSpec(memory_space=shape.memory_space), shapes),
            scratch_shapes=list(scratch),
            cost_estimate=pl.CostEstimate(flops=flops, bytes_accessed=2**20, transcendentals=0),
            compiler_params=pltpu.CompilerParams(vmem_limit_bytes=VMEM_BYTES),
        )(*map(pltpu.with_memory_space_constraint, args, spaces))

    return run


def aligned_groups(count_x, count_y):
    return [
        [(i + di) * count_y + j + dj for di in range(2) for dj in range(2)]
        for i in range(0, count_x, 2)
        for j in range(0, count_y, 2)
    ]


def shifted_groups(count_x, count_y):
    last_x, last_y = count_x - 1, count_y - 1
    groups = [
        [(i, j), (i, j + 1), (i + 1, j), (i + 1, j + 1)]
        for i in range(1, last_x, 2)
        for j in range(1, last_y, 2)
    ]
    for i in (0, last_x):
        pairs = [[(i, j), (i, j + 1)] for j in range(1, last_y, 2)]
        groups.append(pairs.pop(corner_pair(count_y)) + [(i, last_y), (i, 0)])
        groups += [pairs[n] + pairs[n + 1] for n in range(0, len(pairs), 2)]
    for i in range(1, last_x, 4):
        if i + 3 < last_x:
            for j in (0, last_y):
                lanes = (i + 2, i) if j == 0 else (i, i + 2)
                groups.append([(g + d, j) for d in range(2) for g in lanes])
        else:
            groups.append([(i + d, j) for d in range(2) for j in (last_y, 0)])
    return [[i * count_y + j for i, j in group] for group in groups]


def run_upward(samples, order, basis, transfer, near_blocks):
    return call(
        upward_kernel,
        (HBM,) * 5,
        (VMEM((256, 128), BF), VMEM((OWN_ROWS, 128), BF), VMEM((2, 4, 9, 64, 64), BF), VMEM((256, 32), BF)),
        (
            VMEM((8, 128), jnp.int32),
            VMEM((32, 1024), BF),
            VMEM((512, 64), BF),
            VMEM((256, 32), BF),
            pltpu.SemaphoreType.DMA((5,)),
        ),
    )(samples, order, basis, transfer, near_blocks)


def run_cross(group, x, turned, count_x, count_y):
    body = functools.partial(cross_kernel, count_x=count_x, count_y=count_y)
    return call(
        body,
        (VMEM,) * 3,
        (HBM((4, FAR_ROWS, 128), BF), VMEM((5, 32, 128), BF)),
        (VMEM((4, FAR_ROWS, 128), BF), pltpu.SemaphoreType.DMA((2,))),
    )(group, x, turned)


def run_inner(group, x, near, near_blocks, coupling, basis, transfer, order):
    return call(
        inner_kernel,
        (VMEM,) * 3 + (HBM,) * 5,
        (VMEM((264, 128), F32), VMEM((TABLE_ROWS, 256), BF), VMEM((1536, 64), BF)),
        (
            VMEM((2, 4, 9, 64, 64), BF),
            VMEM((3, 32, 32, 40), BF),
            VMEM((512, 64), BF),
            VMEM((256, 32), BF),
            VMEM((8, 128), jnp.int32),
            VMEM((256, 128), F32),
            VMEM((256, 128), F32),
            pltpu.SemaphoreType.DMA((5,)),
        ),
        flops=10**9,
    )(group, x, near, near_blocks, coupling, basis, transfer, order)


def run_downward(group, tiles, inner, cross, shared, count_x, count_y):
    return call(
        downward_kernel(count_x, count_y),
        (VMEM,) * 7,
        HBM((32, 1024), BF),
        (
            VMEM((320, 256), BF),
            VMEM((256, 256), BF),
            VMEM((256, 256), BF),
            VMEM((32, 1024), BF),
            pltpu.SemaphoreType.DMA,
        ),
    )(group, tiles, *inner, cross, shared)


def solution(mesh):
    count_x, count_y = mesh.shape["gx"], mesh.shape["gy"]
    aligned = aligned_groups(count_x, count_y)
    shifted = shifted_groups(count_x, count_y)

    def local(samples, site_order, leaf_basis, near_blocks, transfer, coupling):
        samples = samples.T
        order = site_order.reshape(8, 128)
        basis = leaf_basis.transpose(0, 1, 3, 2).reshape(512, 64)
        transfer = transfer.reshape(256, 32)
        coupling = coupling.transpose(0, 2, 3, 1)
        x, message, near, turned = run_upward(samples, order, basis, transfer, near_blocks)
        group = lax.all_gather(message, AXES, axis_index_groups=aligned)
        send, tiles = run_cross(group, x, turned, count_x, count_y)
        cross = lax.all_to_all(send, AXES, 0, 0, axis_index_groups=shifted)
        inner = run_inner(
            group, x, near, near_blocks, coupling, basis, transfer, order
        )
        shared = lax.all_gather(cross[:, FAR_E2 : FAR_E2 + 32], AXES, axis_index_groups=aligned)
        out = run_downward(group, tiles, inner, cross, shared, count_x, count_y)
        return out.T

    return jax.shard_map(
        local,
        mesh=mesh,
        in_specs=(
            P(("gx", "gy"), None),
            P(("gx", "gy")),
            P("gx", "gy", None, None),
            P("gx", "gy", None, None, None),
            P(),
            P(),
        ),
        out_specs=P(("gx", "gy"), None),
        check_vma=False,
    )
```

```python
import functools

import jax
import jax.numpy as jnp
from jax import lax
from jax.experimental import pallas as pl
from jax.experimental.pallas import tpu as pltpu
from jax.sharding import PartitionSpec as P

BF = jnp.bfloat16
F32 = jnp.float32
AXES = ("gx", "gy")
LEAF, TABLE_ROWS = 672, 928
VMEM_BYTES = 32 * 1024 * 1024
VMEM, HBM = pltpu.VMEM, pltpu.HBM

OWN_ROW, OWN_COL, OWN_E0, OWN_ROWS = 0, 64, 128, 256
FAR_X, FAR_E0, FAR_CORNER, FAR_E1, FAR_E1_SIDE, FAR_E2, FAR_ROWS = 0, 64, 128, 192, 224, 256, 288


def dot(a, b):
    return lax.dot_general(a, b, (((1,), (0,)), ((), ())), preferred_element_type=F32)


def dot_nt(a, b):
    return lax.dot_general(a, b, (((1,), (1,)), ((), ())), preferred_element_type=F32)


def roll(x, lanes):
    lanes = lanes % x.shape[1]
    if lanes == 0:
        return x
    if x.dtype == BF:
        return pltpu.roll(x.astype(F32), lanes, 1).astype(BF)
    return pltpu.roll(x, lanes, 1)


def lane_of(rows, lanes=128):
    return lax.broadcasted_iota(jnp.int32, (rows, lanes), 1)


def slot_of(rows, lanes=128):
    return lane_of(rows, lanes) // 32


def eye(n):
    row = lax.broadcasted_iota(jnp.int32, (n, n), 0)
    return jnp.where(row == lane_of(n, n), 1.0, 0.0).astype(BF)


def place():
    gx, gy = lax.axis_index("gx"), lax.axis_index("gy")
    return gx, gy, lax.rem(gx, 2), lax.rem(gy, 2)


def corner_pair(count_y):
    return (count_y - 8) // 2 if count_y > 8 else 0


def swap_of(gx, gy, count_x, count_y):
    end_x = (gx == 0) | (gx == count_x - 1)
    end_y = (gy == 0) | (gy == count_y - 1)
    corner = corner_pair(count_y)
    pair = lax.div(gy + 1, 2) - 1
    first = (pair == corner) | (lax.rem(jnp.where(pair > corner, pair + 1, pair), 2) == 0)
    along_y = jnp.where(first == (gx == 0), 2, 0)
    along_x = jnp.where(lax.rem(gx + 3, 4) >= 2, 1, 0)
    return jnp.where(end_x & ~end_y, along_y, jnp.where(end_y & ~end_x, along_x, 0))


def merge_diagonal(blocks, height):
    slot = slot_of(height)
    out = jnp.zeros((height, 128), F32)
    for b in range(4):
        out = jnp.where(slot == b, blocks[b * height : (b + 1) * height], out)
    return out


def split_order(order):
    lane = lane_of(1)
    lines = []
    for pair in range(2):
        for b in range(4):
            low = order[4 * pair + b // 2 : 4 * pair + b // 2 + 1, :]
            high = order[4 * pair + 2 + b // 2 : 4 * pair + 3 + b // 2, :]
            if b % 2 == 0:
                lines.append(jnp.where(lane < 64, low, pltpu.roll(high, 64, 1)))
            else:
                lines.append(jnp.where(lane < 64, pltpu.roll(low, 64, 1), high))
    lines = jnp.concatenate(lines, axis=0)
    return lines // 128, lines % 128


def pick_sites(within):
    row = lax.broadcasted_iota(jnp.int32, (128, 128), 0)
    return jnp.where(within == row, 1.0, 0.0).astype(BF)


def fetch(sources, targets, sems):
    copies = [
        pltpu.make_async_copy(source, target, sems.at[n])
        for n, (source, target) in enumerate(zip(sources, targets))
    ]
    for copy in copies:
        copy.start()
    return copies


def upward_kernel(
    samples_hbm, order_hbm, basis_hbm, transfer_hbm, near_hbm,
    x_out, msg, near, turned, order, samples, basis, transfer, sems,
):
    copies = fetch(
        (order_hbm, samples_hbm, basis_hbm, transfer_hbm, near_hbm.at[0:2]),
        (order, samples, basis, transfer, near),
        sems,
    )
    _, _, pi, pj = place()
    copies[0].wait()
    block, within = split_order(order[...])
    picks = [pick_sites(within[n : n + 1, :]) for n in range(8)]
    copies[1].wait()
    table = jnp.concatenate([samples[:, 128 * t : 128 * t + 128] for t in range(8)], axis=0)
    xs, e0s = [], []
    for pair in range(2):
        columns = []
        for b in range(4):
            n = 4 * pair + b
            found = dot(table, picks[n])
            columns.append(
                sum(
                    jnp.where(block[n : n + 1, :] == t, found[32 * t : 32 * t + 32], 0.0)
                    for t in range(8)
                )
            )
        both = jnp.transpose(jnp.concatenate(columns, axis=0)).astype(BF)
        x_out[128 * pair : 128 * pair + 128, :] = both
        xs += [both[:64], both[64:]]
    slot = slot_of(64)
    copies[2].wait()
    for a in range(4):
        e0 = merge_diagonal(dot(basis[a * 128 : (a + 1) * 128, :], xs[a]), 32).astype(BF)
        msg[OWN_E0 + a * 32 : OWN_E0 + (a + 1) * 32, :] = e0
        e0s.append(e0)
    msg[OWN_ROW : OWN_ROW + 64, :] = jnp.where(pi == 0, xs[3], xs[0])
    column_slot = jnp.where(pj == 0, 3, 0)
    packed = jnp.zeros((64, 128), BF)
    for a in range(4):
        packed = jnp.where(slot == lax.rem(column_slot + a, 4), roll(xs[a], 32 * a), packed)
    msg[OWN_COL : OWN_COL + 64, :] = packed

    one = eye(32)
    copies[3].wait()
    blocks = [dot_nt(one, transfer[n * 32 : (n + 1) * 32, :]).astype(BF) for n in range(8)]
    for j in range(2):
        turned[32 * j : 32 * j + 32, :] = jnp.concatenate([blocks[j], blocks[2 + j]], axis=1)
    for n in range(4):
        turned[64 + 32 * n : 96 + 32 * n, 0:32] = blocks[4 + n]
    copies[4].wait()


def lift(group, turned, tiles):
    slot = lax.rem(slot_of(32, 512), 4)
    e1 = jnp.zeros((32, 512), F32)
    for x in range(2):
        rows = slice(OWN_E0 + 64 * x, OWN_E0 + 64 * x + 64)
        lines = jnp.concatenate([group[m, rows, :] for m in range(4)], axis=1)
        parts = dot(turned[0:64, :], lines)
        joined = parts[:32] + roll(parts[32:], -32)
        e1 = jnp.where(slot == 2 * x, roll(joined, 64 * x), e1)
        e1 = jnp.where(slot == 2 * x + 1, roll(joined, 64 * x - 32), e1)
    e1 = e1.astype(BF)
    product = dot(turned[64:192, 0:32], e1)
    slot = slot_of(32)
    top = jnp.zeros((32, 128), F32)
    for m in range(4):
        tiles[m] = e1[:, 128 * m : 128 * m + 128]
        e2 = merge_diagonal(product[:, 128 * m : 128 * m + 128], 32)
        e2 = e2 + roll(e2, 64)
        e2 = e2 + roll(e2, 32)
        top = jnp.where(slot == m, e2, top)
    tiles[4] = top.astype(BF)


def cross_kernel(group, x, turned, send_hbm, tiles, send, sems, *, count_x, count_y):
    gx, gy, pi, pj = place()
    swap = swap_of(gx, gy, count_x, count_y)
    me, across_x, across_y = 2 * pi + pj, 2 * (1 - pi) + pj, 2 * pi + 1 - pj
    lane, slot = lane_of(64), slot_of(64)
    near_half = (lane < 64) == (pj == 0)
    e0 = group[me, OWN_E0 : OWN_E0 + 128, :]
    e0_rows = jnp.where(pi == 0, e0[:64], e0[64:])
    x_row = jnp.where(pi == 0, x[0:64, :], x[192:256, :])
    to = (2 * pi + 1 - pj) ^ swap
    send[to, FAR_X : FAR_X + 64, :] = x_row
    send[to, FAR_E0 : FAR_E0 + 64, :] = e0_rows
    column = group[across_y, OWN_COL : OWN_COL + 64, :]
    column = jnp.where(pi == 0, roll(column, 64), roll(column, -32))
    corner_e0 = group[across_y, pl.ds(OWN_E0 + 64 * pi, 64), :]
    send[to, FAR_CORNER : FAR_CORNER + 64, :] = jnp.where(near_half, corner_e0, column)
    side_y = to

    to = (2 * (1 - pi) + pj) ^ swap
    column_slot = jnp.where(pj == 0, 0, 3)
    packed = jnp.zeros((64, 128), BF)
    for a in range(4):
        moved = roll(x[a * 64 : (a + 1) * 64, :], 32 * a)
        packed = jnp.where(slot == lax.rem(column_slot + a, 4), moved, packed)
    send[to, FAR_X : FAR_X + 64, :] = packed
    send[to, FAR_E0 : FAR_E0 + 64, :] = jnp.where(near_half, e0[:64], roll(e0[64:], 64))
    corner_x = roll(group[across_x, OWN_ROW : OWN_ROW + 64, :], 64)
    corner_e0 = group[across_x, pl.ds(OWN_E0 + 64 * pi, 64), :]
    send[to, FAR_CORNER : FAR_CORNER + 64, :] = jnp.where(near_half, corner_e0, corner_x)
    side_x = to

    to = (2 * pi + pj) ^ swap
    send[to, 0:FAR_CORNER, :] = jnp.zeros((FAR_CORNER, 128), BF)
    send[to, FAR_CORNER : FAR_CORNER + 64, :] = jnp.where(near_half, e0_rows, roll(x_row, 64))
    send[(2 * (1 - pi) + 1 - pj) ^ swap, 0:FAR_E1, :] = jnp.zeros((FAR_E1, 128), BF)
    strips = pltpu.make_async_copy(
        send.at[:, 0:FAR_E1, :], send_hbm.at[:, 0:FAR_E1, :], sems.at[0]
    )
    strips.start()

    lift(group, turned, tiles)
    for m in range(4):
        send[m, FAR_E1 : FAR_E1 + 32, :] = tiles[me]
        send[m, FAR_E1_SIDE : FAR_E1_SIDE + 32, :] = jnp.zeros((32, 128), BF)
        send[m, FAR_E2 : FAR_E2 + 32, :] = tiles[4]
    send[side_y, FAR_E1_SIDE : FAR_E1_SIDE + 32, :] = tiles[across_y]
    send[side_x, FAR_E1_SIDE : FAR_E1_SIDE + 32, :] = tiles[across_x]
    levels = pltpu.make_async_copy(
        send.at[:, FAR_E1:FAR_ROWS, :], send_hbm.at[:, FAR_E1:FAR_ROWS, :], sems.at[1]
    )
    levels.start()
    strips.wait()
    levels.wait()


def store_row_of_tiles(halo, start, left, middle, right):
    lane = lane_of(32)
    low = lane < 64
    nothing = jnp.zeros((32, 128), BF)
    first = jnp.where(low, middle, roll(right, 64))
    second = jnp.where(low, roll(middle, 64), right)
    halo[pl.ds(start, 32), 0:128] = first
    halo[pl.ds(start, 32), 128:256] = jnp.where(low, nothing, roll(left, 64))
    halo[pl.ds(start + 32, 32), 0:128] = second
    halo[pl.ds(start + 32, 32), 128:256] = jnp.where(low, nothing, left)


def far_row(matrix, window, parity):
    lane = lane_of(224, 224)
    admitted = (lane >= 32 * (1 - parity)) & (lane < 224 - 32 * parity)
    product = dot(jnp.where(admitted, matrix, jnp.zeros((224, 224), BF)), window)
    odd = lax.rem(slot_of(32), 2) == 1
    out = jnp.zeros((32, 128), F32)
    for w in range(-3, 4):
        part = product[(w + 3) * 32 : (w + 4) * 32]
        part = part[:, :128] if w == 0 else pltpu.roll(part, (-32 * w) % 256, 1)[:, :128]
        if w == -3:
            part = jnp.where(odd, part, 0.0)
        if w == 3:
            part = jnp.where(odd, 0.0, part)
        out = out + part
    return out


def turn_coupling(coupling, turned, tables):
    row = lax.broadcasted_iota(jnp.int32, (56, 40), 0)
    number = lane_of(56, 40)
    u, w = row // 8 - 3, row % 8 - 3
    outer = (abs(u) >= 2) & (w <= 3)
    inner = (abs(u) < 2) & (abs(w) >= 2) & (w <= 3)
    index = jnp.where(u < -1, (u + 3) * 7 + w + 3, 26 + (u - 2) * 7 + w + 3)
    index = jnp.where(abs(u) < 2, 14 + (u + 1) * 4 + jnp.where(w < 0, w + 3, w), index)
    choose = jnp.where((outer | inner) & (number == index), 1.0, 0.0).astype(BF)
    slot = slot_of(8)
    for level in range(3):
        for block in range(8):
            lines = coupling[level, 4 * block : 4 * block + 4].reshape(128, 40)
            part = dot_nt(choose, lines)
            moved = [part] + [pltpu.roll(part, 32 * q, 1) for q in range(1, 4)]
            for q in range(4):
                i = 4 * block + q
                for half in range(2):
                    out = jnp.zeros((8, 128), F32)
                    for u in range(4 * half, min(4 * half + 4, 7)):
                        piece = moved[(u - q) % 4][8 * u : 8 * u + 8]
                        out = jnp.where(slot == u % 4, piece, out)
                    turned[half][pl.ds(i, 8, stride=32), :] = out
        for half in range(2):
            lines = turned[half][0:224, :].astype(BF)
            tables[224 * level : 224 * level + 224, 128 * half : 128 * half + 128] = lines


def inner_kernel(
    group, x, near_low, near_hbm, coupling_hbm, basis_hbm, transfer_hbm, order_hbm,
    near_out, tables, edges,
    near_high, coupling, basis, transfer, order, turned_low, turned_high, sems,
):
    copies = fetch(
        (coupling_hbm, near_hbm.at[2:4], basis_hbm, transfer_hbm, order_hbm),
        (coupling, near_high, basis, transfer, order),
        sems,
    )
    _, _, pi, pj = place()
    across_x, across_y, across = 2 * (1 - pi) + pj, 2 * pi + 1 - pj, 2 * (1 - pi) + 1 - pj
    slot = slot_of(64)
    windows = {}

    def store_windows(a, middle, inner):
        left = jnp.where(pj == 0, jnp.zeros_like(inner), inner)
        right = jnp.where(pj == 0, inner, jnp.zeros_like(inner))
        windows[a, 0] = middle
        windows[a, -1] = roll(jnp.where(slot == 3, left, middle), 32)
        windows[a, 1] = roll(jnp.where(slot == 0, right, middle), -32)

    beside = group[across_y, OWN_COL : OWN_COL + 64, :]
    for a in range(4):
        store_windows(a, x[a * 64 : (a + 1) * 64, :], roll(beside, -32 * a))
    middle = group[across_x, OWN_ROW : OWN_ROW + 64, :]
    inner = group[across, OWN_ROW : OWN_ROW + 64, :]
    nothing = jnp.zeros((64, 128), BF)
    store_windows(-1, jnp.where(pi == 0, nothing, middle), jnp.where(pi == 0, nothing, inner))
    store_windows(4, jnp.where(pi == 0, middle, nothing), jnp.where(pi == 0, inner, nothing))
    def add_near(a):
        near = near_low if a < 2 else near_high
        total = jnp.zeros((256, 128), F32)
        for n in range(9):
            matrix = near[a % 2, :, n].reshape(256, 64)
            total = total + dot(matrix, windows[a + n // 3 - 1, n % 3 - 1])
        near_out[a * 64 : (a + 1) * 64, :] = merge_diagonal(total, 64)
        for r in range(3):
            row = 768 + 64 * (3 * a + r)
            edges[row : row + 64, :] = near[a % 2, 3 * pj, 3 * r + 2 * pj]

    add_near(0)
    add_near(1)
    copies[0].wait()
    turn_coupling(coupling, (turned_low, turned_high), tables)
    copies[1].wait()
    add_near(2)
    add_near(3)
    for c in range(3):
        above, below = near_low[0, :, c], near_high[1, :, 6 + c]
        edges[256 * c : 256 * c + 256, :] = jnp.where(pi == 0, above, below).reshape(256, 64)
    for copy in copies[2:]:
        copy.wait()
    for a in range(4):
        flat = jnp.transpose(basis[a * 128 : (a + 1) * 128, :].astype(F32))
        tables[LEAF + a * 64 : LEAF + (a + 1) * 64, 0:128] = flat.astype(BF)
    tables[LEAF : LEAF + 256, 128:160] = transfer[...]
    near_out[256:264, :] = order[...].astype(F32)


def downward_kernel(count_x, count_y):
    def body(group, tiles, near_part, tables, edges, cross, shared, out_hbm, h0, h1, h2, out, sem):
        gx, gy, pi, pj = place()
        swap = swap_of(gx, gy, count_x, count_y)
        me, across_x, across_y = 2 * pi + pj, 2 * (1 - pi) + pj, 2 * pi + 1 - pj
        across = 2 * (1 - pi) + 1 - pj
        from_x, from_y = (2 * pi + 1 - pj) ^ swap, (2 * (1 - pi) + pj) ^ swap
        from_xy = (2 * pi + pj) ^ swap
        has_x = jnp.where(pi == 0, gx > 0, gx < count_x - 1)
        has_y = jnp.where(pj == 0, gy > 0, gy < count_y - 1)
        has_xy = has_x & has_y

        def kept(keep, value):
            return jnp.where(keep, value, jnp.zeros_like(value))

        lane = lane_of(64)
        near_half = (lane < 64) == (pj == 0)
        h0[0:32, :] = jnp.zeros((32, 256), BF)
        h0[288:320, :] = jnp.zeros((32, 256), BF)
        h0[96:224, 0:128] = group[me, OWN_E0 : OWN_E0 + 128, :]
        strip = kept(has_y, cross[from_y, FAR_E0 : FAR_E0 + 64, :])
        beside = group[across_y, OWN_E0 : OWN_E0 + 128, :]
        h0[96:160, 128:256] = jnp.where(near_half, beside[:64], strip)
        h0[160:224, 128:256] = jnp.where(near_half, beside[64:], roll(strip, 64))
        start = 32 + 192 * (1 - pi)
        h0[pl.ds(start, 64), 0:128] = group[across_x, pl.ds(OWN_E0 + 64 * pi, 64), :]
        h0[pl.ds(start, 64), 128:256] = jnp.where(
            near_half,
            group[across, pl.ds(OWN_E0 + 64 * pi, 64), :],
            kept(has_y, cross[from_y, FAR_CORNER : FAR_CORNER + 64, :]),
        )
        start = 32 + 192 * pi
        h0[pl.ds(start, 64), 0:128] = kept(has_x, cross[from_x, FAR_E0 : FAR_E0 + 64, :])
        h0[pl.ds(start, 64), 128:256] = jnp.where(
            near_half,
            kept(has_x, cross[from_x, FAR_CORNER : FAR_CORNER + 64, :]),
            kept(has_xy, cross[from_xy, FAR_CORNER : FAR_CORNER + 64, :]),
        )

        def store_sides(start, middle, inner, outer):
            left = jnp.where(pj == 0, outer, inner)
            right = jnp.where(pj == 0, inner, outer)
            store_row_of_tiles(h1, start, left, middle, right)

        for halo in (h1, h2):
            halo[0:32, :] = jnp.zeros((32, 256), BF)
            halo[224:256, :] = jnp.zeros((32, 256), BF)
        far_e1, side_e1 = slice(FAR_E1, FAR_E1 + 32), slice(FAR_E1_SIDE, FAR_E1_SIDE + 32)
        store_sides(
            96, tiles[me], tiles[across_y], kept(has_y, cross[from_y, far_e1, :])
        )
        store_sides(
            32 + 128 * (1 - pi),
            tiles[across_x],
            tiles[across],
            kept(has_y, cross[from_y, side_e1, :]),
        )
        store_sides(
            32 + 128 * pi,
            kept(has_x, cross[from_x, far_e1, :]),
            kept(has_x, cross[from_x, side_e1, :]),
            kept(has_xy, cross[from_xy, far_e1, :]),
        )

        above, below = gx >= 2, gx < count_x - 2
        before, after = gy >= 2, gy < count_y - 2

        def brought(m, slot, keep):
            other = swap_of(gx - pi + m // 2, gy - pj + m % 2, count_x, count_y)
            return kept(keep, shared[m, slot ^ other])

        store_row_of_tiles(
            h2, 32, brought(0, 0, above & before), brought(0, 1, above), brought(1, 1, above & after)
        )
        store_row_of_tiles(h2, 96, brought(0, 2, before), tiles[4], brought(1, 3, after))
        store_row_of_tiles(
            h2, 160, brought(2, 2, below & before), brought(2, 3, below), brought(3, 3, below & after)
        )

        slot = slot_of(32)
        local2 = far_row(tables[448 : 672, 0:224], h2[pl.ds(32 * pi, 224), :], pi)
        local2 = jnp.where(slot == pj, local2, 0.0)
        local2 = local2 + roll(local2, 64)
        local2 = (local2 + roll(local2, 32)).astype(BF)
        transfer = tables[LEAF : LEAF + 256, 128:160]
        spread = dot(transfer[128:256], local2)
        local1 = []
        for i in range(2):
            down = far_row(tables[224 : 448, 0:224], h1[32 * i : 32 * i + 224, :], i)
            for j in range(2):
                n = 2 * i + j
                down = down + jnp.where(slot == j, spread[n * 32 : (n + 1) * 32], 0.0)
            down = jnp.where(slot < 2, down, 0.0)
            wide = jnp.where(slot == 0, down, 0.0) + jnp.where(slot == 2, roll(down, 32), 0.0)
            local1.append((wide + roll(wide, 32)).astype(BF))
        local0 = []
        for i in range(4):
            spread = dot(transfer[64 * (i % 2) : 64 * (i % 2) + 64], local1[i // 2])
            down = far_row(tables[0 : 224, 0:224], h0[32 * i : 32 * i + 224, :], i % 2)
            down = down + jnp.where(lax.rem(slot, 2) == 0, spread[:32], spread[32:])
            local0.append(down.astype(BF))


        slot = slot_of(64)
        column = kept(has_y, cross[from_y, FAR_X : FAR_X + 64, :])
        corner_in = kept(has_y, roll(cross[from_y, FAR_CORNER : FAR_CORNER + 64, :], 64))
        corner_out = kept(has_xy, roll(cross[from_xy, FAR_CORNER : FAR_CORNER + 64, :], 64))
        boxes = {a: roll(column, -32 * a) for a in range(4)}
        boxes[-1] = jnp.where(pi == 0, corner_out, corner_in)
        boxes[4] = jnp.where(pi == 0, corner_in, corner_out)
        edge = slot == 3 * pj
        for a in boxes:
            moved = jnp.where(pj == 0, roll(boxes[a], 32), roll(boxes[a], -32))
            boxes[a] = jnp.where(edge, moved, jnp.zeros_like(moved))
        middle = kept(has_x, cross[from_x, FAR_X : FAR_X + 64, :])
        inner = kept(has_x, roll(cross[from_x, FAR_CORNER : FAR_CORNER + 64, :], 64))
        nothing = jnp.zeros_like(inner)
        left = jnp.where(pj == 0, nothing, inner)
        right = jnp.where(pj == 0, inner, nothing)
        shifts = (
            roll(jnp.where(slot == 3, left, middle), 32),
            middle,
            roll(jnp.where(slot == 0, right, middle), -32),
        )
        beyond = jnp.zeros((256, 128), F32)
        for c in range(3):
            beyond = beyond + dot(edges[256 * c : 256 * c + 256, :], shifts[c])
        beyond = merge_diagonal(beyond, 64)

        block = lax.broadcasted_iota(jnp.int32, (128, 128), 0) // 32 == slot_of(128)
        part, within = split_order(near_part[256:264, :].astype(jnp.int32))
        pick = jnp.concatenate([pick_sites(within[n : n + 1, :]) for n in range(8)], axis=1)
        leaves = []
        for a in range(4):
            total = near_part[a * 64 : (a + 1) * 64, :]
            if a == 0:
                total = total + jnp.where(pi == 0, beyond, 0.0)
            if a == 3:
                total = total + jnp.where(pi == 0, 0.0, beyond)
            for r in range(3):
                row = 768 + 64 * (3 * a + r)
                total = total + dot(edges[row : row + 64, :], boxes[a + r - 1])
            leaf = tables[LEAF + a * 64 : LEAF + (a + 1) * 64, 0:128]
            local = jnp.concatenate([local0[a]] * 4, axis=0)
            total = total + dot(leaf, jnp.where(block, local, jnp.zeros_like(local)))
            leaves.append(total)
        spread = []
        for pair in range(2):
            turned = jnp.transpose(jnp.concatenate(leaves[2 * pair : 2 * pair + 2], axis=0))
            for b in range(4):
                n = 4 * pair + b
                line = turned[32 * b : 32 * b + 32]
                parts = [jnp.where(part[n : n + 1, :] == t, line, 0.0) for t in range(8)]
                spread.append(jnp.concatenate(parts, axis=0).astype(BF))
        done = dot_nt(jnp.concatenate(spread, axis=1), pick).astype(BF)
        for t in range(8):
            out[:, 128 * t : 128 * (t + 1)] = done[32 * t : 32 * t + 32]
        last = pltpu.make_async_copy(out, out_hbm, sem)
        last.start()
        last.wait()

    return body


def call(kernel, spaces, shapes, scratch=(), flops=10**6):
    def run(*args):
        return pl.pallas_call(
            kernel,
            out_shape=shapes,
            in_specs=[pl.BlockSpec(memory_space=space) for space in spaces],
            out_specs=jax.tree.map(lambda shape: pl.BlockSpec(memory_space=shape.memory_space), shapes),
            scratch_shapes=list(scratch),
            cost_estimate=pl.CostEstimate(flops=flops, bytes_accessed=2**20, transcendentals=0),
            compiler_params=pltpu.CompilerParams(vmem_limit_bytes=VMEM_BYTES),
        )(*map(pltpu.with_memory_space_constraint, args, spaces))

    return run


def aligned_groups(count_x, count_y):
    return [
        [(i + di) * count_y + j + dj for di in range(2) for dj in range(2)]
        for i in range(0, count_x, 2)
        for j in range(0, count_y, 2)
    ]


def shifted_groups(count_x, count_y):
    last_x, last_y = count_x - 1, count_y - 1
    groups = [
        [(i, j), (i, j + 1), (i + 1, j), (i + 1, j + 1)]
        for i in range(1, last_x, 2)
        for j in range(1, last_y, 2)
    ]
    for i in (0, last_x):
        pairs = [[(i, j), (i, j + 1)] for j in range(1, last_y, 2)]
        groups.append(pairs.pop(corner_pair(count_y)) + [(i, last_y), (i, 0)])
        groups += [pairs[n] + pairs[n + 1] for n in range(0, len(pairs), 2)]
    for i in range(1, last_x, 4):
        if i + 3 < last_x:
            for j in (0, last_y):
                lanes = (i + 2, i) if j == 0 else (i, i + 2)
                groups.append([(g + d, j) for d in range(2) for g in lanes])
        else:
            groups.append([(i + d, j) for d in range(2) for j in (last_y, 0)])
    return [[i * count_y + j for i, j in group] for group in groups]


def run_upward(samples, order, basis, transfer, near_blocks):
    return call(
        upward_kernel,
        (HBM,) * 5,
        (VMEM((256, 128), BF), VMEM((OWN_ROWS, 128), BF), VMEM((2, 4, 9, 64, 64), BF), VMEM((192, 64), BF)),
        (
            VMEM((8, 128), jnp.int32),
            VMEM((32, 1024), BF),
            VMEM((512, 64), BF),
            VMEM((256, 32), BF),
            pltpu.SemaphoreType.DMA((5,)),
        ),
    )(samples, order, basis, transfer, near_blocks)


def run_cross(group, x, turned, count_x, count_y):
    body = functools.partial(cross_kernel, count_x=count_x, count_y=count_y)
    return call(
        body,
        (VMEM,) * 3,
        (HBM((4, FAR_ROWS, 128), BF), VMEM((5, 32, 128), BF)),
        (VMEM((4, FAR_ROWS, 128), BF), pltpu.SemaphoreType.DMA((2,))),
    )(group, x, turned)


def run_inner(group, x, near, near_blocks, coupling, basis, transfer, order):
    return call(
        inner_kernel,
        (VMEM,) * 3 + (HBM,) * 5,
        (VMEM((264, 128), F32), VMEM((TABLE_ROWS, 256), BF), VMEM((1536, 64), BF)),
        (
            VMEM((2, 4, 9, 64, 64), BF),
            VMEM((3, 32, 32, 40), BF),
            VMEM((512, 64), BF),
            VMEM((256, 32), BF),
            VMEM((8, 128), jnp.int32),
            VMEM((256, 128), F32),
            VMEM((256, 128), F32),
            pltpu.SemaphoreType.DMA((5,)),
        ),
        flops=10**9,
    )(group, x, near, near_blocks, coupling, basis, transfer, order)


def run_downward(group, tiles, inner, cross, shared, count_x, count_y):
    return call(
        downward_kernel(count_x, count_y),
        (VMEM,) * 7,
        HBM((32, 1024), BF),
        (
            VMEM((320, 256), BF),
            VMEM((256, 256), BF),
            VMEM((256, 256), BF),
            VMEM((32, 1024), BF),
            pltpu.SemaphoreType.DMA,
        ),
    )(group, tiles, *inner, cross, shared)


def solution(mesh):
    count_x, count_y = mesh.shape["gx"], mesh.shape["gy"]
    aligned = aligned_groups(count_x, count_y)
    shifted = shifted_groups(count_x, count_y)

    def local(samples, site_order, leaf_basis, near_blocks, transfer, coupling):
        samples = samples.T
        order = site_order.reshape(8, 128)
        basis = leaf_basis.transpose(0, 1, 3, 2).reshape(512, 64)
        transfer = transfer.reshape(256, 32)
        coupling = coupling.transpose(0, 2, 3, 1)
        x, message, near, turned = run_upward(samples, order, basis, transfer, near_blocks)
        group = lax.all_gather(message, AXES, axis_index_groups=aligned)
        send, tiles = run_cross(group, x, turned, count_x, count_y)
        cross = lax.all_to_all(send, AXES, 0, 0, axis_index_groups=shifted)
        inner = run_inner(
            group, x, near, near_blocks, coupling, basis, transfer, order
        )
        shared = lax.all_gather(cross[:, FAR_E2 : FAR_E2 + 32], AXES, axis_index_groups=aligned)
        out = run_downward(group, tiles, inner, cross, shared, count_x, count_y)
        return out.T

    return jax.shard_map(
        local,
        mesh=mesh,
        in_specs=(
            P(("gx", "gy"), None),
            P(("gx", "gy")),
            P("gx", "gy", None, None),
            P("gx", "gy", None, None, None),
            P(),
            P(),
        ),
        out_specs=P(("gx", "gy"), None),
        check_vma=False,
    )
```

```python
import functools

import jax
import jax.numpy as jnp
from jax import lax
from jax.experimental import pallas as pl
from jax.experimental.pallas import tpu as pltpu
from jax.sharding import PartitionSpec as P

BF = jnp.bfloat16
F32 = jnp.float32
AXES = ("gx", "gy")
LEAF, TABLE_ROWS = 672, 928
VMEM_BYTES = 32 * 1024 * 1024
VMEM, HBM = pltpu.VMEM, pltpu.HBM

OWN_ROW, OWN_COL, OWN_E0, OWN_ROWS = 0, 64, 128, 256
FAR_X, FAR_E0, FAR_CORNER, FAR_E1, FAR_E1_SIDE, FAR_E2, FAR_ROWS = 0, 64, 128, 192, 224, 256, 288


def dot(a, b):
    return lax.dot_general(a, b, (((1,), (0,)), ((), ())), preferred_element_type=F32)


def dot_nt(a, b):
    return lax.dot_general(a, b, (((1,), (1,)), ((), ())), preferred_element_type=F32)


def roll(x, lanes):
    lanes = lanes % x.shape[1]
    if lanes == 0:
        return x
    if x.dtype == BF:
        return pltpu.roll(x.astype(F32), lanes, 1).astype(BF)
    return pltpu.roll(x, lanes, 1)


def lane_of(rows, lanes=128):
    return lax.broadcasted_iota(jnp.int32, (rows, lanes), 1)


def slot_of(rows, lanes=128):
    return lane_of(rows, lanes) // 32


def eye(n):
    row = lax.broadcasted_iota(jnp.int32, (n, n), 0)
    return jnp.where(row == lane_of(n, n), 1.0, 0.0).astype(BF)


def place():
    gx, gy = lax.axis_index("gx"), lax.axis_index("gy")
    return gx, gy, lax.rem(gx, 2), lax.rem(gy, 2)


def corner_pair(count_y):
    return (count_y - 8) // 2 if count_y > 8 else 0


def swap_of(gx, gy, count_x, count_y):
    end_x = (gx == 0) | (gx == count_x - 1)
    end_y = (gy == 0) | (gy == count_y - 1)
    corner = corner_pair(count_y)
    pair = lax.div(gy + 1, 2) - 1
    first = (pair == corner) | (lax.rem(jnp.where(pair > corner, pair + 1, pair), 2) == 0)
    along_y = jnp.where(first == (gx == 0), 2, 0)
    along_x = jnp.where(lax.rem(gx + 3, 4) >= 2, 1, 0)
    return jnp.where(end_x & ~end_y, along_y, jnp.where(end_y & ~end_x, along_x, 0))


def merge_diagonal(blocks, height):
    slot = slot_of(height)
    out = jnp.zeros((height, 128), F32)
    for b in range(4):
        out = jnp.where(slot == b, blocks[b * height : (b + 1) * height], out)
    return out


def split_order(order):
    lane = lane_of(1)
    lines = []
    for pair in range(2):
        for b in range(4):
            low = order[4 * pair + b // 2 : 4 * pair + b // 2 + 1, :]
            high = order[4 * pair + 2 + b // 2 : 4 * pair + 3 + b // 2, :]
            if b % 2 == 0:
                lines.append(jnp.where(lane < 64, low, pltpu.roll(high, 64, 1)))
            else:
                lines.append(jnp.where(lane < 64, pltpu.roll(low, 64, 1), high))
    lines = jnp.concatenate(lines, axis=0)
    return lines // 128, lines % 128


def pick_sites(within):
    row = lax.broadcasted_iota(jnp.int32, (128, 128), 0)
    return jnp.where(within == row, 1.0, 0.0).astype(BF)


def fetch(sources, targets, sems):
    copies = [
        pltpu.make_async_copy(source, target, sems.at[n])
        for n, (source, target) in enumerate(zip(sources, targets))
    ]
    for copy in copies:
        copy.start()
    return copies


def upward_kernel(
    samples_hbm, order_hbm, basis_hbm, transfer_hbm, near_hbm,
    x_out, msg, near, turned, order, samples, basis, transfer, sems,
):
    copies = fetch(
        (order_hbm, samples_hbm, basis_hbm, transfer_hbm, near_hbm.at[0:2]),
        (order, samples, basis, transfer, near),
        sems,
    )
    _, _, pi, pj = place()
    copies[0].wait()
    block, within = split_order(order[...])
    picks = [pick_sites(within[n : n + 1, :]) for n in range(8)]
    copies[1].wait()
    table = jnp.concatenate([samples[:, 128 * t : 128 * t + 128] for t in range(8)], axis=0)
    xs, e0s = [], []
    for pair in range(2):
        columns = []
        for b in range(4):
            n = 4 * pair + b
            found = dot(table, picks[n])
            columns.append(
                sum(
                    jnp.where(block[n : n + 1, :] == t, found[32 * t : 32 * t + 32], 0.0)
                    for t in range(8)
                )
            )
        both = jnp.transpose(jnp.concatenate(columns, axis=0)).astype(BF)
        x_out[128 * pair : 128 * pair + 128, :] = both
        xs += [both[:64], both[64:]]
    slot = slot_of(64)
    copies[2].wait()
    for a in range(4):
        e0 = merge_diagonal(dot(basis[a * 128 : (a + 1) * 128, :], xs[a]), 32).astype(BF)
        msg[OWN_E0 + a * 32 : OWN_E0 + (a + 1) * 32, :] = e0
        e0s.append(e0)
    msg[OWN_ROW : OWN_ROW + 64, :] = jnp.where(pi == 0, xs[3], xs[0])
    column_slot = jnp.where(pj == 0, 3, 0)
    packed = jnp.zeros((64, 128), BF)
    for a in range(4):
        packed = jnp.where(slot == lax.rem(column_slot + a, 4), roll(xs[a], 32 * a), packed)
    msg[OWN_COL : OWN_COL + 64, :] = packed

    one = eye(32)
    copies[3].wait()
    for n in range(8):
        block = slice(n * 32, (n + 1) * 32)
        turned[block, :] = dot_nt(one, transfer[block, :]).astype(BF)
    copies[4].wait()


def lift(group, turned, tiles):
    slot = lax.rem(slot_of(32, 512), 4)
    lines = [
        jnp.concatenate(
            [group[m, OWN_E0 + 32 * x : OWN_E0 + 32 * x + 32, :] for m in range(4)], axis=1
        )
        for x in range(4)
    ]
    matrices = [turned[32 * n : 32 * n + 32, :] for n in range(4)]
    e1 = jnp.zeros((32, 512), F32)
    for x in range(2):
        parts = []
        for j in range(2):
            parts.append(dot(matrices[j], lines[2 * x]) + dot(matrices[2 + j], lines[2 * x + 1]))
        joined = parts[0] + roll(parts[1], -32)
        e1 = jnp.where(slot == 2 * x, roll(joined, 64 * x), e1)
        e1 = jnp.where(slot == 2 * x + 1, roll(joined, 64 * x - 32), e1)
    e1 = e1.astype(BF)
    product = dot(turned[128:256, :], e1)
    slot = slot_of(32)
    top = jnp.zeros((32, 128), F32)
    for m in range(4):
        tiles[m] = e1[:, 128 * m : 128 * m + 128]
        e2 = merge_diagonal(product[:, 128 * m : 128 * m + 128], 32)
        e2 = e2 + roll(e2, 64)
        e2 = e2 + roll(e2, 32)
        top = jnp.where(slot == m, e2, top)
    tiles[4] = top.astype(BF)


def cross_kernel(group, x, turned, send_hbm, tiles, send, sems, *, count_x, count_y):
    gx, gy, pi, pj = place()
    swap = swap_of(gx, gy, count_x, count_y)
    me, across_x, across_y = 2 * pi + pj, 2 * (1 - pi) + pj, 2 * pi + 1 - pj
    lane, slot = lane_of(64), slot_of(64)
    near_half = (lane < 64) == (pj == 0)
    e0 = group[me, OWN_E0 : OWN_E0 + 128, :]
    e0_rows = jnp.where(pi == 0, e0[:64], e0[64:])
    x_row = jnp.where(pi == 0, x[0:64, :], x[192:256, :])
    to = (2 * pi + 1 - pj) ^ swap
    send[to, FAR_X : FAR_X + 64, :] = x_row
    send[to, FAR_E0 : FAR_E0 + 64, :] = e0_rows
    column = group[across_y, OWN_COL : OWN_COL + 64, :]
    column = jnp.where(pi == 0, roll(column, 64), roll(column, -32))
    corner_e0 = group[across_y, pl.ds(OWN_E0 + 64 * pi, 64), :]
    send[to, FAR_CORNER : FAR_CORNER + 64, :] = jnp.where(near_half, corner_e0, column)
    side_y = to

    to = (2 * (1 - pi) + pj) ^ swap
    column_slot = jnp.where(pj == 0, 0, 3)
    packed = jnp.zeros((64, 128), BF)
    for a in range(4):
        moved = roll(x[a * 64 : (a + 1) * 64, :], 32 * a)
        packed = jnp.where(slot == lax.rem(column_slot + a, 4), moved, packed)
    send[to, FAR_X : FAR_X + 64, :] = packed
    send[to, FAR_E0 : FAR_E0 + 64, :] = jnp.where(near_half, e0[:64], roll(e0[64:], 64))
    corner_x = roll(group[across_x, OWN_ROW : OWN_ROW + 64, :], 64)
    corner_e0 = group[across_x, pl.ds(OWN_E0 + 64 * pi, 64), :]
    send[to, FAR_CORNER : FAR_CORNER + 64, :] = jnp.where(near_half, corner_e0, corner_x)
    side_x = to

    to = (2 * pi + pj) ^ swap
    send[to, 0:FAR_CORNER, :] = jnp.zeros((FAR_CORNER, 128), BF)
    send[to, FAR_CORNER : FAR_CORNER + 64, :] = jnp.where(near_half, e0_rows, roll(x_row, 64))
    send[(2 * (1 - pi) + 1 - pj) ^ swap, 0:FAR_E1, :] = jnp.zeros((FAR_E1, 128), BF)
    lift(group, turned, tiles)
    for m in range(4):
        send[m, FAR_E1 : FAR_E1 + 32, :] = tiles[me]
        send[m, FAR_E1_SIDE : FAR_E1_SIDE + 32, :] = jnp.zeros((32, 128), BF)
        send[m, FAR_E2 : FAR_E2 + 32, :] = tiles[4]
    send[side_y, FAR_E1_SIDE : FAR_E1_SIDE + 32, :] = tiles[across_y]
    send[side_x, FAR_E1_SIDE : FAR_E1_SIDE + 32, :] = tiles[across_x]
    whole = pltpu.make_async_copy(send, send_hbm, sems.at[0])
    whole.start()
    whole.wait()


def store_row_of_tiles(halo, start, left, middle, right):
    lane = lane_of(32)
    low = lane < 64
    nothing = jnp.zeros((32, 128), BF)
    first = jnp.where(low, middle, roll(right, 64))
    second = jnp.where(low, roll(middle, 64), right)
    halo[pl.ds(start, 32), 0:128] = first
    halo[pl.ds(start, 32), 128:256] = jnp.where(low, nothing, roll(left, 64))
    halo[pl.ds(start + 32, 32), 0:128] = second
    halo[pl.ds(start + 32, 32), 128:256] = jnp.where(low, nothing, left)


def far_row(matrix, window, parity):
    lane = lane_of(224, 224)
    admitted = (lane >= 32 * (1 - parity)) & (lane < 224 - 32 * parity)
    product = dot(jnp.where(admitted, matrix, jnp.zeros((224, 224), BF)), window)
    odd = lax.rem(slot_of(32), 2) == 1
    out = jnp.zeros((32, 128), F32)
    for w in range(-3, 4):
        part = product[(w + 3) * 32 : (w + 4) * 32]
        part = part[:, :128] if w == 0 else pltpu.roll(part, (-32 * w) % 256, 1)[:, :128]
        if w == -3:
            part = jnp.where(odd, part, 0.0)
        if w == 3:
            part = jnp.where(odd, 0.0, part)
        out = out + part
    return out


def turn_coupling(coupling, turned, tables):
    row = lax.broadcasted_iota(jnp.int32, (56, 40), 0)
    number = lane_of(56, 40)
    u, w = row // 8 - 3, row % 8 - 3
    outer = (abs(u) >= 2) & (w <= 3)
    inner = (abs(u) < 2) & (abs(w) >= 2) & (w <= 3)
    index = jnp.where(u < -1, (u + 3) * 7 + w + 3, 26 + (u - 2) * 7 + w + 3)
    index = jnp.where(abs(u) < 2, 14 + (u + 1) * 4 + jnp.where(w < 0, w + 3, w), index)
    choose = jnp.where((outer | inner) & (number == index), 1.0, 0.0).astype(BF)
    slot = slot_of(8)
    for level in range(3):
        for block in range(8):
            lines = coupling[level, 4 * block : 4 * block + 4].reshape(128, 40)
            part = dot_nt(choose, lines)
            moved = [part] + [pltpu.roll(part, 32 * q, 1) for q in range(1, 4)]
            for q in range(4):
                i = 4 * block + q
                for half in range(2):
                    out = jnp.zeros((8, 128), F32)
                    for u in range(4 * half, min(4 * half + 4, 7)):
                        piece = moved[(u - q) % 4][8 * u : 8 * u + 8]
                        out = jnp.where(slot == u % 4, piece, out)
                    turned[half][pl.ds(i, 8, stride=32), :] = out
        for half in range(2):
            lines = turned[half][0:224, :].astype(BF)
            tables[224 * level : 224 * level + 224, 128 * half : 128 * half + 128] = lines


def inner_kernel(
    group, x, near_low, near_hbm, coupling_hbm, basis_hbm, transfer_hbm, order_hbm,
    near_out, tables, edges,
    near_high, coupling, basis, transfer, order, turned_low, turned_high, sems,
):
    copies = fetch(
        (coupling_hbm, near_hbm.at[2:4], basis_hbm, transfer_hbm, order_hbm),
        (coupling, near_high, basis, transfer, order),
        sems,
    )
    _, _, pi, pj = place()
    across_x, across_y, across = 2 * (1 - pi) + pj, 2 * pi + 1 - pj, 2 * (1 - pi) + 1 - pj
    slot = slot_of(64)
    windows = {}

    def store_windows(a, middle, inner):
        left = jnp.where(pj == 0, jnp.zeros_like(inner), inner)
        right = jnp.where(pj == 0, inner, jnp.zeros_like(inner))
        windows[a, 0] = middle
        windows[a, -1] = roll(jnp.where(slot == 3, left, middle), 32)
        windows[a, 1] = roll(jnp.where(slot == 0, right, middle), -32)

    beside = group[across_y, OWN_COL : OWN_COL + 64, :]
    for a in range(4):
        store_windows(a, x[a * 64 : (a + 1) * 64, :], roll(beside, -32 * a))
    middle = group[across_x, OWN_ROW : OWN_ROW + 64, :]
    inner = group[across, OWN_ROW : OWN_ROW + 64, :]
    nothing = jnp.zeros((64, 128), BF)
    store_windows(-1, jnp.where(pi == 0, nothing, middle), jnp.where(pi == 0, nothing, inner))
    store_windows(4, jnp.where(pi == 0, middle, nothing), jnp.where(pi == 0, inner, nothing))
    def add_near(a):
        near = near_low if a < 2 else near_high
        total = jnp.zeros((256, 128), F32)
        for n in range(9):
            matrix = near[a % 2, :, n].reshape(256, 64)
            total = total + dot(matrix, windows[a + n // 3 - 1, n % 3 - 1])
        near_out[a * 64 : (a + 1) * 64, :] = merge_diagonal(total, 64)
        for r in range(3):
            row = 768 + 64 * (3 * a + r)
            edges[row : row + 64, :] = near[a % 2, 3 * pj, 3 * r + 2 * pj]

    add_near(0)
    add_near(1)
    copies[0].wait()
    turn_coupling(coupling, (turned_low, turned_high), tables)
    copies[1].wait()
    add_near(2)
    add_near(3)
    for c in range(3):
        above, below = near_low[0, :, c], near_high[1, :, 6 + c]
        edges[256 * c : 256 * c + 256, :] = jnp.where(pi == 0, above, below).reshape(256, 64)
    for copy in copies[2:]:
        copy.wait()
    for a in range(4):
        flat = jnp.transpose(basis[a * 128 : (a + 1) * 128, :].astype(F32))
        tables[LEAF + a * 64 : LEAF + (a + 1) * 64, 0:128] = flat.astype(BF)
    tables[LEAF : LEAF + 256, 128:160] = transfer[...]
    near_out[256:264, :] = order[...].astype(F32)


def downward_kernel(count_x, count_y):
    def body(group, tiles, near_part, tables, edges, cross, shared, out_hbm, h0, h1, h2, out, sem):
        gx, gy, pi, pj = place()
        swap = swap_of(gx, gy, count_x, count_y)
        me, across_x, across_y = 2 * pi + pj, 2 * (1 - pi) + pj, 2 * pi + 1 - pj
        across = 2 * (1 - pi) + 1 - pj
        from_x, from_y = (2 * pi + 1 - pj) ^ swap, (2 * (1 - pi) + pj) ^ swap
        from_xy = (2 * pi + pj) ^ swap
        has_x = jnp.where(pi == 0, gx > 0, gx < count_x - 1)
        has_y = jnp.where(pj == 0, gy > 0, gy < count_y - 1)
        has_xy = has_x & has_y

        def kept(keep, value):
            return jnp.where(keep, value, jnp.zeros_like(value))

        lane = lane_of(64)
        near_half = (lane < 64) == (pj == 0)
        h0[0:32, :] = jnp.zeros((32, 256), BF)
        h0[288:320, :] = jnp.zeros((32, 256), BF)
        h0[96:224, 0:128] = group[me, OWN_E0 : OWN_E0 + 128, :]
        strip = kept(has_y, cross[from_y, FAR_E0 : FAR_E0 + 64, :])
        beside = group[across_y, OWN_E0 : OWN_E0 + 128, :]
        h0[96:160, 128:256] = jnp.where(near_half, beside[:64], strip)
        h0[160:224, 128:256] = jnp.where(near_half, beside[64:], roll(strip, 64))
        start = 32 + 192 * (1 - pi)
        h0[pl.ds(start, 64), 0:128] = group[across_x, pl.ds(OWN_E0 + 64 * pi, 64), :]
        h0[pl.ds(start, 64), 128:256] = jnp.where(
            near_half,
            group[across, pl.ds(OWN_E0 + 64 * pi, 64), :],
            kept(has_y, cross[from_y, FAR_CORNER : FAR_CORNER + 64, :]),
        )
        start = 32 + 192 * pi
        h0[pl.ds(start, 64), 0:128] = kept(has_x, cross[from_x, FAR_E0 : FAR_E0 + 64, :])
        h0[pl.ds(start, 64), 128:256] = jnp.where(
            near_half,
            kept(has_x, cross[from_x, FAR_CORNER : FAR_CORNER + 64, :]),
            kept(has_xy, cross[from_xy, FAR_CORNER : FAR_CORNER + 64, :]),
        )

        def store_sides(start, middle, inner, outer):
            left = jnp.where(pj == 0, outer, inner)
            right = jnp.where(pj == 0, inner, outer)
            store_row_of_tiles(h1, start, left, middle, right)

        for halo in (h1, h2):
            halo[0:32, :] = jnp.zeros((32, 256), BF)
            halo[224:256, :] = jnp.zeros((32, 256), BF)
        far_e1, side_e1 = slice(FAR_E1, FAR_E1 + 32), slice(FAR_E1_SIDE, FAR_E1_SIDE + 32)
        store_sides(
            96, tiles[me], tiles[across_y], kept(has_y, cross[from_y, far_e1, :])
        )
        store_sides(
            32 + 128 * (1 - pi),
            tiles[across_x],
            tiles[across],
            kept(has_y, cross[from_y, side_e1, :]),
        )
        store_sides(
            32 + 128 * pi,
            kept(has_x, cross[from_x, far_e1, :]),
            kept(has_x, cross[from_x, side_e1, :]),
            kept(has_xy, cross[from_xy, far_e1, :]),
        )

        above, below = gx >= 2, gx < count_x - 2
        before, after = gy >= 2, gy < count_y - 2

        def brought(m, slot, keep):
            other = swap_of(gx - pi + m // 2, gy - pj + m % 2, count_x, count_y)
            return kept(keep, shared[m, slot ^ other])

        store_row_of_tiles(
            h2, 32, brought(0, 0, above & before), brought(0, 1, above), brought(1, 1, above & after)
        )
        store_row_of_tiles(h2, 96, brought(0, 2, before), tiles[4], brought(1, 3, after))
        store_row_of_tiles(
            h2, 160, brought(2, 2, below & before), brought(2, 3, below), brought(3, 3, below & after)
        )

        slot = slot_of(32)
        local2 = far_row(tables[448 : 672, 0:224], h2[pl.ds(32 * pi, 224), :], pi)
        local2 = jnp.where(slot == pj, local2, 0.0)
        local2 = local2 + roll(local2, 64)
        local2 = (local2 + roll(local2, 32)).astype(BF)
        transfer = tables[LEAF : LEAF + 256, 128:160]
        spread = dot(transfer[128:256], local2)
        local1 = []
        for i in range(2):
            down = far_row(tables[224 : 448, 0:224], h1[32 * i : 32 * i + 224, :], i)
            for j in range(2):
                n = 2 * i + j
                down = down + jnp.where(slot == j, spread[n * 32 : (n + 1) * 32], 0.0)
            down = jnp.where(slot < 2, down, 0.0)
            wide = jnp.where(slot == 0, down, 0.0) + jnp.where(slot == 2, roll(down, 32), 0.0)
            local1.append((wide + roll(wide, 32)).astype(BF))
        local0 = []
        for i in range(4):
            spread = dot(transfer[64 * (i % 2) : 64 * (i % 2) + 64], local1[i // 2])
            down = far_row(tables[0 : 224, 0:224], h0[32 * i : 32 * i + 224, :], i % 2)
            down = down + jnp.where(lax.rem(slot, 2) == 0, spread[:32], spread[32:])
            local0.append(down.astype(BF))


        slot = slot_of(64)
        column = kept(has_y, cross[from_y, FAR_X : FAR_X + 64, :])
        corner_in = kept(has_y, roll(cross[from_y, FAR_CORNER : FAR_CORNER + 64, :], 64))
        corner_out = kept(has_xy, roll(cross[from_xy, FAR_CORNER : FAR_CORNER + 64, :], 64))
        boxes = {a: roll(column, -32 * a) for a in range(4)}
        boxes[-1] = jnp.where(pi == 0, corner_out, corner_in)
        boxes[4] = jnp.where(pi == 0, corner_in, corner_out)
        edge = slot == 3 * pj
        for a in boxes:
            moved = jnp.where(pj == 0, roll(boxes[a], 32), roll(boxes[a], -32))
            boxes[a] = jnp.where(edge, moved, jnp.zeros_like(moved))
        middle = kept(has_x, cross[from_x, FAR_X : FAR_X + 64, :])
        inner = kept(has_x, roll(cross[from_x, FAR_CORNER : FAR_CORNER + 64, :], 64))
        nothing = jnp.zeros_like(inner)
        left = jnp.where(pj == 0, nothing, inner)
        right = jnp.where(pj == 0, inner, nothing)
        shifts = (
            roll(jnp.where(slot == 3, left, middle), 32),
            middle,
            roll(jnp.where(slot == 0, right, middle), -32),
        )
        beyond = jnp.zeros((256, 128), F32)
        for c in range(3):
            beyond = beyond + dot(edges[256 * c : 256 * c + 256, :], shifts[c])
        beyond = merge_diagonal(beyond, 64)

        block = lax.broadcasted_iota(jnp.int32, (128, 128), 0) // 32 == slot_of(128)
        part, within = split_order(near_part[256:264, :].astype(jnp.int32))
        pick = jnp.concatenate([pick_sites(within[n : n + 1, :]) for n in range(8)], axis=1)
        leaves = []
        for a in range(4):
            total = near_part[a * 64 : (a + 1) * 64, :]
            if a == 0:
                total = total + jnp.where(pi == 0, beyond, 0.0)
            if a == 3:
                total = total + jnp.where(pi == 0, 0.0, beyond)
            for r in range(3):
                row = 768 + 64 * (3 * a + r)
                total = total + dot(edges[row : row + 64, :], boxes[a + r - 1])
            leaf = tables[LEAF + a * 64 : LEAF + (a + 1) * 64, 0:128]
            local = jnp.concatenate([local0[a]] * 4, axis=0)
            total = total + dot(leaf, jnp.where(block, local, jnp.zeros_like(local)))
            leaves.append(total)
        spread = []
        for pair in range(2):
            turned = jnp.transpose(jnp.concatenate(leaves[2 * pair : 2 * pair + 2], axis=0))
            for b in range(4):
                n = 4 * pair + b
                line = turned[32 * b : 32 * b + 32]
                parts = [jnp.where(part[n : n + 1, :] == t, line, 0.0) for t in range(8)]
                spread.append(jnp.concatenate(parts, axis=0).astype(BF))
        done = dot_nt(jnp.concatenate(spread, axis=1), pick).astype(BF)
        for t in range(8):
            out[:, 128 * t : 128 * (t + 1)] = done[32 * t : 32 * t + 32]
        last = pltpu.make_async_copy(out, out_hbm, sem)
        last.start()
        last.wait()

    return body


def call(kernel, spaces, shapes, scratch=(), flops=10**6):
    def run(*args):
        return pl.pallas_call(
            kernel,
            out_shape=shapes,
            in_specs=[pl.BlockSpec(memory_space=space) for space in spaces],
            out_specs=jax.tree.map(lambda shape: pl.BlockSpec(memory_space=shape.memory_space), shapes),
            scratch_shapes=list(scratch),
            cost_estimate=pl.CostEstimate(flops=flops, bytes_accessed=2**20, transcendentals=0),
            compiler_params=pltpu.CompilerParams(vmem_limit_bytes=VMEM_BYTES),
        )(*map(pltpu.with_memory_space_constraint, args, spaces))

    return run


def aligned_groups(count_x, count_y):
    return [
        [(i + di) * count_y + j + dj for di in range(2) for dj in range(2)]
        for i in range(0, count_x, 2)
        for j in range(0, count_y, 2)
    ]


def shifted_groups(count_x, count_y):
    last_x, last_y = count_x - 1, count_y - 1
    groups = [
        [(i, j), (i, j + 1), (i + 1, j), (i + 1, j + 1)]
        for i in range(1, last_x, 2)
        for j in range(1, last_y, 2)
    ]
    for i in (0, last_x):
        pairs = [[(i, j), (i, j + 1)] for j in range(1, last_y, 2)]
        groups.append(pairs.pop(corner_pair(count_y)) + [(i, last_y), (i, 0)])
        groups += [pairs[n] + pairs[n + 1] for n in range(0, len(pairs), 2)]
    for i in range(1, last_x, 4):
        if i + 3 < last_x:
            for j in (0, last_y):
                lanes = (i + 2, i) if j == 0 else (i, i + 2)
                groups.append([(g + d, j) for d in range(2) for g in lanes])
        else:
            groups.append([(i + d, j) for d in range(2) for j in (last_y, 0)])
    return [[i * count_y + j for i, j in group] for group in groups]


def run_upward(samples, order, basis, transfer, near_blocks):
    return call(
        upward_kernel,
        (HBM,) * 5,
        (VMEM((256, 128), BF), VMEM((OWN_ROWS, 128), BF), VMEM((2, 4, 9, 64, 64), BF), VMEM((256, 32), BF)),
        (
            VMEM((8, 128), jnp.int32),
            VMEM((32, 1024), BF),
            VMEM((512, 64), BF),
            VMEM((256, 32), BF),
            pltpu.SemaphoreType.DMA((5,)),
        ),
    )(samples, order, basis, transfer, near_blocks)


def run_cross(group, x, turned, count_x, count_y):
    body = functools.partial(cross_kernel, count_x=count_x, count_y=count_y)
    return call(
        body,
        (VMEM,) * 3,
        (HBM((4, FAR_ROWS, 128), BF), VMEM((5, 32, 128), BF)),
        (VMEM((4, FAR_ROWS, 128), BF), pltpu.SemaphoreType.DMA((2,))),
    )(group, x, turned)


def run_inner(group, x, near, near_blocks, coupling, basis, transfer, order):
    return call(
        inner_kernel,
        (VMEM,) * 3 + (HBM,) * 5,
        (VMEM((264, 128), F32), VMEM((TABLE_ROWS, 256), BF), VMEM((1536, 64), BF)),
        (
            VMEM((2, 4, 9, 64, 64), BF),
            VMEM((3, 32, 32, 40), BF),
            VMEM((512, 64), BF),
            VMEM((256, 32), BF),
            VMEM((8, 128), jnp.int32),
            VMEM((256, 128), F32),
            VMEM((256, 128), F32),
            pltpu.SemaphoreType.DMA((5,)),
        ),
        flops=10**9,
    )(group, x, near, near_blocks, coupling, basis, transfer, order)


def run_downward(group, tiles, inner, cross, shared, count_x, count_y):
    return call(
        downward_kernel(count_x, count_y),
        (VMEM,) * 7,
        HBM((32, 1024), BF),
        (
            VMEM((320, 256), BF),
            VMEM((256, 256), BF),
            VMEM((256, 256), BF),
            VMEM((32, 1024), BF),
            pltpu.SemaphoreType.DMA,
        ),
    )(group, tiles, *inner, cross, shared)


def solution(mesh):
    count_x, count_y = mesh.shape["gx"], mesh.shape["gy"]
    aligned = aligned_groups(count_x, count_y)
    shifted = shifted_groups(count_x, count_y)

    def local(samples, site_order, leaf_basis, near_blocks, transfer, coupling):
        samples = samples.T
        order = site_order.reshape(8, 128)
        basis = leaf_basis.transpose(0, 1, 3, 2).reshape(512, 64)
        transfer = transfer.reshape(256, 32)
        coupling = coupling.transpose(0, 2, 3, 1)
        x, message, near, turned = run_upward(samples, order, basis, transfer, near_blocks)
        group = lax.all_gather(message, AXES, axis_index_groups=aligned)
        send, tiles = run_cross(group, x, turned, count_x, count_y)
        cross = lax.all_to_all(send, AXES, 0, 0, axis_index_groups=shifted)
        inner = run_inner(
            group, x, near, near_blocks, coupling, basis, transfer, order
        )
        shared = lax.all_gather(cross[:, FAR_E2 : FAR_E2 + 32], AXES, axis_index_groups=aligned)
        out = run_downward(group, tiles, inner, cross, shared, count_x, count_y)
        return out.T

    return jax.shard_map(
        local,
        mesh=mesh,
        in_specs=(
            P(("gx", "gy"), None),
            P(("gx", "gy")),
            P("gx", "gy", None, None),
            P("gx", "gy", None, None, None),
            P(),
            P(),
        ),
        out_specs=P(("gx", "gy"), None),
        check_vma=False,
    )
```
